32 devices in a mesh: tx: 8 (over y, x, core), ty: 4 (over z).
Axes of the slice: x: 2, y: 2, z: 4, core: 2. Of those that a mesh axis runs over, the one named last changes fastest.
Arguments:
- object_slab: float32 [2, 2, 2048, 4096], P(None, None, 'tx', 'ty'), may hold values from -5 to 5
- probe: float32 [2, 256, 256], replicated, may hold values from -6 to 6
- patterns: float32 [256, 256, 256], P(('tx', 'ty')), may hold values from 0 to 4
- centers: int32 [256, 2], P(('tx', 'ty')), may hold values from 128 to 3968, as said below
- counts: int32 [32], replicated, may hold values from 0 to 8, as said below
Outputs:
- object_gradient: float32 [2, 2, 2048, 4096], P(None, None, 'tx', 'ty')
- probe_gradient: float32 [2, 256, 256], replicated
The draws below stay inside these ranges and needn't reach their ends.
Inputs may be any that keep to these rules, and one draw needn't show every extreme that they name: Slot block d = i * (devices along ty) + j belongs to the device at tx-index i and ty-index j; each of its centers lies in that device's tile, rows i * 256 to (i + 1) * 256 - 1 and columns j * 1024 to (j + 1) * 1024 - 1, and the window of side 256 around it lies inside the object. Entry i * (devices along ty) + j is the number of used slots, always the first ones, of the device at tx-index i and ty-index j. The counts of two devices with the same ty-index whose tx-indices differ by half the tx axis add up to at most 8; some device has 8.
All inputs are finite; a program needn't handle non-finite values.
Results may differ from the reference program's by a relative error of at most 0.0003.
Values sent between devices are 32-bit elements; how exact they have to be, the bound alone decides.
No kernel may reach another device: no remote copies, remote signals or barrier semaphores. Data moves between devices by JAX's collectives and lax.ppermute only.
A program may use at most 128 MiB of HBM per device.

```python
import math
import jax
import jax.numpy as jnp
from jax import lax

W = 256
S = 2
TR = 256
TC = 1024
CAP = 8
NX = 2048
NY = 4096
SLOTS = 256


def draw_centers(key, part):
    key = jax.random.fold_in(key, 11)
    rows_dev = NX // TR
    cols_dev = NY // TC
    slot = jnp.arange(rows_dev * cols_dev * CAP, dtype=jnp.int32)
    device = slot // CAP
    tile_row = device // cols_dev
    tile_col = device % cols_dev
    half = W // 2
    row_lo = jnp.maximum(tile_row * TR, half)
    row_hi = jnp.minimum((tile_row + 1) * TR, NX - half + 1)
    col_lo = jnp.maximum(tile_col * TC, half)
    col_hi = jnp.minimum((tile_col + 1) * TC, NY - half + 1)
    key_rows, key_cols = jax.random.split(key)
    rows = jax.random.randint(key_rows, slot.shape, row_lo, row_hi)
    cols = jax.random.randint(key_cols, slot.shape, col_lo, col_hi)
    return jnp.stack([rows, cols], axis=1).astype(jnp.int32)


def draw_counts(key, part):
    key = jax.random.fold_in(key, 23)
    rows_dev = NX // TR
    cols_dev = NY // TC
    pairs = rows_dev // 2 * cols_dev
    key_a, key_b, key_c, key_d = jax.random.split(key, 4)
    heavy = jax.random.randint(key_a, (pairs,), 0, CAP + 1)
    light = jax.random.randint(key_b, (pairs,), 0, CAP - heavy + 1)
    chosen = jax.random.randint(key_c, (), 0, pairs)
    index = jnp.arange(pairs, dtype=jnp.int32)
    heavy = jnp.where(index == chosen, CAP, heavy)
    light = jnp.where(index == chosen, 0, light)
    flip = jax.random.randint(key_d, (pairs,), 0, 2)
    upper = jnp.where(flip == 1, heavy, light)
    lower = jnp.where(flip == 1, light, heavy)
    grid = jnp.concatenate([upper.reshape(rows_dev // 2, cols_dev), lower.reshape(rows_dev // 2, cols_dev)], axis=0)
    return grid.reshape(-1).astype(jnp.int32)


def steps_of(rng, shape, pieces, smallest, high):
    def one(position, shards_of):
        steps = jax.random.uniform(jax.random.fold_in(jax.random.fold_in(rng, 6), position), (shards_of,), jnp.float32, smallest / len(pieces), high / len(pieces))
        return jnp.repeat(jnp.exp(steps), shape[position] // shards_of).reshape((-1,) + (1,) * (len(shape) - position - 1))

    factor_of = one(*pieces[0])
    for cut in pieces[1:]:
        factor_of = factor_of * one(*cut)
    return factor_of


def bell_draw(rng, extent, scale, most, cuts=(), kind=jnp.bfloat16):
    level = steps_of(rng, extent, cuts, -0.22, 0.18) if cuts else 1.0
    array = jax.random.normal(rng, extent, jnp.float32) * scale * level
    return jnp.minimum(jnp.maximum(array, -most), most).astype(kind)


def setup_inputs(seed: int = 0) -> dict:
    key_of = jax.random.split(jax.random.key(seed), 6)
    return {
        "object_slab": bell_draw(key_of[0], (S, 2, NX, NY), 0.7, 5.0, ((2, 8), (3, 4)), jnp.float32),
        "probe": bell_draw(key_of[1], (2, W, W), 1.0, 6.0, (), jnp.float32),
        "patterns": jnp.clip(4.0 * jax.random.uniform(key_of[2], (SLOTS, W, W), jnp.float32) ** steps_of(key_of[2], (SLOTS, W, W), ((0, 32),), -0.2, 0.2), 0.0, 4.0),
        "centers": draw_centers(jax.random.fold_in(key_of[5], 71), 0),
        "counts": draw_counts(jax.random.fold_in(key_of[5], 71), 0),
    }


KAPPA = 40.0
HIGH = lax.Precision.HIGHEST

def transforms(width):
    idx = jnp.arange(width, dtype=jnp.int32)
    product = idx[:, None] * idx[None, :] % width
    angle = product.astype(jnp.float32) * (2.0 * math.pi / width)
    scale = 1.0 / math.sqrt(width)
    cosine = jnp.cos(angle) * scale
    sine = jnp.sin(angle) * scale
    fwd_left = jnp.concatenate([jnp.concatenate([cosine, sine], axis=1), jnp.concatenate([-sine, cosine], axis=1)], axis=0)
    fwd_right = jnp.concatenate([jnp.concatenate([cosine, -sine], axis=1), jnp.concatenate([sine, cosine], axis=1)], axis=0)
    freq = ((idx + width // 2) % width - width // 2).astype(jnp.float32) / width
    phase = -math.pi * KAPPA * (freq[:, None] * freq[:, None] + freq[None, :] * freq[None, :])
    kernel = jnp.stack([jnp.cos(phase), jnp.sin(phase)])
    return (fwd_left, fwd_right, kernel)

def transform(field, left, right):
    width = field.shape[-1]
    stacked = jnp.dot(left, field.reshape(2 * width, width), precision=HIGH)
    wide = jnp.concatenate([stacked[:width], stacked[width:]], axis=1)
    result = jnp.dot(wide, right, precision=HIGH)
    return jnp.stack([result[:, :width], result[:, width:]])

def cmul(first, second):
    return jnp.stack([first[0] * second[0] - first[1] * second[1], first[0] * second[1] + first[1] * second[0]])

def conj(field):
    return jnp.stack([field[0], -field[1]])

def slot_terms(patch, probe, pattern, tables):
    fwd_left, fwd_right, kernel = tables
    slices = patch.shape[0]
    inputs = []
    wave = probe
    for level in range(slices):
        if level > 0:
            wave = transform(cmul(kernel, transform(wave, fwd_left, fwd_right)), fwd_right, fwd_left)
        inputs.append(wave)
        wave = cmul(wave, patch[level])
    far = transform(wave, fwd_left, fwd_right)
    soft = jnp.sqrt(far[0] * far[0] + far[1] * far[1] + 1.0)
    factor = 1.0 - jnp.sqrt(pattern) / soft
    chi = transform(far * factor[None], fwd_right, fwd_left)
    grads = [None] * slices
    for level in range(slices - 1, -1, -1):
        grads[level] = cmul(conj(inputs[level]), chi)
        chi = cmul(conj(patch[level]), chi)
        if level > 0:
            chi = transform(cmul(conj(kernel), transform(chi, fwd_left, fwd_right)), fwd_right, fwd_left)
    return (jnp.stack(grads), chi)

def reference(object_slab, probe, patterns, centers, counts):
    tables = transforms(W)
    half = W // 2
    slots = patterns.shape[0]
    zero = jnp.zeros((), jnp.int32)

    def visit(carry, slot):
        total, probe_part = carry
        row = (centers[slot, 0] - half).astype(jnp.int32)
        col = (centers[slot, 1] - half).astype(jnp.int32)
        start = (zero, zero, row, col)
        patch = lax.dynamic_slice(object_slab, start, (S, 2, W, W))
        used = (slot % CAP < counts[slot // CAP]).astype(jnp.float32)
        grads, probe_term = slot_terms(patch, probe, patterns[slot], tables)
        current = lax.dynamic_slice(total, start, (S, 2, W, W))
        total = lax.dynamic_update_slice(total, current + used * grads, start)
        return ((total, probe_part + used * probe_term), None)
    init = (jnp.zeros(object_slab.shape, jnp.float32), jnp.zeros(probe.shape, jnp.float32))
    (total, probe_part), _ = lax.scan(visit, init, jnp.arange(slots, dtype=jnp.int32))
    positions = jnp.maximum(jnp.sum(counts), 1).astype(jnp.float32)
    return (total, probe_part / jnp.sqrt(positions))
```

```python
import math

import jax
import jax.numpy as jnp
import ml_dtypes
import numpy as np
from jax import lax
from jax.experimental import pallas as pl
from jax.experimental.pallas import tpu as pltpu
from jax.sharding import PartitionSpec as P

KAPPA = 40.0
F32 = jnp.float32
FWD, INV, PROP, ADJ = 0, 1, 2, 3
LEFT = {FWD: (0, 2), INV: (1, 3), PROP: (4, 6), ADJ: (5, 7)}
RIGHT = {FWD: (1, 3), INV: (0, 2), PROP: (5, 7), ADJ: (4, 6)}


def tables(width):
    half = width // 2
    n = np.arange(half)
    freq = ((np.arange(width) + half) % width - half) / width
    factor = np.exp(-1j * math.pi * KAPPA * freq * freq)
    turn = 2j * np.pi / width
    scale = 1.0 / math.sqrt(width)
    even = np.exp(-turn * ((2 * n[:, None] * n[None, :]) % width)) * scale
    odd = np.exp(-turn * (((2 * n[:, None] + 1) * n[None, :]) % width)) * scale

    def combined(freqs):
        apart = n[:, None] - n[None, :]
        total = np.zeros((half, half), complex)
        for k in freqs:
            total += factor[k] * np.exp(turn * ((k * apart) % width))
        return total / width

    lefts, rights = [], []
    for c in (even, odd, combined(range(0, width, 2)), combined(range(1, width, 2))):
        real = np.block([[c.real, -c.imag], [c.imag, c.real]])
        for m in (real, real.T):
            hi = m.astype(ml_dtypes.bfloat16)
            lo = (m - hi.astype(np.float64)).astype(ml_dtypes.bfloat16)
            lefts.append(np.concatenate([hi, hi, lo], axis=1))
            rights.append(np.concatenate([hi, hi, lo], axis=0))
    return jnp.asarray(np.stack(lefts)), jnp.asarray(np.stack(rights))


def split(x):
    hi = x.astype(jnp.bfloat16)
    return hi, (x - hi.astype(F32)).astype(jnp.bfloat16)


def pair(x, y, axis):
    return jnp.concatenate([x, y], axis=axis)


def one_side(re, im, kind, axis, table):
    half = re.shape[axis] // 2

    def halves(x):
        return (x[:half], x[half:]) if axis == 0 else (x[:, :half], x[:, half:])

    a, b = halves(re)
    c, d = halves(im)
    if kind != INV:
        a, b, c, d = a + b, a - b, c + d, c - d

    def product(x, index):
        hi, lo = split(x)
        stacked = jnp.concatenate([hi, lo, hi], axis=axis)
        if axis == 0:
            return jnp.dot(table[index], stacked, preferred_element_type=F32)
        return jnp.dot(stacked, table[index], preferred_element_type=F32)

    even, odd = (LEFT if axis == 0 else RIGHT)[kind]
    a, c = halves(product(pair(a, c, axis), even))
    b, d = halves(product(pair(b, d, axis), odd))
    if kind == FWD:
        return pair(a, b, axis), pair(c, d, axis)
    return pair(a + b, a - b, axis), pair(c + d, c - d, axis)


def transform(re, im, kind, lefts, rights):
    re, im = one_side(re, im, kind, 1, rights)
    return one_side(re, im, kind, 0, lefts)


def times(a, b, c, d):
    return a * c - b * d, a * d + b * c


def conj_times(a, b, c, d):
    return a * c + b * d, a * d - b * c


def blocks_of(cols, width, rim):
    pieces = []
    at = 0
    while at < cols:
        block, inside = divmod(at + rim, width)
        count = min(width - inside, cols - at)
        pieces.append((at, count, block, inside))
        at += count
    return pieces


def kernel_body(
    rows, cols, bounds, mid, top, bottom, left, left_ends, right, right_ends, patterns, probe, lefts, rights,
    g_mid, g_top, g_bottom, g_left, g_right, g_probe, obj, acc, sem,
):
    width = probe.shape[-1]
    rim = width // 2
    tile_rows, tile_cols = mid.shape[2], mid.shape[3]
    last = obj.shape[0] - 1
    bands = ((rim, tile_rows), (0, rim), (rim + tile_rows, rim))

    copies = []
    for source, (row, count) in zip((mid, top, bottom), bands):
        for at, span, block, inside in blocks_of(tile_cols, width, rim):
            copies.append((source.at[:, :, :, at : at + span], obj.at[block, :, :, row : row + count, inside : inside + span]))
    for own, ends, block, inside in ((left, left_ends, 0, 0), (right, right_ends, last, rim)):
        lanes = slice(inside, inside + rim)
        copies.append((own, obj.at[block, :, :, rim : rim + tile_rows, lanes]))
        copies.append((ends.at[:, :, :rim], obj.at[block, :, :, :rim, lanes]))
        copies.append((ends.at[:, :, rim:], obj.at[block, :, :, rim + tile_rows :, lanes]))
    copies = [pltpu.make_async_copy(a, b, sem.at[i]) for i, (a, b) in enumerate(copies)]
    for copy in copies:
        copy.start()
    acc[...] = jnp.zeros_like(acc)
    g_probe[...] = jnp.zeros_like(g_probe)
    for copy in copies:
        copy.wait()

    row_index = lax.broadcasted_iota(jnp.int32, (width, width), 0)
    col_index = lax.broadcasted_iota(jnp.int32, (width, width), 1)

    def visit(slot, _):
        row, col = rows[slot], cols[slot]
        block = col // width
        shift = col % width
        below = row_index < row
        beside = col_index < shift

        def cut(level, part):
            upper = jnp.where(beside, obj[block + 1, level, part, :width], obj[block, level, part, :width])
            lower = jnp.where(beside, obj[block + 1, level, part, width:], obj[block, level, part, width:])
            return jnp.where(below, lower, upper)

        def deposit(level, part, term):
            zero = jnp.zeros_like(term)
            upper = jnp.where(below, zero, term)
            lower = jnp.where(below, term, zero)
            acc[block, level, part, :width] += jnp.where(beside, zero, upper)
            acc[block, level, part, width:] += jnp.where(beside, zero, lower)
            acc[block + 1, level, part, :width] += jnp.where(beside, upper, zero)
            acc[block + 1, level, part, width:] += jnp.where(beside, lower, zero)

        def rolled(x, down, along):
            return pltpu.roll(pltpu.roll(x, down, 0), along, 1)

        u0 = rolled(probe[0], row, shift), rolled(probe[1], row, shift)
        o0 = cut(0, 0), cut(0, 1)
        u1 = transform(*times(*u0, *o0), PROP, lefts, rights)
        o1 = cut(1, 0), cut(1, 1)
        far_re, far_im = transform(*times(*u1, *o1), FWD, lefts, rights)
        factor = 1.0 - patterns[slot] * lax.rsqrt(far_re * far_re + far_im * far_im + 1.0)
        chi = transform(far_re * factor, far_im * factor, INV, lefts, rights)
        for part, term in enumerate(conj_times(*u1, *chi)):
            deposit(1, part, term)
        chi = transform(*conj_times(*o1, *chi), ADJ, lefts, rights)
        for part, term in enumerate(conj_times(*u0, *chi)):
            deposit(0, part, term)
        up, back = (width - row) % width, (width - shift) % width
        for part, term in enumerate(conj_times(*o0, *chi)):
            g_probe[part] += rolled(term, up, back)
        return 0

    lax.fori_loop(bounds[0], bounds[1], visit, 0)

    copies = []
    for target, (row, count) in zip((g_mid, g_top, g_bottom), bands):
        for at, span, block, inside in blocks_of(tile_cols, width, rim):
            copies.append((acc.at[block, :, :, row : row + count, inside : inside + span], target.at[:, :, :, at : at + span]))
    copies.append((acc.at[0, :, :, :, :rim], g_left))
    copies.append((acc.at[last, :, :, :, rim:], g_right))
    copies = [pltpu.make_async_copy(a, b, sem.at[i]) for i, (a, b) in enumerate(copies)]
    for copy in copies:
        copy.start()
    for copy in copies:
        copy.wait()


def slot_gradients(rows, cols, bounds, mid, top, bottom, left, left_ends, right, right_ends, patterns, probe):
    width = probe.shape[-1]
    rim = width // 2
    slices, _, tile_rows, tile_cols = mid.shape
    blocks = (tile_cols + 2 * rim) // width
    smem = pl.BlockSpec(memory_space=pltpu.SMEM)
    vmem = pl.BlockSpec(memory_space=pltpu.VMEM)
    hbm = pl.BlockSpec(memory_space=pl.ANY)
    lefts, rights = tables(width)
    padded = (blocks, slices, 2, tile_rows + 2 * rim, width)
    row_part = jax.ShapeDtypeStruct(top.shape, F32)
    col_part = jax.ShapeDtypeStruct((slices, 2, tile_rows + 2 * rim, rim), F32)
    return pl.pallas_call(
        kernel_body,
        out_shape=(
            jax.ShapeDtypeStruct(mid.shape, F32), row_part, row_part, col_part, col_part,
            jax.ShapeDtypeStruct(probe.shape, F32),
        ),
        in_specs=[smem] * 3 + [hbm] * 7 + [vmem] * 4,
        out_specs=(hbm,) * 5 + (vmem,),
        scratch_shapes=[
            pltpu.VMEM(padded, F32),
            pltpu.VMEM(padded, F32),
            pltpu.SemaphoreType.DMA((3 * blocks + 6,)),
        ],
        compiler_params=pltpu.CompilerParams(vmem_limit_bytes=48 * 2**20),
        cost_estimate=pl.CostEstimate(flops=10**10, bytes_accessed=2 * 10**7, transcendentals=0),
    )(rows, cols, bounds, mid, top, bottom, left, left_ends, right, right_ends, patterns, probe, lefts, rights)


def send(x, axis, step):
    count = lax.axis_size(axis)
    return lax.ppermute(x, axis, [(i, i + step) for i in range(count) if 0 <= i + step < count])


def sum_everywhere(x, axes):
    flat = x.reshape(-1, x.shape[-1])
    done = []
    for axis in axes:
        count = lax.axis_size(axis)
        apart = 1
        while apart < count:
            bit = (lax.axis_index(axis) // apart) % 2
            half = flat.shape[0] // 2
            pairs = [(i, i ^ apart) for i in range(count)]
            mine = lax.dynamic_slice_in_dim(flat, bit * half, half, 0)
            other = lax.dynamic_slice_in_dim(flat, (1 - bit) * half, half, 0)
            flat = mine + lax.ppermute(other, axis, pairs)
            done.append((axis, pairs, bit))
            apart *= 2
    for axis, pairs, bit in reversed(done):
        other = lax.ppermute(flat, axis, pairs)
        low = jnp.where(bit == 0, flat, other)
        high = jnp.where(bit == 0, other, flat)
        flat = jnp.concatenate([low, high], axis=0)
    return flat.reshape(x.shape)


def per_device(object_slab, probe, patterns, centers, counts):
    tile_rows, tile_cols = object_slab.shape[2:]
    width = probe.shape[-1]
    rim = width // 2
    row_index = lax.axis_index("tx")
    col_index = lax.axis_index("ty")
    my_count = counts[row_index * lax.axis_size("ty") + col_index]
    bounds = jnp.stack([jnp.zeros((), jnp.int32), my_count])
    rows = centers[:, 0] - row_index * tile_rows
    cols = centers[:, 1] - col_index * tile_cols
    slots = patterns.shape[0]
    amplitudes = jnp.sqrt(patterns).reshape(slots, rim, 2, rim, 2).transpose(0, 2, 1, 4, 3).reshape(patterns.shape)

    top = send(object_slab[:, :, tile_rows - rim :], "tx", 1)
    bottom = send(object_slab[:, :, :rim], "tx", -1)
    left = send(object_slab[:, :, :, tile_cols - rim :], "ty", 1)
    right = send(object_slab[:, :, :, :rim], "ty", -1)
    ends = jnp.concatenate([top, bottom], axis=2)
    left_ends = send(ends[:, :, :, tile_cols - rim :], "ty", 1)
    right_ends = send(ends[:, :, :, :rim], "ty", -1)

    g_mid, g_top, g_bottom, g_left, g_right, g_probe = slot_gradients(
        rows, cols, bounds, object_slab, top, bottom, left, left_ends, right, right_ends, amplitudes, probe
    )

    from_left = send(g_right, "ty", 1)
    from_right = send(g_left, "ty", -1)

    def edges(x, first, last):
        x = x.at[:, :, :, :rim].add(from_left[:, :, first:last])
        return x.at[:, :, :, tile_cols - rim :].add(from_right[:, :, first:last])

    from_below = send(edges(g_top, 0, rim), "tx", -1)
    from_above = send(edges(g_bottom, tile_rows + rim, tile_rows + 2 * rim), "tx", 1)
    inner = edges(g_mid, rim, tile_rows + rim)
    inner = inner.at[:, :, :rim].add(from_above)
    inner = inner.at[:, :, tile_rows - rim :].add(from_below)
    probe_sum = sum_everywhere(g_probe, ("tx", "ty"))
    positions = jnp.maximum(jnp.sum(counts), 1).astype(F32)
    return (inner, probe_sum / jnp.sqrt(positions))


def solution(mesh):
    placed = (
        P(None, None, "tx", "ty"),
        P(),
        P(("tx", "ty"), None, None),
        P(("tx", "ty"), None),
        P(),
    )
    return jax.shard_map(
        per_device,
        mesh=mesh,
        in_specs=placed,
        out_specs=(P(None, None, "tx", "ty"), P()),
        check_vma=False,
    )
```

```python
import math

import jax
import jax.numpy as jnp
import ml_dtypes
import numpy as np
from jax import lax
from jax.experimental import pallas as pl
from jax.experimental.pallas import tpu as pltpu
from jax.sharding import PartitionSpec as P

KAPPA = 40.0
F32 = jnp.float32
FWD, INV, PROP, ADJ = 0, 1, 2, 3
LEFT = {FWD: (0, 2), INV: (1, 3), PROP: (4, 6), ADJ: (5, 7)}
RIGHT = {FWD: (1, 3), INV: (0, 2), PROP: (5, 7), ADJ: (4, 6)}


def tables(width):
    half = width // 2
    n = np.arange(half)
    freq = ((np.arange(width) + half) % width - half) / width
    factor = np.exp(-1j * math.pi * KAPPA * freq * freq)
    turn = 2j * np.pi / width
    scale = 1.0 / math.sqrt(width)
    even = np.exp(-turn * ((2 * n[:, None] * n[None, :]) % width)) * scale
    odd = np.exp(-turn * (((2 * n[:, None] + 1) * n[None, :]) % width)) * scale

    def combined(freqs):
        apart = n[:, None] - n[None, :]
        total = np.zeros((half, half), complex)
        for k in freqs:
            total += factor[k] * np.exp(turn * ((k * apart) % width))
        return total / width

    lefts, rights = [], []
    for c in (even, odd, combined(range(0, width, 2)), combined(range(1, width, 2))):
        real = np.block([[c.real, -c.imag], [c.imag, c.real]])
        for m in (real, real.T):
            hi = m.astype(ml_dtypes.bfloat16)
            lo = (m - hi.astype(np.float64)).astype(ml_dtypes.bfloat16)
            lefts.append(np.concatenate([hi, hi, lo], axis=1))
            rights.append(np.concatenate([hi, hi, lo], axis=0))
    return jnp.asarray(np.stack(lefts)), jnp.asarray(np.stack(rights))


def split(x):
    hi = x.astype(jnp.bfloat16)
    return hi, (x - hi.astype(F32)).astype(jnp.bfloat16)


def pair(x, y, axis):
    return jnp.concatenate([x, y], axis=axis)


def one_side(re, im, kind, axis, table):
    half = re.shape[axis] // 2

    def halves(x):
        return (x[:half], x[half:]) if axis == 0 else (x[:, :half], x[:, half:])

    a, b = halves(re)
    c, d = halves(im)
    if kind != INV:
        a, b, c, d = a + b, a - b, c + d, c - d

    def product(x, index):
        hi, lo = split(x)
        stacked = jnp.concatenate([hi, lo, hi], axis=axis)
        if axis == 0:
            return jnp.dot(table[index], stacked, preferred_element_type=F32)
        return jnp.dot(stacked, table[index], preferred_element_type=F32)

    even, odd = (LEFT if axis == 0 else RIGHT)[kind]
    a, c = halves(product(pair(a, c, axis), even))
    b, d = halves(product(pair(b, d, axis), odd))
    if kind == FWD:
        return pair(a, b, axis), pair(c, d, axis)
    return pair(a + b, a - b, axis), pair(c + d, c - d, axis)


def transform(re, im, kind, lefts, rights):
    re, im = one_side(re, im, kind, 1, rights)
    return one_side(re, im, kind, 0, lefts)


def times(a, b, c, d):
    return a * c - b * d, a * d + b * c


def conj_times(a, b, c, d):
    return a * c + b * d, a * d - b * c


def field_loop(wanted, place, rows, cols, counts, patterns, probe, lefts, rights, obj, acc, g_probe):
    width = probe.shape[-1]
    row_index = lax.broadcasted_iota(jnp.int32, (width, width), 0)
    col_index = lax.broadcasted_iota(jnp.int32, (width, width), 1)

    def visit(slot):
        row, col = rows[slot], cols[slot]
        block = place(col // width)
        shift = col % width
        below = row_index < row
        beside = col_index < shift

        def cut(level, part):
            upper = jnp.where(beside, obj[block + 1, level, part, :width], obj[block, level, part, :width])
            lower = jnp.where(beside, obj[block + 1, level, part, width:], obj[block, level, part, width:])
            return jnp.where(below, lower, upper)

        def deposit(level, part, term):
            zero = jnp.zeros_like(term)
            upper = jnp.where(below, zero, term)
            lower = jnp.where(below, term, zero)
            acc[block, level, part, :width] += jnp.where(beside, zero, upper)
            acc[block, level, part, width:] += jnp.where(beside, zero, lower)
            acc[block + 1, level, part, :width] += jnp.where(beside, upper, zero)
            acc[block + 1, level, part, width:] += jnp.where(beside, lower, zero)

        def rolled(x, down, along):
            return pltpu.roll(pltpu.roll(x, down, 0), along, 1)

        u0 = rolled(probe[0], row, shift), rolled(probe[1], row, shift)
        o0 = cut(0, 0), cut(0, 1)
        u1 = transform(*times(*u0, *o0), PROP, lefts, rights)
        o1 = cut(1, 0), cut(1, 1)
        far_re, far_im = transform(*times(*u1, *o1), FWD, lefts, rights)
        factor = 1.0 - patterns[slot] * lax.rsqrt(far_re * far_re + far_im * far_im + 1.0)
        chi = transform(far_re * factor, far_im * factor, INV, lefts, rights)
        for part, term in enumerate(conj_times(*u1, *chi)):
            deposit(1, part, term)
        chi = transform(*conj_times(*o1, *chi), ADJ, lefts, rights)
        for part, term in enumerate(conj_times(*u0, *chi)):
            deposit(0, part, term)
        up, back = (width - row) % width, (width - shift) % width
        for part, term in enumerate(conj_times(*o0, *chi)):
            g_probe[part] += rolled(term, up, back)

    def step(slot, _):
        pl.when(wanted(cols[slot] // width))(lambda: visit(slot))
        return 0

    lax.fori_loop(0, counts[0], step, 0)


def run_all(pairs, sem):
    copies = [pltpu.make_async_copy(a, b, sem.at[i]) for i, (a, b) in enumerate(pairs)]
    for copy in copies:
        copy.start()
    return copies


def wait_all(copies):
    for copy in copies:
        copy.wait()


def chosen_copy(flag, other, usual, target, sem):
    pl.when(flag == 1)(lambda: pltpu.make_async_copy(other, target, sem).start())
    pl.when(flag != 1)(lambda: pltpu.make_async_copy(usual, target, sem).start())
    return pltpu.make_async_copy(usual, target, sem)


def outer_body(
    rows, cols, counts, tile, top_ends, bottom_ends, top_quarters, bottom_quarters, relayed, left, left_ends, right,
    right_ends, patterns, probe, lefts, rights,
    g_tile_ends, g_top_ends, g_bottom_ends, g_left, g_right, g_quarters, g_probe, obj, acc, sem,
):
    width = probe.shape[-1]
    rim = width // 2
    tile_rows, tile_cols = tile.shape[2], tile.shape[3]
    full = tile_rows + 2 * rim
    last_block = (tile_cols + 2 * rim) // width - 2
    own = slice(rim, rim + tile_rows)
    below = slice(rim + tile_rows, full)
    one, two = slice(0, rim), slice(rim, width)
    pairs = []
    for k, lanes, first in ((0, two, 0), (1, slice(0, width), rim), (2, slice(0, width), tile_cols - rim - width), (3, one, tile_cols - rim)):
        span = lanes.stop - lanes.start
        pairs.append((tile.at[:, :, :, first : first + span], obj.at[k, :, :, own, lanes]))
    for k, lanes, first in ((0, two, 0), (3, one, rim)):
        pairs.append((top_ends.at[:, :, :, first : first + rim], obj.at[k, :, :, :rim, lanes]))
        pairs.append((bottom_ends.at[:, :, :, first : first + rim], obj.at[k, :, :, below, lanes]))
    for k, lanes, side, ends in ((0, one, left, left_ends), (3, two, right, right_ends)):
        pairs.append((side, obj.at[k, :, :, own, lanes]))
        pairs.append((ends.at[:, :, :rim], obj.at[k, :, :, :rim, lanes]))
        pairs.append((ends.at[:, :, rim:], obj.at[k, :, :, below, lanes]))
    copies = run_all(pairs, sem)
    at = len(copies)
    for k in (0, 1):
        lanes = slice(k * width, (k + 1) * width)
        for flag, usual, place in ((1, top_quarters, slice(0, rim)), (2, bottom_quarters, below)):
            copies.append(chosen_copy(counts[flag], relayed.at[:, :, :, lanes], usual.at[:, :, :, lanes], obj.at[1 + k, :, :, place], sem.at[at]))
            at += 1
    acc[...] = jnp.zeros_like(acc)
    g_probe[...] = jnp.zeros_like(g_probe)
    wait_all(copies)

    field_loop(
        lambda block: (block == 0) | (block == last_block), lambda block: jnp.where(block == 0, 0, 2),
        rows, cols, counts, patterns, probe, lefts, rights, obj, acc, g_probe,
    )

    pairs = [(acc.at[0, :, :, :, one], g_left), (acc.at[3, :, :, :, two], g_right), (acc.at[1:3], g_quarters)]
    for k, lanes, half in ((0, two, one), (3, one, two)):
        pairs.append((acc.at[k, :, :, own, lanes], g_tile_ends.at[:, :, :, half]))
        pairs.append((acc.at[k, :, :, :rim, lanes], g_top_ends.at[:, :, :, half]))
        pairs.append((acc.at[k, :, :, below, lanes], g_bottom_ends.at[:, :, :, half]))
    wait_all(run_all(pairs, sem))


def inner_body(
    rows, cols, counts, tile, top_quarters, bottom_quarters, relayed, top_mid, bottom_mid, patterns, probe, lefts, rights,
    carried, carried_probe,
    g_tile, g_top_quarters, g_bottom_quarters, g_relay, g_top_mid, g_bottom_mid, g_probe, obj, acc, sem,
):
    width = probe.shape[-1]
    rim = width // 2
    tile_rows, tile_cols = tile.shape[2], tile.shape[3]
    full = tile_rows + 2 * rim
    blocks = (tile_cols - 2 * rim) // width
    own = slice(rim, rim + tile_rows)
    below = slice(rim + tile_rows, full)
    last = blocks - 1
    pairs = [(carried.at[0], acc.at[0]), (carried.at[1], acc.at[last])]
    for k in range(blocks):
        pairs.append((tile.at[:, :, :, rim + k * width : rim + (k + 1) * width], obj.at[k, :, :, own]))
    for k in range(1, last):
        lanes = slice((k - 1) * width, k * width)
        pairs.append((top_mid.at[:, :, :, lanes], obj.at[k, :, :, :rim]))
        pairs.append((bottom_mid.at[:, :, :, lanes], obj.at[k, :, :, below]))
    copies = run_all(pairs, sem)
    at = len(copies)
    for k, block in ((0, 0), (1, last)):
        lanes = slice(k * width, (k + 1) * width)
        for flag, usual, place in ((1, top_quarters, slice(0, rim)), (2, bottom_quarters, below)):
            copies.append(chosen_copy(counts[flag], relayed.at[:, :, :, lanes], usual.at[:, :, :, lanes], obj.at[block, :, :, place], sem.at[at]))
            at += 1
    for k in range(1, last):
        acc[k] = jnp.zeros_like(acc[k])
    g_probe[...] = carried_probe[...]
    wait_all(copies)

    field_loop(
        lambda block: (block > 0) & (block < blocks), lambda block: block - 1,
        rows, cols, counts, patterns, probe, lefts, rights, obj, acc, g_probe,
    )

    pairs = []
    for k in range(blocks):
        pairs.append((acc.at[k, :, :, own], g_tile.at[:, :, :, k * width : (k + 1) * width]))
    for k, block in ((0, 0), (1, last)):
        lanes = slice(k * width, (k + 1) * width)
        pairs.append((acc.at[block, :, :, :rim], g_top_quarters.at[:, :, :, lanes]))
        pairs.append((acc.at[block, :, :, below], g_bottom_quarters.at[:, :, :, lanes]))
    for k in range(1, last):
        lanes = slice((k - 1) * width, k * width)
        pairs.append((acc.at[k, :, :, :rim], g_top_mid.at[:, :, :, lanes]))
        pairs.append((acc.at[k, :, :, below], g_bottom_mid.at[:, :, :, lanes]))
    copies = run_all(pairs, sem)
    at = len(copies)
    for k, block in ((0, 0), (1, last)):
        lanes = slice(k * width, (k + 1) * width)
        copies.append(chosen_copy(counts[1], acc.at[block, :, :, :rim], acc.at[block, :, :, below], g_relay.at[:, :, :, lanes], sem.at[at]))
        at += 1
    wait_all(copies)


SMEM = pl.BlockSpec(memory_space=pltpu.SMEM)
VMEM = pl.BlockSpec(memory_space=pltpu.VMEM)
HBM = pl.BlockSpec(memory_space=pl.ANY)


def shape(*dims):
    return jax.ShapeDtypeStruct(dims, F32)


def field_call(body, blocks, scalars, arrays, fields, extra, outs, probe, tile_rows, flops):
    width = probe.shape[-1]
    padded = (blocks, 2, 2, tile_rows + width, width)
    return pl.pallas_call(
        body,
        out_shape=tuple(outs) + (jax.ShapeDtypeStruct(probe.shape, F32),),
        in_specs=[SMEM] * len(scalars) + [HBM] * len(arrays) + [VMEM] * len(fields) + [HBM, VMEM][: len(extra)],
        out_specs=(HBM,) * len(outs) + (VMEM,),
        scratch_shapes=[pltpu.VMEM(padded, F32), pltpu.VMEM(padded, F32), pltpu.SemaphoreType.DMA((32,))],
        compiler_params=pltpu.CompilerParams(vmem_limit_bytes=48 * 2**20),
        cost_estimate=pl.CostEstimate(flops=flops, bytes_accessed=2 * 10**7, transcendentals=0),
    )(*scalars, *arrays, *fields, *extra)


def amplitude_body(counts, patterns, pick, out):
    def work():
        hi, lo = split(jnp.sqrt(patterns[0]))
        both = jnp.dot(pick[0], pair(hi, lo, 1), preferred_element_type=F32).astype(jnp.bfloat16)
        out[0] = jnp.dot(pair(both[:, : hi.shape[1]], both[:, hi.shape[1] :], 1), pick[1:].reshape(-1, hi.shape[1]), preferred_element_type=F32)

    pl.when(pl.program_id(0) < counts[0])(work)


def amplitudes_of(counts, patterns):
    width = patterns.shape[-1]
    pick = np.zeros((width, width))
    pick[np.arange(width), np.concatenate([np.arange(0, width, 2), np.arange(1, width, 2)])] = 1
    pick = jnp.asarray(np.stack([pick, pick.T, pick.T]).astype(ml_dtypes.bfloat16))
    block = pl.BlockSpec((1, width, width), lambda i: (i, 0, 0))
    return pl.pallas_call(
        amplitude_body,
        grid=(patterns.shape[0],),
        out_shape=jax.ShapeDtypeStruct(patterns.shape, F32),
        in_specs=[SMEM, block, VMEM],
        out_specs=block,
        cost_estimate=pl.CostEstimate(flops=10**9, bytes_accessed=2 * patterns.size * 4, transcendentals=0),
    )(counts, patterns, pick)


def total_body(counts, ends, mids, left, right, above_ends, below_ends, above_q, below_q, relay, above_mid, below_mid, out):
    rim = left.shape[-1]
    rows = ends.shape[2]
    cols = out.shape[3]
    mid = cols - 2 * rim
    quarter = above_q.shape[3] // 2
    for first, count, x_ends, x_q, x_mid, flag in (
        (0, rim, above_ends, above_q, above_mid, 1), (rows - rim, rim, below_ends, below_q, below_mid, 2),
    ):
        here = slice(first, first + count)
        there = slice(rim + first, rim + first + count)
        out[:, :, here, :rim] = ends[:, :, here, :rim] + left[:, :, there] + x_ends[:, :, :, :rim]
        out[:, :, here, cols - rim :] = ends[:, :, here, rim:] + right[:, :, there] + x_ends[:, :, :, rim:]
        side = jnp.where(counts[flag] == 1, relay[...], x_q[...])
        out[:, :, here, rim : rim + quarter] = mids[:, :, here, :quarter] + side[:, :, :, :quarter]
        out[:, :, here, cols - rim - quarter : cols - rim] = mids[:, :, here, mid - quarter :] + side[:, :, :, quarter:]
        out[:, :, here, rim + quarter : cols - rim - quarter] = mids[:, :, here, quarter : mid - quarter] + x_mid[...]


def total_of(counts, parts, tile_shape):
    def block(dims):
        return pl.BlockSpec((1, 1) + tuple(dims[2:]), lambda i, j: (i, j, 0, 0))

    return pl.pallas_call(
        total_body,
        grid=tile_shape[:2],
        out_shape=jax.ShapeDtypeStruct(tile_shape, F32),
        in_specs=[SMEM] + [block(x.shape) for x in parts],
        out_specs=block(tile_shape),
        compiler_params=pltpu.CompilerParams(vmem_limit_bytes=32 * 2**20),
        cost_estimate=pl.CostEstimate(flops=10**7, bytes_accessed=2 * 10**7, transcendentals=0),
    )(counts, *parts)


def send(x, axis, step, skip=None):
    count = lax.axis_size(axis)
    return lax.ppermute(x, axis, [(i, i + step) for i in range(count) if 0 <= i + step < count and i != skip])


def relay(x):
    count = lax.axis_size("tx")
    low = count // 2 - 1
    x = lax.ppermute(x, "tx", [(low, count - 1), (low + 1, 0)])
    return lax.ppermute(x, "tx", [(count - 1, low + 1), (0, low)])


def sum_everywhere(x):
    flat = x.reshape(-1, x.shape[-1])
    done = []
    count = lax.axis_size("tx")
    apart = 1
    while apart < count:
        bit = (lax.axis_index("tx") // apart) % 2
        half = flat.shape[0] // 2
        pairs = [(i, i ^ apart) for i in range(count)]
        mine = lax.dynamic_slice_in_dim(flat, bit * half, half, 0)
        other = lax.dynamic_slice_in_dim(flat, (1 - bit) * half, half, 0)
        flat = mine + lax.ppermute(other, "tx", pairs)
        done.append((pairs, bit))
        apart *= 2
    count = lax.axis_size("ty")
    held = flat
    for step in range(1, count):
        flat = flat + lax.ppermute(held, "ty", [(i, (i + step) % count) for i in range(count)])
    for pairs, bit in reversed(done):
        other = lax.ppermute(flat, "tx", pairs)
        low = jnp.where(bit == 0, flat, other)
        high = jnp.where(bit == 0, other, flat)
        flat = jnp.concatenate([low, high], axis=0)
    return flat.reshape(x.shape)


def per_device(object_slab, probe, patterns, centers, counts):
    slices, _, tile_rows, tile_cols = object_slab.shape
    width = probe.shape[-1]
    rim = width // 2
    row_index = lax.axis_index("tx")
    col_index = lax.axis_index("ty")
    middle = lax.axis_size("tx") // 2
    my_count = counts[row_index * lax.axis_size("ty") + col_index]
    flags = jnp.stack([my_count, (row_index == middle).astype(jnp.int32), (row_index == middle - 1).astype(jnp.int32)])
    rows = centers[:, 0] - row_index * tile_rows
    cols = centers[:, 1] - col_index * tile_cols
    quarter = rim + width
    low, high = object_slab[:, :, :rim], object_slab[:, :, tile_rows - rim :]

    def ends_of(x):
        return jnp.concatenate([x[..., :rim], x[..., tile_cols - rim :]], axis=3)

    def quarters_of(x):
        return jnp.concatenate([x[..., rim:quarter], x[..., tile_cols - quarter : tile_cols - rim]], axis=3)

    def mid_of(x):
        return x[..., quarter : tile_cols - quarter]

    top_ends = send(ends_of(high), "tx", 1)
    bottom_ends = send(ends_of(low), "tx", -1)
    left = send(object_slab[..., tile_cols - rim :], "ty", 1)
    right = send(object_slab[..., :rim], "ty", -1)
    facing = lax.dynamic_slice_in_dim(object_slab, jnp.where(row_index < middle, tile_rows - rim, 0), rim, 2)
    relayed = relay(quarters_of(facing))
    top_quarters = send(quarters_of(high), "tx", 1, middle - 1)
    bottom_quarters = send(quarters_of(low), "tx", -1, middle)
    ends = jnp.concatenate([top_ends, bottom_ends], axis=2)
    left_ends = send(ends[..., rim:], "ty", 1)
    right_ends = send(ends[..., :rim], "ty", -1)
    top_mid = send(mid_of(high), "tx", 1)
    bottom_mid = send(mid_of(low), "tx", -1)

    scalars = (rows, cols, flags)
    fields = (amplitudes_of(flags, patterns), probe) + tables(width)
    full = tile_rows + width
    mid_cols = tile_cols - 2 * quarter
    ends_shape = shape(slices, 2, rim, width)
    quarters_shape = shape(slices, 2, rim, 2 * width)
    mid_shape = shape(slices, 2, rim, mid_cols)
    side_shape = shape(slices, 2, full, rim)
    g_tile_ends, g_top_ends, g_bottom_ends, g_left, g_right, g_quarters, g_probe = field_call(
        outer_body, 4, scalars,
        (object_slab, top_ends, bottom_ends, top_quarters, bottom_quarters, relayed, left, left_ends, right, right_ends),
        fields, (),
        (shape(slices, 2, tile_rows, width), ends_shape, ends_shape, side_shape, side_shape, shape(2, slices, 2, full, width)),
        probe, tile_rows, 8 * 10**9,
    )
    from_left = send(g_right, "ty", 1)
    from_right = send(g_left, "ty", -1)
    g_tile, g_top_quarters, g_bottom_quarters, g_relay, g_top_mid, g_bottom_mid, g_probe = field_call(
        inner_body, (tile_cols - 2 * rim) // width, scalars,
        (object_slab, top_quarters, bottom_quarters, relayed, top_mid, bottom_mid),
        fields, (g_quarters, g_probe),
        (shape(slices, 2, tile_rows, tile_cols - 2 * rim), quarters_shape, quarters_shape, quarters_shape, mid_shape, mid_shape),
        probe, tile_rows, 8 * 10**9,
    )
    back = relay(g_relay)
    below_quarters = send(g_top_quarters, "tx", -1, middle)
    above_quarters = send(g_bottom_quarters, "tx", 1, middle - 1)
    below_mid = send(g_top_mid, "tx", -1)
    above_mid = send(g_bottom_mid, "tx", 1)

    def with_sides(x, first, last):
        return x + jnp.concatenate([from_left[:, :, first:last], from_right[:, :, first:last]], axis=3)

    below_ends = send(with_sides(g_top_ends, 0, rim), "tx", -1)
    above_ends = send(with_sides(g_bottom_ends, full - rim, full), "tx", 1)
    probe_sum = sum_everywhere(g_probe)
    inner = total_of(
        flags,
        (g_tile_ends, g_tile, from_left, from_right, above_ends, below_ends, above_quarters, below_quarters, back, above_mid, below_mid),
        object_slab.shape,
    )
    positions = jnp.maximum(jnp.sum(counts), 1).astype(F32)
    return (inner, probe_sum / jnp.sqrt(positions))


def solution(mesh):
    placed = (
        P(None, None, "tx", "ty"),
        P(),
        P(("tx", "ty"), None, None),
        P(("tx", "ty"), None),
        P(),
    )
    return jax.shard_map(
        per_device,
        mesh=mesh,
        in_specs=placed,
        out_specs=(P(None, None, "tx", "ty"), P()),
        check_vma=False,
    )
```

```python
import functools
import math

import jax
import jax.numpy as jnp
import ml_dtypes
import numpy as np
from jax import lax
from jax.experimental import pallas as pl
from jax.experimental.pallas import tpu as pltpu
from jax.sharding import PartitionSpec as P

KAPPA = 40.0
F32 = jnp.float32
FWD, INV, PROP, ADJ = 0, 1, 2, 3
LEFT = {FWD: (0, 2), INV: (1, 3), PROP: (4, 6), ADJ: (5, 7)}
RIGHT = {FWD: (1, 3), INV: (0, 2), PROP: (5, 7), ADJ: (4, 6)}


def tables(width):
    half = width // 2
    n = np.arange(half)
    freq = ((np.arange(width) + half) % width - half) / width
    factor = np.exp(-1j * math.pi * KAPPA * freq * freq)
    turn = 2j * np.pi / width
    scale = 1.0 / math.sqrt(width)
    even = np.exp(-turn * ((2 * n[:, None] * n[None, :]) % width)) * scale
    odd = np.exp(-turn * (((2 * n[:, None] + 1) * n[None, :]) % width)) * scale

    def combined(freqs):
        apart = n[:, None] - n[None, :]
        total = np.zeros((half, half), complex)
        for k in freqs:
            total += factor[k] * np.exp(turn * ((k * apart) % width))
        return total / width

    parts = []
    for c in (even, odd, combined(range(0, width, 2)), combined(range(1, width, 2))):
        real = np.block([[c.real, -c.imag], [c.imag, c.real]])
        for m in (real, real.T):
            hi = m.astype(ml_dtypes.bfloat16)
            lo = (m - hi.astype(np.float64)).astype(ml_dtypes.bfloat16)
            parts.append(np.concatenate([hi, lo], axis=0))
    return jnp.asarray(np.stack(parts))


def split(x):
    hi = x.astype(jnp.bfloat16)
    return hi, (x - hi.astype(F32)).astype(jnp.bfloat16)


def pair(x, y, axis):
    return jnp.concatenate([x, y], axis=axis)


def product(x, both, axis):
    size = both.shape[1]
    hi, lo = split(x)
    if axis == 0:
        first = jnp.dot(both, hi, preferred_element_type=F32)
        return first[:size] + first[size:] + jnp.dot(both[:size], lo, preferred_element_type=F32)
    first = jnp.dot(pair(hi, lo, 0), both[:size], preferred_element_type=F32)
    return first[: x.shape[0]] + first[x.shape[0] :] + jnp.dot(hi, both[size:], preferred_element_type=F32)


def one_side(re, im, kind, axis, table):
    half = re.shape[axis] // 2

    def halves(x):
        return (x[:half], x[half:]) if axis == 0 else (x[:, :half], x[:, half:])

    a, b = halves(re)
    c, d = halves(im)
    if kind != INV:
        a, b, c, d = a + b, a - b, c + d, c - d
    even, odd = (LEFT if axis == 0 else RIGHT)[kind]
    a, c = halves(product(pair(a, c, axis), table[even], axis))
    b, d = halves(product(pair(b, d, axis), table[odd], axis))
    if kind == FWD:
        return pair(a, b, axis), pair(c, d, axis)
    return pair(a + b, a - b, axis), pair(c + d, c - d, axis)


def transform(re, im, kind, table):
    re, im = one_side(re, im, kind, 1, table)
    return one_side(re, im, kind, 0, table)


def times(a, b, c, d):
    return a * c - b * d, a * d + b * c


def conj_times(a, b, c, d):
    return a * c + b * d, a * d - b * c


def visit(start, block, amplitude, probe, table, obj, acc, g_probe):
    width = probe.shape[-1]
    row, shift = start[0], start[1] % width
    below = lax.broadcasted_iota(jnp.int32, (width, width), 0) < row
    beside = lax.broadcasted_iota(jnp.int32, (width, width), 1) < shift

    def cut(level, part):
        upper = jnp.where(beside, obj[block + 1, level, part, :width], obj[block, level, part, :width])
        lower = jnp.where(beside, obj[block + 1, level, part, width:], obj[block, level, part, width:])
        return jnp.where(below, lower, upper)

    def deposit(level, part, term):
        zero = jnp.zeros_like(term)
        upper = jnp.where(below, zero, term)
        lower = jnp.where(below, term, zero)
        acc[block, level, part, :width] += jnp.where(beside, zero, upper)
        acc[block, level, part, width:] += jnp.where(beside, zero, lower)
        acc[block + 1, level, part, :width] += jnp.where(beside, upper, zero)
        acc[block + 1, level, part, width:] += jnp.where(beside, lower, zero)

    def rolled(x, down, along):
        return pltpu.roll(pltpu.roll(x, down, 0), along, 1)

    u0 = rolled(probe[0], row, shift), rolled(probe[1], row, shift)
    o0 = cut(0, 0), cut(0, 1)
    u1 = transform(*times(*u0, *o0), PROP, table)
    o1 = cut(1, 0), cut(1, 1)
    far_re, far_im = transform(*times(*u1, *o1), FWD, table)
    factor = 1.0 - amplitude() * lax.rsqrt(far_re * far_re + far_im * far_im + 1.0)
    chi = transform(far_re * factor, far_im * factor, INV, table)
    for part, term in enumerate(conj_times(*u1, *chi)):
        deposit(1, part, term)
    chi = transform(*conj_times(*o1, *chi), ADJ, table)
    for part, term in enumerate(conj_times(*u0, *chi)):
        deposit(0, part, term)
    up, back = (width - row) % width, (width - shift) % width
    for part, term in enumerate(conj_times(*o0, *chi)):
        g_probe[part] += rolled(term, up, back)


class Place:
    def __init__(self, axes, scalars, tile_rows, tile_cols, rim):
        down, along, self.centers, counts = scalars
        tx, ty = down[0], along[0]
        odd = tx % 2
        self.count = counts[tx * axes[1] + ty]
        self.relayed = (tx == axes[0] // 2) | (tx == axes[0] // 2 - 1)
        self.first = tx * tile_rows, ty * tile_cols
        inner = tile_rows - rim
        self.on_tile, self.off_tile = rows_at((1 - odd) * inner, rim), rows_at(odd * inner, rim)
        outer = tile_rows + rim
        self.on, self.off = rows_at((1 - odd) * outer, rim), rows_at(odd * outer, rim)

    def start(self, slot):
        return self.centers[slot, 0] - self.first[0], self.centers[slot, 1] - self.first[1]


def rows_at(first, count):
    return pl.ds(pl.multiple_of(first, count), count)


def start_all(pairs, sem, at):
    copies = [pltpu.make_async_copy(a, b, sem.at[at + i]) for i, (a, b) in enumerate(pairs)]
    for copy in copies:
        copy.start()
    return copies


def run_all(pairs, sem):
    return start_all(pairs, sem, 0)


def wait_all(copies):
    for copy in copies:
        copy.wait()


def start_chosen(flag, other, usual, pairs, sem, at):
    for k, (lanes, target) in enumerate(pairs):
        for here, source in ((flag, other), (jnp.logical_not(flag), usual)):
            pl.when(here)(lambda s=source.at[:, :, :, lanes], t=target, i=at + k: pltpu.make_async_copy(s, t, sem.at[i]).start())
    return [pltpu.make_async_copy(usual.at[:, :, :, lanes], target, sem.at[at + k]) for k, (lanes, target) in enumerate(pairs)]


def two_groups(here, firsts, step, loads, stores, amplitudes, amps, amp_sem, sem, probe, table, obj, acc, g_probe):
    width = probe.shape[-1]

    def mine(slot, g):
        return here.start(slot)[1] // width == jnp.where(g == 0, firsts[0], firsts[1])

    def amplitude_copy(slot):
        return pltpu.make_async_copy(amplitudes.at[slot], amps.at[slot], amp_sem.at[slot])

    def fetch(slot, _):
        pl.when(mine(slot, 0) | mine(slot, 1))(lambda: amplitude_copy(slot).start())
        return 0

    lax.fori_loop(0, here.count, fetch, 0)

    def group(g, _):
        for k in (0, 1):
            pl.when(g == k)(functools.partial(wait_all, loads[k]))

        def work(slot):
            def amplitude():
                amplitude_copy(slot).wait()
                return amps[slot]

            visit(here.start(slot), step * g, amplitude, probe, table, obj, acc, g_probe)

        def each(slot, _):
            pl.when(mine(slot, g))(lambda: work(slot))
            return 0

        lax.fori_loop(0, here.count, each, 0)
        for k in (0, 1):
            pl.when(g == k)(lambda k=k: start_all(stores[k], sem, k * len(stores[0])) and None)
        return 0

    lax.fori_loop(0, 2, group, 0)
    for k in (0, 1):
        wait_all([pltpu.make_async_copy(a, b, sem.at[k * len(stores[0]) + i]) for i, (a, b) in enumerate(stores[k])])


def inner_body(
    axes, tx, ty, centers, counts, tile, on, off_quarters, relayed, off_mid, amplitudes, probe_in, table_in,
    g_quarters, g_tile_mid, g_on_mid, g_off_mid, g_probe, obj, acc, probe, table, amps, sem, out_sem, amp_sem,
):
    width = probe.shape[-1]
    rim = width // 2
    tile_rows, tile_cols = tile.shape[2], tile.shape[3]
    here = Place(axes, (tx, ty, centers, counts), tile_rows, tile_cols, rim)
    own = slice(rim, rim + tile_rows)
    loads = ([(probe_in, probe), (table_in, table)], [])
    for k in range(3):
        there = slice(rim + k * width, rim + (k + 1) * width)
        loads[k // 2].append((tile.at[:, :, :, there], obj.at[k, :, :, own]))
        loads[k // 2].append((on.at[:, :, :, (k + 1) * width : (k + 2) * width], obj.at[k, :, :, here.on]))
    loads[0].append((off_mid, obj.at[1, :, :, here.off]))
    waits = []
    for k in (0, 1):
        at = 16 * k
        started = start_all(loads[k], sem, at)
        lanes = slice(k * width, (k + 1) * width)
        waits.append(started + start_chosen(here.relayed, relayed, off_quarters, [(lanes, obj.at[2 * k, :, :, here.off])], sem, at + len(started)))
    acc[...] = jnp.zeros_like(acc)
    g_probe[...] = jnp.zeros_like(g_probe)
    stores = (
        [(acc.at[0], g_quarters.at[0])],
        [
            (acc.at[2], g_quarters.at[1]),
            (acc.at[1, :, :, own], g_tile_mid),
            (acc.at[1, :, :, here.on], g_on_mid),
            (acc.at[1, :, :, here.off], g_off_mid),
        ],
    )
    two_groups(here, (1, 2), 1, waits, stores, amplitudes, amps, amp_sem, out_sem, probe, table, obj, acc, g_probe)


def outer_body(
    axes, tx, ty, centers, counts, tile, on, off_quarters, relayed, off_ends, left, right, carried, carried_probe, amplitudes, probe_in, table_in,
    g_tile_ends, g_tile_quarters, g_on_ends, g_on_quarters, g_off_ends, g_off_quarters, g_left, g_right, g_probe,
    obj, acc, probe, table, amps, sem, out_sem, amp_sem,
):
    width = probe.shape[-1]
    rim = width // 2
    tile_rows, tile_cols = tile.shape[2], tile.shape[3]
    here = Place(axes, (tx, ty, centers, counts), tile_rows, tile_cols, rim)
    own = slice(rim, rim + tile_rows)
    one, two = slice(0, rim), slice(rim, width)
    waits, stores = [], []
    for k, (end, quarter, near, far, half, side, g_side) in enumerate((
        (0, 1, two, slice(0, rim), one, left, g_left),
        (3, 2, one, slice(tile_cols - rim, tile_cols), two, right, g_right),
    )):
        first = rim if k == 0 else tile_cols - rim - width
        there = slice(first, first + width)
        edge = k * tile_cols
        loads = [(probe_in, probe), (table_in, table), (carried_probe, g_probe)] if k == 0 else []
        loads += [
            (tile.at[:, :, :, far], obj.at[end, :, :, own, near]),
            (side, obj.at[end, :, :, own, half]),
            (on.at[:, :, :, edge : edge + width], obj.at[end, :, :, here.on]),
            (off_ends.at[:, :, :, k * width : (k + 1) * width], obj.at[end, :, :, here.off]),
            (tile.at[:, :, :, there], obj.at[quarter, :, :, own]),
            (on.at[:, :, :, first + rim : first + rim + width], obj.at[quarter, :, :, here.on]),
            (carried.at[k], acc.at[quarter]),
        ]
        started = start_all(loads, sem, 16 * k)
        lanes = slice(k * width, (k + 1) * width)
        waits.append(started + start_chosen(here.relayed, relayed, off_quarters, [(lanes, obj.at[quarter, :, :, here.off])], sem, 16 * k + len(started)))
        stores.append([
            (acc.at[end, :, :, own, near], g_tile_ends.at[:, :, :, half]),
            (acc.at[end, :, :, here.on, near], g_on_ends.at[:, :, :, half]),
            (acc.at[end, :, :, here.off, near], g_off_ends.at[:, :, :, half]),
            (acc.at[end, :, :, :, half], g_side),
            (acc.at[quarter, :, :, own], g_tile_quarters.at[:, :, :, lanes]),
            (acc.at[quarter, :, :, here.on], g_on_quarters.at[:, :, :, lanes]),
            (acc.at[quarter, :, :, here.off], g_off_quarters.at[:, :, :, lanes]),
        ])
    for end in (0, 3):
        acc[end] = jnp.zeros_like(acc[end])
    last_block = (tile_cols + 2 * rim) // width - 2
    two_groups(here, (0, last_block), 2, waits, stores, amplitudes, amps, amp_sem, out_sem, probe, table, obj, acc, g_probe)


SMEM = pl.BlockSpec(memory_space=pltpu.SMEM)
VMEM = pl.BlockSpec(memory_space=pltpu.VMEM)
HBM = pl.BlockSpec(memory_space=pl.ANY)
ROOM = pltpu.CompilerParams(vmem_limit_bytes=60 * 2**20)


def shape(*dims):
    return jax.ShapeDtypeStruct(dims, F32)


def costs(flops):
    return pl.CostEstimate(flops=flops, bytes_accessed=10**7, transcendentals=0)


def field_call(body, axes, blocks, scalars, arrays, amplitudes, probe, outs, tile_rows):
    width = probe.shape[-1]
    padded = (blocks, 2, 2, tile_rows + width, width)
    table = tables(width)
    return pl.pallas_call(
        functools.partial(body, axes),
        out_shape=tuple(outs) + (jax.ShapeDtypeStruct(probe.shape, F32),),
        in_specs=[SMEM] * len(scalars) + [HBM] * (len(arrays) + 3),
        out_specs=(HBM,) * len(outs) + (VMEM,),
        scratch_shapes=[
            pltpu.VMEM(padded, F32),
            pltpu.VMEM(padded, F32),
            pltpu.VMEM(probe.shape, F32),
            pltpu.VMEM(table.shape, table.dtype),
            pltpu.VMEM(amplitudes.shape, F32),
            pltpu.SemaphoreType.DMA((32,)),
            pltpu.SemaphoreType.DMA((16,)),
            pltpu.SemaphoreType.DMA((amplitudes.shape[0],)),
        ],
        compiler_params=ROOM,
        cost_estimate=costs(2 * 10**10),
    )(*scalars, *arrays, amplitudes, probe, table)


def pack_body(tx, tile, left, right, quarters, mid, sem):
    rim = left.shape[-1]
    width = 2 * rim
    tile_rows, tile_cols = tile.shape[2], tile.shape[3]
    rows = rows_at((tx[0] % 2) * (tile_rows - rim), rim)
    quarter = rim + width
    far = tile_cols - quarter
    wait_all(run_all([
        (tile.at[:, :, :, :rim], left),
        (tile.at[:, :, :, tile_cols - rim :], right),
        (tile.at[:, :, rows, rim:quarter], quarters.at[:, :, :, :width]),
        (tile.at[:, :, rows, far : far + width], quarters.at[:, :, :, width:]),
        (tile.at[:, :, rows, quarter:far], mid),
    ], sem))


def strips_body(tx, tile, left, right, on, ends, sem):
    rim = left.shape[-1]
    tile_rows, tile_cols = tile.shape[2], tile.shape[3]
    odd = tx[0] % 2
    inner = tile_rows - rim
    on_rows, off_rows = rows_at((1 - odd) * inner, rim), rows_at(odd * inner, rim)
    wait_all(run_all([
        (left.at[:, :, on_rows], on.at[:, :, :, :rim]),
        (tile.at[:, :, on_rows], on.at[:, :, :, rim : rim + tile_cols]),
        (right.at[:, :, on_rows], on.at[:, :, :, rim + tile_cols :]),
        (left.at[:, :, off_rows], ends.at[:, :, :, :rim]),
        (tile.at[:, :, off_rows, :rim], ends.at[:, :, :, rim : 2 * rim]),
        (tile.at[:, :, off_rows, tile_cols - rim :], ends.at[:, :, :, 2 * rim : 3 * rim]),
        (right.at[:, :, off_rows], ends.at[:, :, :, 3 * rim :]),
    ], sem))


def copies_call(body, scalars, arrays, outs, flops):
    return pl.pallas_call(
        body,
        out_shape=tuple(outs),
        in_specs=[SMEM] * len(scalars) + [HBM] * len(arrays),
        out_specs=(VMEM,) * len(outs),
        scratch_shapes=[pltpu.SemaphoreType.DMA((8,))],
        compiler_params=ROOM,
        cost_estimate=costs(flops),
    )(*scalars, *arrays)


def amplitude_body(axes, tx, ty, counts, patterns, pick, out):
    width = patterns.shape[-1]

    def work():
        hi, lo = split(jnp.sqrt(patterns[0]))
        both = jnp.dot(pick[0], pair(hi, lo, 1), preferred_element_type=F32).astype(jnp.bfloat16)
        out[0] = jnp.dot(both, pick[1:].reshape(-1, width), preferred_element_type=F32)

    pl.when(pl.program_id(0) < counts[tx[0] * axes[1] + ty[0]])(work)


def amplitudes_of(axes, scalars, patterns):
    width = patterns.shape[-1]
    pick = np.zeros((width, width))
    pick[np.arange(width), np.concatenate([np.arange(0, width, 2), np.arange(1, width, 2)])] = 1
    pick = jnp.asarray(np.stack([pick, pick.T, pick.T]).astype(ml_dtypes.bfloat16))
    block = pl.BlockSpec((1, width, width), lambda i: (i, 0, 0))
    return pl.pallas_call(
        functools.partial(amplitude_body, axes),
        grid=(patterns.shape[0],),
        out_shape=jax.ShapeDtypeStruct(patterns.shape, F32),
        in_specs=[SMEM, SMEM, SMEM, block, VMEM],
        out_specs=block,
        compiler_params=ROOM,
        cost_estimate=costs(10**11),
    )(*scalars, patterns, pick)


def merge_body(tx, on_ends, off_ends, left, right, quarters, mid, on, off, sides, sem):
    rim = left.shape[-1]
    width = 2 * rim
    below = left.shape[2] - rim
    odd = tx[0] % 2
    on_rows, off_rows = rows_at((1 - odd) * below, rim), rows_at(odd * below, rim)
    wait_all(run_all([
        (on_ends, on.at[:, :, :, :width]),
        (quarters, on.at[:, :, :, width : 3 * width]),
        (mid, on.at[:, :, :, 3 * width :]),
        (off_ends, off),
        (left.at[:, :, on_rows], sides.at[0, :, :, :, :rim]),
        (right.at[:, :, on_rows], sides.at[0, :, :, :, rim:]),
        (left.at[:, :, off_rows], sides.at[1, :, :, :, :rim]),
        (right.at[:, :, off_rows], sides.at[1, :, :, :, rim:]),
    ], sem))
    on[:, :, :, :width] += sides[0]
    off[...] += sides[1]


def merged(tx, on_ends, off_ends, left, right, quarters, mid):
    slices, _, rim, width = on_ends.shape
    cols = width + quarters.shape[3] + mid.shape[3]
    return pl.pallas_call(
        merge_body,
        out_shape=(shape(slices, 2, rim, cols), jax.ShapeDtypeStruct(off_ends.shape, F32)),
        in_specs=[SMEM] + [HBM] * 6,
        out_specs=(VMEM, VMEM),
        scratch_shapes=[pltpu.VMEM((2,) + on_ends.shape, F32), pltpu.SemaphoreType.DMA((8,))],
        compiler_params=ROOM,
        cost_estimate=costs(10**11),
    )(tx, on_ends, off_ends, left, right, quarters, mid)


def halves_body(tx, x, mine, other):
    half = mine.shape[0]
    bit = tx[0] % 2
    mine[...] = x[rows_at(bit * half, half)]
    other[...] = x[rows_at((1 - bit) * half, half)]


def halves_of(tx, x):
    half = shape(x.shape[0] // 2, x.shape[1])
    return pl.pallas_call(
        halves_body,
        out_shape=(half, half),
        in_specs=[SMEM, VMEM],
        out_specs=(VMEM, VMEM),
        compiler_params=ROOM,
        cost_estimate=costs(10**11),
    )(tx, x)


def scaled_body(counts, *refs):
    parts, out = refs[:-1], refs[-1]
    positions = lax.fori_loop(0, counts.shape[0], lambda i, n: n + counts[i], jnp.zeros((), jnp.int32))
    total = parts[0][...]
    for part in parts[1:]:
        total += part[...]
    out[...] = total / jnp.sqrt(jnp.full(out.shape, jnp.maximum(positions, 1).astype(F32)))


def scaled_sum(counts, parts):
    return pl.pallas_call(
        scaled_body,
        out_shape=jax.ShapeDtypeStruct(parts[0].shape, F32),
        in_specs=[SMEM] + [VMEM] * len(parts),
        out_specs=VMEM,
        compiler_params=ROOM,
        cost_estimate=costs(10**8),
    )(counts, *parts)


def total_body(tx, ends, quarters, mid, left, right, on, off_quarters, off_ends, off_mid, out):
    rim = left.shape[-1]
    rows, cols = out.shape[2:]
    width = 2 * rim
    one, five = slice(0, rim), slice(cols - rim, cols)
    two, four = slice(rim, rim + width), slice(cols - rim - width, cols - rim)
    three = slice(rim + width, cols - rim - width)
    odd = tx[0] % 2
    out[0, 0, :, one] = ends[0, 0, :, :rim] + left[0, 0, rim : rim + rows]
    out[0, 0, :, five] = ends[0, 0, :, rim:] + right[0, 0, rim : rim + rows]
    out[0, 0, :, two] = quarters[0, 0, :, :width]
    out[0, 0, :, four] = quarters[0, 0, :, width:]
    out[0, 0, :, three] = mid[0, 0]
    here = rows_at((1 - odd) * (rows - rim), rim)
    out[0, 0, here, one] += on[0, 0, :, :rim]
    out[0, 0, here, five] += on[0, 0, :, rim:width]
    out[0, 0, here, two] += on[0, 0, :, width : 2 * width]
    out[0, 0, here, four] += on[0, 0, :, 2 * width : 3 * width]
    out[0, 0, here, three] += on[0, 0, :, 3 * width :]
    here = rows_at(odd * (rows - rim), rim)
    out[0, 0, here, one] += off_ends[0, 0, :, :rim]
    out[0, 0, here, five] += off_ends[0, 0, :, rim:]
    out[0, 0, here, two] += off_quarters[0, 0, :, :width]
    out[0, 0, here, four] += off_quarters[0, 0, :, width:]
    out[0, 0, here, three] += off_mid[0, 0]


def total_of(tx, parts, tile_shape):
    def block(dims):
        return pl.BlockSpec((1, 1) + tuple(dims[2:]), lambda i, j: (i, j, 0, 0))

    return pl.pallas_call(
        total_body,
        grid=tile_shape[:2],
        out_shape=jax.ShapeDtypeStruct(tile_shape, F32),
        in_specs=[SMEM] + [block(x.shape) for x in parts],
        out_specs=block(tile_shape),
        compiler_params=ROOM,
        cost_estimate=costs(10**11),
    )(tx, *parts)


def along(x, step):
    count = lax.axis_size("ty")
    return lax.ppermute(x, "ty", [(i, i + step) for i in range(count) if 0 <= i + step < count])


def across(x, first, skip=None):
    pairs = []
    for i in range(first, lax.axis_size("tx") - 1, 2):
        if i != skip:
            pairs += [(i, i + 1), (i + 1, i)]
    return lax.ppermute(x, "tx", pairs)


def relay_out(x):
    count = lax.axis_size("tx")
    return lax.ppermute(x, "tx", [(count // 2 - 1, count - 1), (count // 2, 0)])


def relay_in(x):
    count = lax.axis_size("tx")
    return lax.ppermute(x, "tx", [(count - 1, count // 2), (0, count // 2 - 1)])


def after(x, *others):
    return lax.optimization_barrier((x,) + others)[0]


def halved(flat, apart):
    bit = (lax.axis_index("tx") // apart) % 2
    half = flat.shape[0] // 2
    pairs = [(i, i ^ apart) for i in range(lax.axis_size("tx"))]
    mine = lax.dynamic_slice_in_dim(flat, bit * half, half, 0)
    other = lax.dynamic_slice_in_dim(flat, (1 - bit) * half, half, 0)
    return mine + lax.ppermute(other, "tx", pairs)


def joined_body(apart, tx, *refs):
    pieces, out = refs[:-1], refs[-1]
    rows = out.shape[0] // len(pieces)
    mine = sum(((tx[0] // step) % 2) * 2**k for k, step in enumerate(apart))
    for i, piece in enumerate(pieces):
        out[rows_at((mine ^ i) * rows, rows)] = piece[...]


def spread(flat, apart, count):
    pieces = [flat]
    for i in range(1, 2 ** len(apart)):
        flip = sum(step for k, step in enumerate(apart) if i >> k & 1)
        pieces.append(lax.ppermute(flat, "tx", [(j, j ^ flip) for j in range(count)]))
    return pieces


def joined(tx, pieces, apart):
    rows, cols = pieces[0].shape
    return pl.pallas_call(
        functools.partial(joined_body, apart),
        out_shape=shape(rows * len(pieces), cols),
        in_specs=[SMEM] + [VMEM] * len(pieces),
        out_specs=VMEM,
        compiler_params=ROOM,
        cost_estimate=costs(10**8),
    )(tx, *pieces)


def per_device(object_slab, probe, patterns, centers, counts):
    slices, _, tile_rows, tile_cols = object_slab.shape
    width = probe.shape[-1]
    rim = width // 2
    axes = lax.axis_size("tx"), lax.axis_size("ty")
    middle = axes[0] // 2
    tx, ty = (lax.axis_index(axis).astype(jnp.int32).reshape(1) for axis in ("tx", "ty"))
    full = tile_rows + width
    mid_cols = tile_cols - 3 * width
    ends_shape = shape(slices, 2, rim, width)
    quarters_shape = shape(slices, 2, rim, 2 * width)
    mid_shape = shape(slices, 2, rim, mid_cols)
    side_shape = shape(slices, 2, full, rim)
    tile = object_slab

    column_shape = shape(slices, 2, tile_rows, rim)
    to_left, to_right, quarters, mid = copies_call(
        pack_body, (tx,), (tile,), (column_shape, column_shape, quarters_shape, mid_shape), 10**8
    )
    carried = relay_out(quarters)
    left, right = along(to_right, 1), along(to_left, -1)
    off_quarters = across(quarters, 1, middle - 1)
    off_mid = across(mid, 1)
    amplitudes = amplitudes_of(axes, (tx, ty, counts), after(patterns, to_left))
    on_shape = shape(slices, 2, rim, tile_cols + width)

    def strips(tile, left, right):
        on, ends = copies_call(strips_body, (tx,), (tile, left, right), (on_shape, quarters_shape), 10**8)
        return across(on, 0), ends

    def nothing(tile, left, right):
        return jnp.zeros(on_shape.shape, F32), jnp.zeros(quarters_shape.shape, F32)

    relayed = relay_in(carried)
    on, ends = lax.cond(counts[0] >= 0, strips, nothing, after(tile, amplitudes, carried), left, right)
    off_ends = across(ends, 1)

    scalars = (tx, ty, centers, counts)
    g_quarters, g_tile_mid, g_on_mid, g_off_mid, g_probe = field_call(
        inner_body, axes, 3, scalars, (tile, on, off_quarters, relayed, off_mid), amplitudes, probe,
        (shape(2, slices, 2, full, width), shape(slices, 2, tile_rows, mid_cols), mid_shape, mid_shape), tile_rows,
    )
    back_mid = across(g_off_mid, 1)
    g_tile_ends, g_tile_quarters, g_on_ends, g_on_quarters, g_off_ends, g_off_quarters, g_left, g_right, g_probe = field_call(
        outer_body, axes, 4, scalars, (tile, on, off_quarters, relayed, off_ends, left, right, g_quarters, g_probe), amplitudes, probe,
        (
            shape(slices, 2, tile_rows, width), shape(slices, 2, tile_rows, 2 * width), ends_shape, quarters_shape,
            ends_shape, quarters_shape, side_shape, side_shape,
        ),
        tile_rows,
    )
    from_left = along(g_right, 1)
    from_right = along(g_left, -1)
    back_quarters = across(g_off_quarters, 1)

    apart = [2**k for k in range(1, axes[0].bit_length() - 1)]
    mine, other = halves_of(tx, after(g_probe.reshape(-1, width), back_mid))
    flat = mine + lax.ppermute(other, "tx", [(i, i ^ 1) for i in range(axes[0])])
    for step in reversed(apart):
        flat = halved(flat, step)
    on_all, off_ends = merged(tx, after(g_on_ends, back_quarters, flat), g_off_ends, from_left, from_right, g_on_quarters, g_on_mid)
    back_ends = across(off_ends, 1)
    back_on = across(on_all, 0)
    flat = after(flat, on_all)
    others = [lax.ppermute(flat, "ty", [(i, (i + step) % axes[1]) for i in range(axes[1])]) for step in range(1, axes[1])]
    flat = after(scaled_sum(counts, (flat, *others)), back_ends, back_on)
    inner = total_of(
        tx,
        (g_tile_ends, g_tile_quarters, g_tile_mid, from_left, from_right, back_on, back_quarters, back_ends, back_mid),
        tile.shape,
    )
    pieces = spread(flat, apart[:2], axes[0])
    pieces = after(pieces[0], inner), *pieces[1:]
    while apart:
        flat = joined(tx, pieces, apart[:2])
        apart = apart[2:]
        pieces = spread(flat, apart[:2] or [1], axes[0])
    probe_sum = joined(tx, pieces, [1]).reshape(probe.shape)
    return (inner, probe_sum)


def solution(mesh):
    placed = (
        P(None, None, "tx", "ty"),
        P(),
        P(("tx", "ty"), None, None),
        P(("tx", "ty"), None),
        P(),
    )
    return jax.shard_map(
        per_device,
        mesh=mesh,
        in_specs=placed,
        out_specs=(P(None, None, "tx", "ty"), P()),
        check_vma=False,
    )
```

```python
import functools
import math

import jax
import jax.numpy as jnp
import ml_dtypes
import numpy as np
from jax import lax
from jax.experimental import pallas as pl
from jax.experimental.pallas import tpu as pltpu
from jax.sharding import PartitionSpec as P

KAPPA = 40.0
F32 = jnp.float32
FWD, INV, PROP, ADJ = 0, 1, 2, 3
LEFT = {FWD: (0, 2), INV: (1, 3), PROP: (4, 6), ADJ: (5, 7)}
RIGHT = {FWD: (1, 3), INV: (0, 2), PROP: (5, 7), ADJ: (4, 6)}


def tables(width):
    half = width // 2
    n = np.arange(half)
    freq = ((np.arange(width) + half) % width - half) / width
    factor = np.exp(-1j * math.pi * KAPPA * freq * freq)
    turn = 2j * np.pi / width
    scale = 1.0 / math.sqrt(width)
    even = np.exp(-turn * ((2 * n[:, None] * n[None, :]) % width)) * scale
    odd = np.exp(-turn * (((2 * n[:, None] + 1) * n[None, :]) % width)) * scale

    def combined(freqs):
        apart = n[:, None] - n[None, :]
        total = np.zeros((half, half), complex)
        for k in freqs:
            total += factor[k] * np.exp(turn * ((k * apart) % width))
        return total / width

    parts = []
    for c in (even, odd, combined(range(0, width, 2)), combined(range(1, width, 2))):
        real = np.block([[c.real, -c.imag], [c.imag, c.real]])
        for m in (real, real.T):
            hi = m.astype(ml_dtypes.bfloat16)
            lo = (m - hi.astype(np.float64)).astype(ml_dtypes.bfloat16)
            parts.append(np.concatenate([hi, lo], axis=0))
    return jnp.asarray(np.stack(parts))


def split(x):
    hi = x.astype(jnp.bfloat16)
    return hi, (x - hi.astype(F32)).astype(jnp.bfloat16)


def pair(x, y, axis):
    return jnp.concatenate([x, y], axis=axis)


def product(x, both, axis):
    size = both.shape[1]
    hi, lo = split(x)
    if axis == 0:
        first = jnp.dot(both, hi, preferred_element_type=F32)
        return first[:size] + first[size:] + jnp.dot(both[:size], lo, preferred_element_type=F32)
    first = jnp.dot(pair(hi, lo, 0), both[:size], preferred_element_type=F32)
    return first[: x.shape[0]] + first[x.shape[0] :] + jnp.dot(hi, both[size:], preferred_element_type=F32)


def one_side(re, im, kind, axis, table):
    half = re.shape[axis] // 2

    def halves(x):
        return (x[:half], x[half:]) if axis == 0 else (x[:, :half], x[:, half:])

    a, b = halves(re)
    c, d = halves(im)
    if kind != INV:
        a, b, c, d = a + b, a - b, c + d, c - d
    even, odd = (LEFT if axis == 0 else RIGHT)[kind]
    a, c = halves(product(pair(a, c, axis), table[even], axis))
    b, d = halves(product(pair(b, d, axis), table[odd], axis))
    if kind == FWD:
        return pair(a, b, axis), pair(c, d, axis)
    return pair(a + b, a - b, axis), pair(c + d, c - d, axis)


def transform(re, im, kind, table):
    re, im = one_side(re, im, kind, 1, table)
    return one_side(re, im, kind, 0, table)


def times(a, b, c, d):
    return a * c - b * d, a * d + b * c


def conj_times(a, b, c, d):
    return a * c + b * d, a * d - b * c


class Slot:
    def __init__(self, start, block, amplitude, obj, acc):
        width = obj.shape[-1]
        self.width, self.block, self.amplitude, self.obj, self.acc = width, block, amplitude, obj, acc
        self.row, self.shift = start[0], start[1] % width
        self.below = lax.broadcasted_iota(jnp.int32, (width, width), 0) < self.row
        self.beside = lax.broadcasted_iota(jnp.int32, (width, width), 1) < self.shift

    def cut(self, level):
        width, block, obj = self.width, self.block, self.obj

        def part(k):
            upper = jnp.where(self.beside, obj[block + 1, level, k, :width], obj[block, level, k, :width])
            lower = jnp.where(self.beside, obj[block + 1, level, k, width:], obj[block, level, k, width:])
            return jnp.where(self.below, lower, upper)

        return part(0), part(1)

    def deposit(self, level, terms):
        width, block, acc = self.width, self.block, self.acc
        for k, term in enumerate(terms):
            zero = jnp.zeros_like(term)
            upper = jnp.where(self.below, zero, term)
            lower = jnp.where(self.below, term, zero)
            acc[block, level, k, :width] += jnp.where(self.beside, zero, upper)
            acc[block, level, k, width:] += jnp.where(self.beside, zero, lower)
            acc[block + 1, level, k, :width] += jnp.where(self.beside, upper, zero)
            acc[block + 1, level, k, width:] += jnp.where(self.beside, lower, zero)

    def rolled(self, x):
        return pltpu.roll(pltpu.roll(x, self.row, 0), self.shift, 1)

    def rolled_back(self, x):
        width = self.width
        return pltpu.roll(pltpu.roll(x, (width - self.row) % width, 0), (width - self.shift) % width, 1)


def visit(slots, probe, table, g_probe):
    def transformed(fields, kind):
        for axis in (1, 0):
            fields = [one_side(*field, kind, axis, table) for field in fields]
        return fields

    u0 = [(slot.rolled(probe[0]), slot.rolled(probe[1])) for slot in slots]
    o0 = [slot.cut(0) for slot in slots]
    u1 = transformed([times(*u, *o) for u, o in zip(u0, o0)], PROP)
    o1 = [slot.cut(1) for slot in slots]
    far = transformed([times(*u, *o) for u, o in zip(u1, o1)], FWD)
    factors = [1.0 - slot.amplitude() * lax.rsqrt(re * re + im * im + 1.0) for slot, (re, im) in zip(slots, far)]
    chi = transformed([(re * factor, im * factor) for factor, (re, im) in zip(factors, far)], INV)
    back = [conj_times(*o, *x) for o, x in zip(o1, chi)]
    for slot, u, x in zip(slots, u1, chi):
        slot.deposit(1, conj_times(*u, *x))
    chi = transformed(back, ADJ)
    for slot, u, x in zip(slots, u0, chi):
        slot.deposit(0, conj_times(*u, *x))
    for slot, o, x in zip(slots, o0, chi):
        for part, term in enumerate(conj_times(*o, *x)):
            g_probe[part] += slot.rolled_back(term)


class Place:
    def __init__(self, axes, scalars, tile_rows, tile_cols, rim):
        down, along, self.centers, counts = scalars
        tx, ty = down[0], along[0]
        odd = tx % 2
        self.count = counts[tx * axes[1] + ty]
        self.relayed = (tx == axes[0] // 2) | (tx == axes[0] // 2 - 1)
        self.first = tx * tile_rows, ty * tile_cols
        inner = tile_rows - rim
        self.on_tile, self.off_tile = rows_at((1 - odd) * inner, rim), rows_at(odd * inner, rim)
        outer = tile_rows + rim
        self.on, self.off = rows_at((1 - odd) * outer, rim), rows_at(odd * outer, rim)

    def start(self, slot):
        return self.centers[slot, 0] - self.first[0], self.centers[slot, 1] - self.first[1]


def rows_at(first, count):
    return pl.ds(pl.multiple_of(first, count), count)


def start_all(pairs, sem, at):
    copies = [pltpu.make_async_copy(a, b, sem.at[at + i]) for i, (a, b) in enumerate(pairs)]
    for copy in copies:
        copy.start()
    return copies


def run_all(pairs, sem):
    return start_all(pairs, sem, 0)


def wait_all(copies):
    for copy in copies:
        copy.wait()


class Loads:
    def __init__(self, pairs, sem, at):
        self.pairs, self.sem, self.at = pairs, sem, at

    def copies(self):
        return [pltpu.make_async_copy(a, b, self.sem.at[self.at + i]) for i, (a, b) in enumerate(self.pairs)]

    def start(self):
        for copy in self.copies():
            copy.start()

    def wait(self):
        wait_all(self.copies())


class ChosenLoads(Loads):
    def __init__(self, pairs, flag, other, sem, at):
        super().__init__(pairs, sem, at)
        self.flag, self.other = flag, other

    def start(self):
        copies = self.copies()
        for copy in copies[:-1]:
            copy.start()
        place = self.sem.at[self.at + len(copies) - 1]
        pl.when(self.flag)(lambda: pltpu.make_async_copy(self.other, self.pairs[-1][1], place).start())
        pl.when(jnp.logical_not(self.flag))(lambda: copies[-1].start())


def two_groups(here, firsts, step, loads, stores, amplitudes, amps, amp_sem, order, sem, probe, table, obj, acc, g_probe):
    width = probe.shape[-1]

    def listed(g, count):
        def look(slot, n):
            order[n] = slot
            return n + (here.start(slot)[1] // width == firsts[g]).astype(jnp.int32)

        return lax.fori_loop(0, here.count, look, count)

    first = listed(0, jnp.zeros((), jnp.int32))
    count = listed(1, first)

    def amplitude_copy(slot):
        return pltpu.make_async_copy(amplitudes.at[slot], amps.at[slot], amp_sem.at[slot])

    def fetch(i, _):
        amplitude_copy(order[i]).start()
        return 0

    lax.fori_loop(0, count, fetch, 0)

    def store(g):
        start_all(stores[g], sem, g * len(stores[0]))

    def slot_at(i):
        slot = order[i]

        def amplitude():
            amplitude_copy(slot).wait()
            return amps[slot]

        return Slot(here.start(slot), step * (i >= first).astype(jnp.int32), amplitude, obj, acc)

    def after_first(i):
        pl.when((i < first) & (first <= i + 2))(lambda: store(0))

    def two(p, _):
        i = 2 * p
        pl.when((i + 1 >= first) & (i - 1 < first))(loads[1].wait)
        visit([slot_at(i), slot_at(i + 1)], probe, table, g_probe)
        after_first(i)
        return 0

    def one():
        visit([slot_at(count - 1)], probe, table, g_probe)
        after_first(count - 1)

    loads[0].wait()
    loads[1].start()
    pl.when(first == 0)(lambda: store(0))
    pairs = count // 2
    lax.fori_loop(0, pairs, two, 0)
    pl.when(2 * pairs - 1 < first)(loads[1].wait)
    pl.when(count % 2 == 1)(one)
    store(1)
    for g in (0, 1):
        wait_all([pltpu.make_async_copy(a, b, sem.at[g * len(stores[0]) + i]) for i, (a, b) in enumerate(stores[g])])


def inner_body(
    axes, tx, ty, centers, counts, tile, on, off_quarters, relayed, off_mid, amplitudes, probe_in, table_in,
    g_quarters, g_tile_mid, g_on_mid, g_off_mid, g_probe, obj, acc, probe, table, amps, order, sem, out_sem, amp_sem,
):
    width = probe.shape[-1]
    rim = width // 2
    tile_rows, tile_cols = tile.shape[2], tile.shape[3]
    here = Place(axes, (tx, ty, centers, counts), tile_rows, tile_cols, rim)
    own = slice(rim, rim + tile_rows)
    loads = ([(probe_in, probe), (table_in, table)], [])
    for k in range(3):
        there = slice(rim + k * width, rim + (k + 1) * width)
        loads[k // 2].append((tile.at[:, :, :, there], obj.at[k, :, :, own]))
        loads[k // 2].append((on.at[:, :, :, (k + 1) * width : (k + 2) * width], obj.at[k, :, :, here.on]))
    loads[0].append((off_mid, obj.at[1, :, :, here.off]))
    waits = []
    for k in (0, 1):
        lanes = slice(k * width, (k + 1) * width)
        loads[k].append((off_quarters.at[:, :, :, lanes], obj.at[2 * k, :, :, here.off]))
        waits.append(ChosenLoads(loads[k], here.relayed, relayed.at[:, :, :, lanes], sem, 16 * k))
    waits[0].start()
    acc[...] = jnp.zeros_like(acc)
    g_probe[...] = jnp.zeros_like(g_probe)
    stores = (
        [(acc.at[0], g_quarters.at[0])],
        [
            (acc.at[2], g_quarters.at[1]),
            (acc.at[1, :, :, own], g_tile_mid),
            (acc.at[1, :, :, here.on], g_on_mid),
            (acc.at[1, :, :, here.off], g_off_mid),
        ],
    )
    two_groups(here, (1, 2), 1, waits, stores, amplitudes, amps, amp_sem, order, out_sem, probe, table, obj, acc, g_probe)


def outer_body(
    axes, tx, ty, centers, counts, tile, on, off_quarters, relayed, off_ends, left, right, carried, carried_probe, amplitudes, probe_in, table_in,
    g_tile_ends, g_tile_quarters, g_on_ends, g_on_quarters, g_off_ends, g_off_quarters,
    g_left, g_left_corners, g_right, g_right_corners, g_probe,
    obj, acc, probe, table, amps, order, sem, out_sem, amp_sem,
):
    width = probe.shape[-1]
    rim = width // 2
    tile_rows, tile_cols = tile.shape[2], tile.shape[3]
    here = Place(axes, (tx, ty, centers, counts), tile_rows, tile_cols, rim)
    own = slice(rim, rim + tile_rows)
    one, two = slice(0, rim), slice(rim, width)
    waits, stores = [], []
    for k, (end, quarter, near, far, half, side, g_side, g_corners) in enumerate((
        (0, 1, two, slice(0, rim), one, left, g_left, g_left_corners),
        (3, 2, one, slice(tile_cols - rim, tile_cols), two, right, g_right, g_right_corners),
    )):
        first = rim if k == 0 else tile_cols - rim - width
        there = slice(first, first + width)
        edge = k * tile_cols
        loads = [(probe_in, probe), (table_in, table), (carried_probe, g_probe)] if k == 0 else []
        loads += [
            (tile.at[:, :, :, far], obj.at[end, :, :, own, near]),
            (side, obj.at[end, :, :, own, half]),
            (on.at[:, :, :, edge : edge + width], obj.at[end, :, :, here.on]),
            (off_ends.at[:, :, :, k * width : (k + 1) * width], obj.at[end, :, :, here.off]),
            (tile.at[:, :, :, there], obj.at[quarter, :, :, own]),
            (on.at[:, :, :, first + rim : first + rim + width], obj.at[quarter, :, :, here.on]),
            (carried.at[k], acc.at[quarter]),
        ]
        lanes = slice(k * width, (k + 1) * width)
        loads.append((off_quarters.at[:, :, :, lanes], obj.at[quarter, :, :, here.off]))
        waits.append(ChosenLoads(loads, here.relayed, relayed.at[:, :, :, lanes], sem, 16 * k))
        stores.append([
            (acc.at[end, :, :, own, near], g_tile_ends.at[:, :, :, half]),
            (acc.at[end, :, :, here.on, near], g_on_ends.at[:, :, :, half]),
            (acc.at[end, :, :, here.off, near], g_off_ends.at[:, :, :, half]),
            (acc.at[end, :, :, own, half], g_side),
            (acc.at[end, :, :, here.on, half], g_corners.at[:, :, :rim]),
            (acc.at[end, :, :, here.off, half], g_corners.at[:, :, rim:]),
            (acc.at[quarter, :, :, own], g_tile_quarters.at[:, :, :, lanes]),
            (acc.at[quarter, :, :, here.on], g_on_quarters.at[:, :, :, lanes]),
            (acc.at[quarter, :, :, here.off], g_off_quarters.at[:, :, :, lanes]),
        ])
    waits[0].start()
    for end in (0, 3):
        acc[end] = jnp.zeros_like(acc[end])
    last_block = (tile_cols + 2 * rim) // width - 2
    two_groups(here, (0, last_block), 2, waits, stores, amplitudes, amps, amp_sem, order, out_sem, probe, table, obj, acc, g_probe)


SMEM = pl.BlockSpec(memory_space=pltpu.SMEM)
VMEM = pl.BlockSpec(memory_space=pltpu.VMEM)
HBM = pl.BlockSpec(memory_space=pl.ANY)
ROOM = pltpu.CompilerParams(vmem_limit_bytes=60 * 2**20)


def shape(*dims):
    return jax.ShapeDtypeStruct(dims, F32)


def costs(flops):
    return pl.CostEstimate(flops=flops, bytes_accessed=10**7, transcendentals=0)


def field_call(body, axes, blocks, scalars, arrays, amplitudes, probe, outs, tile_rows):
    width = probe.shape[-1]
    padded = (blocks, 2, 2, tile_rows + width, width)
    table = tables(width)
    return pl.pallas_call(
        functools.partial(body, axes),
        out_shape=tuple(outs) + (jax.ShapeDtypeStruct(probe.shape, F32),),
        in_specs=[SMEM] * len(scalars) + [HBM] * (len(arrays) + 3),
        out_specs=(HBM,) * len(outs) + (VMEM,),
        scratch_shapes=[
            pltpu.VMEM(padded, F32),
            pltpu.VMEM(padded, F32),
            pltpu.VMEM(probe.shape, F32),
            pltpu.VMEM(table.shape, table.dtype),
            pltpu.VMEM(amplitudes.shape, F32),
            pltpu.SMEM((amplitudes.shape[0] + 1,), jnp.int32),
            pltpu.SemaphoreType.DMA((32,)),
            pltpu.SemaphoreType.DMA((18,)),
            pltpu.SemaphoreType.DMA((amplitudes.shape[0],)),
        ],
        compiler_params=ROOM,
        cost_estimate=costs(2 * 10**10),
    )(*scalars, *arrays, amplitudes, probe, table)


def pack_body(tx, tile, left, right, quarters, mid, sem):
    rim = left.shape[-1]
    width = 2 * rim
    tile_rows, tile_cols = tile.shape[2], tile.shape[3]
    rows = rows_at((tx[0] % 2) * (tile_rows - rim), rim)
    quarter = rim + width
    far = tile_cols - quarter
    wait_all(run_all([
        (tile.at[:, :, :, :rim], left),
        (tile.at[:, :, :, tile_cols - rim :], right),
        (tile.at[:, :, rows, rim:quarter], quarters.at[:, :, :, :width]),
        (tile.at[:, :, rows, far : far + width], quarters.at[:, :, :, width:]),
        (tile.at[:, :, rows, quarter:far], mid),
    ], sem))


def strips_body(tx, tile, left, right, on, ends, sem):
    rim = left.shape[-1]
    tile_rows, tile_cols = tile.shape[2], tile.shape[3]
    odd = tx[0] % 2
    inner = tile_rows - rim
    on_rows, off_rows = rows_at((1 - odd) * inner, rim), rows_at(odd * inner, rim)
    wait_all(run_all([
        (left.at[:, :, on_rows], on.at[:, :, :, :rim]),
        (tile.at[:, :, on_rows], on.at[:, :, :, rim : rim + tile_cols]),
        (right.at[:, :, on_rows], on.at[:, :, :, rim + tile_cols :]),
        (left.at[:, :, off_rows], ends.at[:, :, :, :rim]),
        (tile.at[:, :, off_rows, :rim], ends.at[:, :, :, rim : 2 * rim]),
        (tile.at[:, :, off_rows, tile_cols - rim :], ends.at[:, :, :, 2 * rim : 3 * rim]),
        (right.at[:, :, off_rows], ends.at[:, :, :, 3 * rim :]),
    ], sem))


def copies_call(body, scalars, arrays, outs, flops):
    return pl.pallas_call(
        body,
        out_shape=tuple(outs),
        in_specs=[SMEM] * len(scalars) + [HBM] * len(arrays),
        out_specs=(VMEM,) * len(outs),
        scratch_shapes=[pltpu.SemaphoreType.DMA((8,))],
        compiler_params=ROOM,
        cost_estimate=costs(flops),
    )(*scalars, *arrays)


def amplitude_body(axes, tx, ty, counts, patterns, pick, out):
    width = patterns.shape[-1]

    def work():
        hi, lo = split(jnp.sqrt(patterns[0]))
        both = jnp.dot(pick[0], pair(hi, lo, 1), preferred_element_type=F32).astype(jnp.bfloat16)
        out[0] = jnp.dot(both, pick[1:].reshape(-1, width), preferred_element_type=F32)

    pl.when(pl.program_id(0) < counts[tx[0] * axes[1] + ty[0]])(work)


def amplitudes_of(axes, scalars, patterns):
    width = patterns.shape[-1]
    pick = np.zeros((width, width))
    pick[np.arange(width), np.concatenate([np.arange(0, width, 2), np.arange(1, width, 2)])] = 1
    pick = jnp.asarray(np.stack([pick, pick.T, pick.T]).astype(ml_dtypes.bfloat16))
    block = pl.BlockSpec((1, width, width), lambda i: (i, 0, 0))
    return pl.pallas_call(
        functools.partial(amplitude_body, axes),
        grid=(patterns.shape[0],),
        out_shape=jax.ShapeDtypeStruct(patterns.shape, F32),
        in_specs=[SMEM, SMEM, SMEM, block, VMEM],
        out_specs=block,
        compiler_params=ROOM,
        cost_estimate=costs(10**11),
    )(*scalars, patterns, pick)


def merge_body(on_ends, off_ends, left, right, quarters, mid, on, off, sides, sem):
    rim = left.shape[-1]
    width = 2 * rim
    wait_all(run_all([
        (on_ends, on.at[:, :, :, :width]),
        (off_ends, off),
        (left.at[:, :, :rim], sides.at[0, :, :, :, :rim]),
        (right.at[:, :, :rim], sides.at[0, :, :, :, rim:]),
        (left.at[:, :, rim:], sides.at[1, :, :, :, :rim]),
        (right.at[:, :, rim:], sides.at[1, :, :, :, rim:]),
        (quarters, on.at[:, :, :, width : 3 * width]),
        (mid, on.at[:, :, :, 3 * width :]),
    ], sem))
    on[:, :, :, :width] += sides[0]
    off[...] += sides[1]


def merged(on_ends, off_ends, left, right, quarters, mid):
    slices, _, rim, width = on_ends.shape
    cols = width + quarters.shape[3] + mid.shape[3]
    return pl.pallas_call(
        merge_body,
        out_shape=(shape(slices, 2, rim, cols), jax.ShapeDtypeStruct(off_ends.shape, F32)),
        in_specs=[HBM] * 6,
        out_specs=(VMEM, VMEM),
        scratch_shapes=[pltpu.VMEM((2,) + on_ends.shape, F32), pltpu.SemaphoreType.DMA((8,))],
        compiler_params=ROOM,
        cost_estimate=pl.CostEstimate(flops=10**6, bytes_accessed=10**5, transcendentals=0),
    )(on_ends, off_ends, left, right, quarters, mid)


def total_body(tx, ends, quarters, mid, left, right, on, off_quarters, off_ends, off_mid, out):
    rim = left.shape[-1]
    rows, cols = out.shape[2:]
    width = 2 * rim
    one, five = slice(0, rim), slice(cols - rim, cols)
    two, four = slice(rim, rim + width), slice(cols - rim - width, cols - rim)
    three = slice(rim + width, cols - rim - width)
    odd = tx[0] % 2
    out[0, 0, :, one] = ends[0, 0, :, :rim] + left[0, 0]
    out[0, 0, :, five] = ends[0, 0, :, rim:] + right[0, 0]
    out[0, 0, :, two] = quarters[0, 0, :, :width]
    out[0, 0, :, four] = quarters[0, 0, :, width:]
    out[0, 0, :, three] = mid[0, 0]
    here = rows_at((1 - odd) * (rows - rim), rim)
    out[0, 0, here, one] += on[0, 0, :, :rim]
    out[0, 0, here, five] += on[0, 0, :, rim:width]
    out[0, 0, here, two] += on[0, 0, :, width : 2 * width]
    out[0, 0, here, four] += on[0, 0, :, 2 * width : 3 * width]
    out[0, 0, here, three] += on[0, 0, :, 3 * width :]
    here = rows_at(odd * (rows - rim), rim)
    out[0, 0, here, one] += off_ends[0, 0, :, :rim]
    out[0, 0, here, five] += off_ends[0, 0, :, rim:]
    out[0, 0, here, two] += off_quarters[0, 0, :, :width]
    out[0, 0, here, four] += off_quarters[0, 0, :, width:]
    out[0, 0, here, three] += off_mid[0, 0]


def total_of(tx, parts, tile_shape):
    def block(dims):
        return pl.BlockSpec((1, 1) + tuple(dims[2:]), lambda i, j: (i, j, 0, 0))

    return pl.pallas_call(
        total_body,
        grid=tile_shape[:2],
        out_shape=jax.ShapeDtypeStruct(tile_shape, F32),
        in_specs=[SMEM] + [block(x.shape) for x in parts],
        out_specs=block(tile_shape),
        compiler_params=ROOM,
        cost_estimate=costs(10**11),
    )(tx, *parts)


def along(x, step):
    count = lax.axis_size("ty")
    return lax.ppermute(x, "ty", [(i, i + step) for i in range(count) if 0 <= i + step < count])


def across(x, first, skip=None):
    pairs = []
    for i in range(first, lax.axis_size("tx") - 1, 2):
        if i != skip:
            pairs += [(i, i + 1), (i + 1, i)]
    return lax.ppermute(x, "tx", pairs)


def relay_out(x):
    count = lax.axis_size("tx")
    return lax.ppermute(x, "tx", [(count // 2 - 1, count - 1), (count // 2, 0)])


def relay_in(x):
    count = lax.axis_size("tx")
    return lax.ppermute(x, "tx", [(count - 1, count // 2), (0, count // 2 - 1)])


def after(x, *others):
    return lax.optimization_barrier((x,) + others)[0]


def halved(flat, apart):
    bit = (lax.axis_index("tx") // apart) % 2
    half = flat.shape[0] // 2
    pairs = [(i, i ^ apart) for i in range(lax.axis_size("tx"))]
    mine = lax.dynamic_slice_in_dim(flat, bit * half, half, 0)
    other = lax.dynamic_slice_in_dim(flat, (1 - bit) * half, half, 0)
    return mine + lax.ppermute(other, "tx", pairs)


def doubled(flat, apart):
    bit = (lax.axis_index("tx") // apart) % 2
    return joined(flat, lax.ppermute(flat, "tx", [(i, i ^ apart) for i in range(lax.axis_size("tx"))]), bit)


def joined(flat, other, bit):
    return jnp.concatenate([jnp.where(bit == 0, flat, other), jnp.where(bit == 0, other, flat)], axis=0)


def per_device(object_slab, probe, patterns, centers, counts):
    slices, _, tile_rows, tile_cols = object_slab.shape
    width = probe.shape[-1]
    rim = width // 2
    axes = lax.axis_size("tx"), lax.axis_size("ty")
    middle = axes[0] // 2
    tx, ty = (lax.axis_index(axis).astype(jnp.int32).reshape(1) for axis in ("tx", "ty"))
    full = tile_rows + width
    mid_cols = tile_cols - 3 * width
    ends_shape = shape(slices, 2, rim, width)
    quarters_shape = shape(slices, 2, rim, 2 * width)
    mid_shape = shape(slices, 2, rim, mid_cols)
    side_shape = shape(slices, 2, full, rim)
    tile = object_slab

    column_shape = shape(slices, 2, tile_rows, rim)
    to_left, to_right, quarters, mid = copies_call(
        pack_body, (tx,), (tile,), (column_shape, column_shape, quarters_shape, mid_shape), 10**8
    )
    carried = relay_out(quarters)
    left, right = along(to_right, 1), along(to_left, -1)
    off_quarters = across(quarters, 1, middle - 1)
    off_mid = across(mid, 1)
    on_shape = shape(slices, 2, rim, tile_cols + width)
    amplitudes = amplitudes_of(axes, (tx, ty, counts), after(patterns, to_left))

    def strips(tile, left, right):
        on, ends = copies_call(strips_body, (tx,), (tile, left, right), (on_shape, quarters_shape), 10**8)
        return across(on, 0), ends

    def nothing(tile, left, right):
        return jnp.zeros(on_shape.shape, F32), jnp.zeros(quarters_shape.shape, F32)

    relayed = relay_in(carried)
    on, ends = lax.cond(counts[0] >= 0, strips, nothing, after(tile, amplitudes, carried), left, right)
    off_ends = across(ends, 1)

    scalars = (tx, ty, centers, counts)
    g_quarters, g_tile_mid, g_on_mid, g_off_mid, g_probe = field_call(
        inner_body, axes, 3, scalars, (tile, on, off_quarters, relayed, off_mid), amplitudes, probe,
        (shape(2, slices, 2, full, width), shape(slices, 2, tile_rows, mid_cols), mid_shape, mid_shape), tile_rows,
    )
    back_mid = across(g_off_mid, 1)
    (
        g_tile_ends, g_tile_quarters, g_on_ends, g_on_quarters, g_off_ends, g_off_quarters,
        g_left, g_left_corners, g_right, g_right_corners, g_probe,
    ) = field_call(
        outer_body, axes, 4, scalars, (tile, on, off_quarters, relayed, off_ends, left, right, g_quarters, g_probe), amplitudes, probe,
        (
            shape(slices, 2, tile_rows, width), shape(slices, 2, tile_rows, 2 * width), ends_shape, quarters_shape,
            ends_shape, quarters_shape, column_shape, column_shape, column_shape, column_shape,
        ),
        tile_rows,
    )
    g_off_quarters, g_left_corners, g_right_corners, g_probe, _ = lax.optimization_barrier(
        (g_off_quarters, g_left_corners, g_right_corners, g_probe, back_mid)
    )
    corners_left, corners_right = along(g_right_corners, 1), along(g_left_corners, -1)
    back_quarters = across(g_off_quarters, 1)
    apart = [1] + [2**k for k in range(axes[0].bit_length() - 2, 1, -1)]
    shard = g_probe.size // width // 2 ** len(apart)

    def shared(flat):
        for step in apart:
            flat = halved(flat, step)
        for step in (2**k for k in range(axes[1].bit_length() - 1)):
            flat = flat + lax.ppermute(flat, "ty", [(i, i ^ step) for i in range(axes[1])])
        return flat / jnp.sqrt(jnp.maximum(jnp.sum(counts), 1).astype(F32))

    flat = lax.cond(counts[0] >= 0, shared, lambda x: x[:shard], g_probe.reshape(-1, width))
    other = lax.ppermute(flat, "tx", [(i, i ^ 2) for i in range(axes[0])])
    on_all, off_ends = merged(after(g_on_ends, flat, back_quarters), g_off_ends, corners_left, corners_right, g_on_quarters, g_on_mid)
    back_ends = across(off_ends, 1)
    back_on = across(on_all, 0)
    from_left, from_right = along(g_right, 1), along(g_left, -1)
    flat = after(flat + other, on_all)
    for step in reversed(apart[1:]):
        flat = doubled(flat, step)
    flat = after(flat, from_left, from_right)
    last = lax.ppermute(flat, "tx", [(i, i ^ 1) for i in range(axes[0])])
    inner = total_of(
        tx,
        (g_tile_ends, g_tile_quarters, g_tile_mid, from_left, from_right, back_on, back_quarters, back_ends, back_mid),
        tile.shape,
    )
    probe_sum = joined(flat, after(last, inner), lax.axis_index("tx") % 2).reshape(probe.shape)
    return (inner, probe_sum)


def solution(mesh):
    placed = (
        P(None, None, "tx", "ty"),
        P(),
        P(("tx", "ty"), None, None),
        P(("tx", "ty"), None),
        P(),
    )
    return jax.shard_map(
        per_device,
        mesh=mesh,
        in_specs=placed,
        out_specs=(P(None, None, "tx", "ty"), P()),
        check_vma=False,
    )
```

```python
import functools
import math

import jax
import jax.numpy as jnp
import ml_dtypes
import numpy as np
from jax import lax
from jax.experimental import pallas as pl
from jax.experimental.pallas import tpu as pltpu
from jax.sharding import PartitionSpec as P

KAPPA = 40.0
F32 = jnp.float32
FWD, INV, PROP, ADJ = 0, 1, 2, 3
LEFT = {FWD: (0, 2), INV: (1, 3), PROP: (4, 6), ADJ: (5, 7)}
RIGHT = {FWD: (1, 3), INV: (0, 2), PROP: (5, 7), ADJ: (4, 6)}


def tables(width):
    half = width // 2
    n = np.arange(half)
    freq = ((np.arange(width) + half) % width - half) / width
    factor = np.exp(-1j * math.pi * KAPPA * freq * freq)
    turn = 2j * np.pi / width
    scale = 1.0 / math.sqrt(width)
    even = np.exp(-turn * ((2 * n[:, None] * n[None, :]) % width)) * scale
    odd = np.exp(-turn * (((2 * n[:, None] + 1) * n[None, :]) % width)) * scale

    def combined(freqs):
        apart = n[:, None] - n[None, :]
        total = np.zeros((half, half), complex)
        for k in freqs:
            total += factor[k] * np.exp(turn * ((k * apart) % width))
        return total / width

    parts = []
    for c in (even, odd, combined(range(0, width, 2)), combined(range(1, width, 2))):
        real = np.block([[c.real, -c.imag], [c.imag, c.real]])
        for m in (real, real.T):
            hi = m.astype(ml_dtypes.bfloat16)
            lo = (m - hi.astype(np.float64)).astype(ml_dtypes.bfloat16)
            parts.append(np.concatenate([hi, lo], axis=0))
    return jnp.asarray(np.stack(parts))


def split(x):
    hi = x.astype(jnp.bfloat16)
    return hi, (x - hi.astype(F32)).astype(jnp.bfloat16)


def pair(x, y, axis):
    return jnp.concatenate([x, y], axis=axis)


def product(x, both, axis):
    size = both.shape[1]
    hi, lo = split(x)
    if axis == 0:
        first = jnp.dot(both, hi, preferred_element_type=F32)
        return first[:size] + first[size:] + jnp.dot(both[:size], lo, preferred_element_type=F32)
    first = jnp.dot(pair(hi, lo, 0), both[:size], preferred_element_type=F32)
    return first[: x.shape[0]] + first[x.shape[0] :] + jnp.dot(hi, both[size:], preferred_element_type=F32)


def one_side(re, im, kind, axis, table):
    half = re.shape[axis] // 2

    def halves(x):
        return (x[:half], x[half:]) if axis == 0 else (x[:, :half], x[:, half:])

    a, b = halves(re)
    c, d = halves(im)
    if kind != INV:
        a, b, c, d = a + b, a - b, c + d, c - d
    even, odd = (LEFT if axis == 0 else RIGHT)[kind]
    a, c = halves(product(pair(a, c, axis), table[even], axis))
    b, d = halves(product(pair(b, d, axis), table[odd], axis))
    if kind == FWD:
        return pair(a, b, axis), pair(c, d, axis)
    return pair(a + b, a - b, axis), pair(c + d, c - d, axis)


def transform(re, im, kind, table):
    re, im = one_side(re, im, kind, 1, table)
    return one_side(re, im, kind, 0, table)


def times(a, b, c, d):
    return a * c - b * d, a * d + b * c


def conj_times(a, b, c, d):
    return a * c + b * d, a * d - b * c


class Slot:
    def __init__(self, start, block, amplitude, obj, acc):
        width = obj.shape[-1]
        self.width, self.block, self.amplitude, self.obj, self.acc = width, block, amplitude, obj, acc
        self.row, self.shift = start[0], start[1] % width
        self.below = lax.broadcasted_iota(jnp.int32, (width, width), 0) < self.row
        self.beside = lax.broadcasted_iota(jnp.int32, (width, width), 1) < self.shift

    def cut(self, level):
        width, block, obj = self.width, self.block, self.obj

        def part(k):
            upper = jnp.where(self.beside, obj[block + 1, level, k, :width], obj[block, level, k, :width])
            lower = jnp.where(self.beside, obj[block + 1, level, k, width:], obj[block, level, k, width:])
            return jnp.where(self.below, lower, upper)

        return part(0), part(1)

    def deposit(self, level, terms):
        width, block, acc = self.width, self.block, self.acc
        for k, term in enumerate(terms):
            zero = jnp.zeros_like(term)
            upper = jnp.where(self.below, zero, term)
            lower = jnp.where(self.below, term, zero)
            acc[block, level, k, :width] += jnp.where(self.beside, zero, upper)
            acc[block, level, k, width:] += jnp.where(self.beside, zero, lower)
            acc[block + 1, level, k, :width] += jnp.where(self.beside, upper, zero)
            acc[block + 1, level, k, width:] += jnp.where(self.beside, lower, zero)

    def rolled(self, x):
        return pltpu.roll(pltpu.roll(x, self.row, 0), self.shift, 1)

    def rolled_back(self, x):
        width = self.width
        return pltpu.roll(pltpu.roll(x, (width - self.row) % width, 0), (width - self.shift) % width, 1)


def visit(slots, probe, table, g_probe):
    def transformed(fields, kind):
        for axis in (1, 0):
            fields = [one_side(*field, kind, axis, table) for field in fields]
        return fields

    u0 = [(slot.rolled(probe[0]), slot.rolled(probe[1])) for slot in slots]
    o0 = [slot.cut(0) for slot in slots]
    u1 = transformed([times(*u, *o) for u, o in zip(u0, o0)], PROP)
    o1 = [slot.cut(1) for slot in slots]
    far = transformed([times(*u, *o) for u, o in zip(u1, o1)], FWD)
    factors = [1.0 - slot.amplitude() * lax.rsqrt(re * re + im * im + 1.0) for slot, (re, im) in zip(slots, far)]
    chi = transformed([(re * factor, im * factor) for factor, (re, im) in zip(factors, far)], INV)
    back = [conj_times(*o, *x) for o, x in zip(o1, chi)]
    for slot, u, x in zip(slots, u1, chi):
        slot.deposit(1, conj_times(*u, *x))
    chi = transformed(back, ADJ)
    for slot, u, x in zip(slots, u0, chi):
        slot.deposit(0, conj_times(*u, *x))
    for slot, o, x in zip(slots, o0, chi):
        for part, term in enumerate(conj_times(*o, *x)):
            g_probe[part] += slot.rolled_back(term)


class Place:
    def __init__(self, axes, scalars, tile_rows, tile_cols, rim):
        down, along, self.centers, counts = scalars
        tx, ty = down[0], along[0]
        odd = tx % 2
        self.count = counts[tx * axes[1] + ty]
        self.relayed = (tx == axes[0] // 2) | (tx == axes[0] // 2 - 1)
        self.first = tx * tile_rows, ty * tile_cols
        inner = tile_rows - rim
        self.on_tile, self.off_tile = rows_at((1 - odd) * inner, rim), rows_at(odd * inner, rim)
        outer = tile_rows + rim
        self.on, self.off = rows_at((1 - odd) * outer, rim), rows_at(odd * outer, rim)

    def start(self, slot):
        return self.centers[slot, 0] - self.first[0], self.centers[slot, 1] - self.first[1]


def rows_at(first, count):
    return pl.ds(pl.multiple_of(first, count), count)


def start_all(pairs, sem, at):
    copies = [pltpu.make_async_copy(a, b, sem.at[at + i]) for i, (a, b) in enumerate(pairs)]
    for copy in copies:
        copy.start()
    return copies


def run_all(pairs, sem):
    return start_all(pairs, sem, 0)


def wait_all(copies):
    for copy in copies:
        copy.wait()


class Loads:
    def __init__(self, pairs, sem, at):
        self.pairs, self.sem, self.at = pairs, sem, at

    def copies(self):
        return [pltpu.make_async_copy(a, b, self.sem.at[self.at + i]) for i, (a, b) in enumerate(self.pairs)]

    def start(self):
        for copy in self.copies():
            copy.start()

    def wait(self):
        wait_all(self.copies())


class ChosenLoads(Loads):
    def __init__(self, pairs, flag, other, sem, at):
        super().__init__(pairs, sem, at)
        self.flag, self.other = flag, other

    def start(self):
        copies = self.copies()
        for copy in copies[:-1]:
            copy.start()
        place = self.sem.at[self.at + len(copies) - 1]
        pl.when(self.flag)(lambda: pltpu.make_async_copy(self.other, self.pairs[-1][1], place).start())
        pl.when(jnp.logical_not(self.flag))(lambda: copies[-1].start())


def two_groups(here, firsts, step, loads, stores, amplitudes, amps, amp_sem, order, sem, probe, table, obj, acc, g_probe):
    width = probe.shape[-1]

    def listed(g, count):
        def look(slot, n):
            order[n] = slot
            return n + (here.start(slot)[1] // width == firsts[g]).astype(jnp.int32)

        return lax.fori_loop(0, here.count, look, count)

    first = listed(0, jnp.zeros((), jnp.int32))
    count = listed(1, first)

    part = amplitudes[0].shape[0]

    def amplitude_copy(slot, source):
        return pltpu.make_async_copy(source, amps.at[slot], amp_sem.at[slot])

    def fetch(i, _):
        slot = order[i]
        pl.when(slot < part)(lambda: amplitude_copy(slot, amplitudes[0].at[slot]).start())
        pl.when(slot >= part)(lambda: amplitude_copy(slot, amplitudes[1].at[slot - part]).start())
        return 0

    lax.fori_loop(0, count, fetch, 0)

    def store(g):
        start_all(stores[g], sem, g * len(stores[0]))

    def slot_at(i):
        slot = order[i]

        def amplitude():
            amplitude_copy(slot, amplitudes[0].at[0]).wait()
            return amps[slot]

        return Slot(here.start(slot), step * (i >= first).astype(jnp.int32), amplitude, obj, acc)

    def after_first(i):
        pl.when((i < first) & (first <= i + 2))(lambda: store(0))

    def two(p, _):
        i = 2 * p
        pl.when((i + 1 >= first) & (i - 1 < first))(loads[1].wait)
        visit([slot_at(i), slot_at(i + 1)], probe, table, g_probe)
        after_first(i)
        return 0

    def one():
        visit([slot_at(count - 1)], probe, table, g_probe)
        after_first(count - 1)

    loads[0].wait()
    loads[1].start()
    pl.when(first == 0)(lambda: store(0))
    pairs = count // 2
    lax.fori_loop(0, pairs, two, 0)
    pl.when(2 * pairs - 1 < first)(loads[1].wait)
    pl.when(count % 2 == 1)(one)
    store(1)
    for g in (0, 1):
        wait_all([pltpu.make_async_copy(a, b, sem.at[g * len(stores[0]) + i]) for i, (a, b) in enumerate(stores[g])])


def inner_body(
    axes, tx, ty, centers, counts, tile, on, off_quarters, relayed, off_mid, early, late, probe_in, table_in,
    g_quarters, g_tile_mid, g_on_mid, g_off_mid, g_probe, obj, acc, probe, table, amps, order, sem, out_sem, amp_sem,
):
    width = probe.shape[-1]
    rim = width // 2
    tile_rows, tile_cols = tile.shape[2], tile.shape[3]
    here = Place(axes, (tx, ty, centers, counts), tile_rows, tile_cols, rim)
    own = slice(rim, rim + tile_rows)
    loads = ([(probe_in, probe), (table_in, table)], [])
    for k in range(3):
        there = slice(rim + k * width, rim + (k + 1) * width)
        loads[k // 2].append((tile.at[:, :, :, there], obj.at[k, :, :, own]))
        loads[k // 2].append((on.at[:, :, :, (k + 1) * width : (k + 2) * width], obj.at[k, :, :, here.on]))
    loads[0].append((off_mid, obj.at[1, :, :, here.off]))
    waits = []
    for k in (0, 1):
        lanes = slice(k * width, (k + 1) * width)
        loads[k].append((off_quarters.at[:, :, :, lanes], obj.at[2 * k, :, :, here.off]))
        waits.append(ChosenLoads(loads[k], here.relayed, relayed.at[:, :, :, lanes], sem, 16 * k))
    waits[0].start()
    acc[...] = jnp.zeros_like(acc)
    g_probe[...] = jnp.zeros_like(g_probe)
    stores = (
        [(acc.at[0], g_quarters.at[0])],
        [
            (acc.at[2], g_quarters.at[1]),
            (acc.at[1, :, :, own], g_tile_mid),
            (acc.at[1, :, :, here.on], g_on_mid),
            (acc.at[1, :, :, here.off], g_off_mid),
        ],
    )
    two_groups(here, (1, 2), 1, waits, stores, (early, late), amps, amp_sem, order, out_sem, probe, table, obj, acc, g_probe)


def outer_body(
    axes, tx, ty, centers, counts, tile, on, off_quarters, relayed, off_ends, left, right, carried, carried_probe, early, late, probe_in, table_in,
    g_tile_ends, g_tile_quarters, g_on_ends, g_on_quarters, g_off_ends, g_off_quarters,
    g_left, g_right, g_probe,
    obj, acc, probe, table, amps, order, sem, out_sem, amp_sem,
):
    width = probe.shape[-1]
    rim = width // 2
    tile_rows, tile_cols = tile.shape[2], tile.shape[3]
    here = Place(axes, (tx, ty, centers, counts), tile_rows, tile_cols, rim)
    own = slice(rim, rim + tile_rows)
    one, two = slice(0, rim), slice(rim, width)
    waits, stores = [], []
    for k, (end, quarter, near, far, half, side, g_side) in enumerate((
        (0, 1, two, slice(0, rim), one, left, g_left),
        (3, 2, one, slice(tile_cols - rim, tile_cols), two, right, g_right),
    )):
        first = rim if k == 0 else tile_cols - rim - width
        there = slice(first, first + width)
        edge = k * tile_cols
        loads = [(probe_in, probe), (table_in, table), (carried_probe, g_probe)] if k == 0 else []
        loads += [
            (tile.at[:, :, :, far], obj.at[end, :, :, own, near]),
            (side, obj.at[end, :, :, own, half]),
            (on.at[:, :, :, edge : edge + width], obj.at[end, :, :, here.on]),
            (off_ends.at[:, :, :, k * width : (k + 1) * width], obj.at[end, :, :, here.off]),
            (tile.at[:, :, :, there], obj.at[quarter, :, :, own]),
            (on.at[:, :, :, first + rim : first + rim + width], obj.at[quarter, :, :, here.on]),
            (carried.at[k], acc.at[quarter]),
        ]
        lanes = slice(k * width, (k + 1) * width)
        loads.append((off_quarters.at[:, :, :, lanes], obj.at[quarter, :, :, here.off]))
        waits.append(ChosenLoads(loads, here.relayed, relayed.at[:, :, :, lanes], sem, 16 * k))
        stores.append([
            (acc.at[end, :, :, own, near], g_tile_ends.at[:, :, :, half]),
            (acc.at[end, :, :, here.on, near], g_on_ends.at[:, :, :, half]),
            (acc.at[end, :, :, here.off, near], g_off_ends.at[:, :, :, half]),
            (acc.at[end, :, :, own, half], g_side.at[:, :, :tile_rows]),
            (acc.at[end, :, :, here.on, half], g_side.at[:, :, tile_rows : tile_rows + rim]),
            (acc.at[end, :, :, here.off, half], g_side.at[:, :, tile_rows + rim :]),
            (acc.at[quarter, :, :, own], g_tile_quarters.at[:, :, :, lanes]),
            (acc.at[quarter, :, :, here.on], g_on_quarters.at[:, :, :, lanes]),
            (acc.at[quarter, :, :, here.off], g_off_quarters.at[:, :, :, lanes]),
        ])
    waits[0].start()
    for end in (0, 3):
        acc[end] = jnp.zeros_like(acc[end])
    last_block = (tile_cols + 2 * rim) // width - 2
    two_groups(here, (0, last_block), 2, waits, stores, (early, late), amps, amp_sem, order, out_sem, probe, table, obj, acc, g_probe)


SMEM = pl.BlockSpec(memory_space=pltpu.SMEM)
VMEM = pl.BlockSpec(memory_space=pltpu.VMEM)
HBM = pl.BlockSpec(memory_space=pltpu.HBM)
ROOM = pltpu.CompilerParams(vmem_limit_bytes=63 * 2**20)


def shape(*dims):
    return jax.ShapeDtypeStruct(dims, F32)


def costs(flops):
    return pl.CostEstimate(flops=flops, bytes_accessed=10**7, transcendentals=0)


def field_call(body, axes, blocks, scalars, arrays, amplitudes, probe, outs, tile_rows):
    width = probe.shape[-1]
    padded = (blocks, 2, 2, tile_rows + width, width)
    table = tables(width)
    slots = sum(part.shape[0] for part in amplitudes)
    return pl.pallas_call(
        functools.partial(body, axes),
        out_shape=tuple(outs) + (jax.ShapeDtypeStruct(probe.shape, F32),),
        in_specs=[SMEM] * len(scalars) + [HBM] * (len(arrays) + 4),
        out_specs=(HBM,) * len(outs) + (VMEM,),
        scratch_shapes=[
            pltpu.VMEM(padded, F32),
            pltpu.VMEM(padded, F32),
            pltpu.VMEM(probe.shape, F32),
            pltpu.VMEM(table.shape, table.dtype),
            pltpu.VMEM((slots, width, width), F32),
            pltpu.SMEM((slots + 1,), jnp.int32),
            pltpu.SemaphoreType.DMA((32,)),
            pltpu.SemaphoreType.DMA((18,)),
            pltpu.SemaphoreType.DMA((slots,)),
        ],
        compiler_params=ROOM,
        cost_estimate=costs(2 * 10**10),
    )(*scalars, *arrays, *amplitudes, probe, table)


def pack_body(tx, tile, left, right, quarters, mid, sem):
    rim = left.shape[-1]
    width = 2 * rim
    tile_rows, tile_cols = tile.shape[2], tile.shape[3]
    rows = rows_at((tx[0] % 2) * (tile_rows - rim), rim)
    quarter = rim + width
    far = tile_cols - quarter
    wait_all(run_all([
        (tile.at[:, :, :, :rim], left),
        (tile.at[:, :, :, tile_cols - rim :], right),
        (tile.at[:, :, rows, rim:quarter], quarters.at[:, :, :, :width]),
        (tile.at[:, :, rows, far : far + width], quarters.at[:, :, :, width:]),
        (tile.at[:, :, rows, quarter:far], mid),
    ], sem))


def strips_body(tx, tile, left, right, on, ends, sem):
    rim = left.shape[-1]
    tile_rows, tile_cols = tile.shape[2], tile.shape[3]
    odd = tx[0] % 2
    inner = tile_rows - rim
    on_rows, off_rows = rows_at((1 - odd) * inner, rim), rows_at(odd * inner, rim)
    wait_all(run_all([
        (left.at[:, :, on_rows], on.at[:, :, :, :rim]),
        (tile.at[:, :, on_rows], on.at[:, :, :, rim : rim + tile_cols]),
        (right.at[:, :, on_rows], on.at[:, :, :, rim + tile_cols :]),
        (left.at[:, :, off_rows], ends.at[:, :, :, :rim]),
        (tile.at[:, :, off_rows, :rim], ends.at[:, :, :, rim : 2 * rim]),
        (tile.at[:, :, off_rows, tile_cols - rim :], ends.at[:, :, :, 2 * rim : 3 * rim]),
        (right.at[:, :, off_rows], ends.at[:, :, :, 3 * rim :]),
    ], sem))


def copies_call(body, scalars, arrays, outs, flops):
    return pl.pallas_call(
        body,
        out_shape=tuple(outs),
        in_specs=[SMEM] * len(scalars) + [HBM] * len(arrays),
        out_specs=(VMEM,) * len(outs),
        scratch_shapes=[pltpu.SemaphoreType.DMA((8,))],
        compiler_params=ROOM,
        cost_estimate=costs(flops),
    )(*scalars, *arrays)


def amplitude_body(axes, first, tx, ty, counts, patterns, pick, out):
    width = patterns.shape[-1]

    def work():
        hi, lo = split(jnp.sqrt(patterns[0]))
        both = jnp.dot(pick[0], pair(hi, lo, 1), preferred_element_type=F32).astype(jnp.bfloat16)
        out[0] = jnp.dot(both, pick[1:].reshape(-1, width), preferred_element_type=F32)

    pl.when(first + pl.program_id(0) < counts[tx[0] * axes[1] + ty[0]])(work)


def amplitudes_of(axes, scalars, patterns, first, count):
    width = patterns.shape[-1]
    pick = np.zeros((width, width))
    pick[np.arange(width), np.concatenate([np.arange(0, width, 2), np.arange(1, width, 2)])] = 1
    pick = jnp.asarray(np.stack([pick, pick.T, pick.T]).astype(ml_dtypes.bfloat16))
    block = pl.BlockSpec((1, width, width), lambda i: (first + i, 0, 0))
    return pl.pallas_call(
        functools.partial(amplitude_body, axes, first),
        grid=(count,),
        out_shape=shape(count, width, width),
        in_specs=[SMEM, SMEM, SMEM, block, VMEM],
        out_specs=pl.BlockSpec((1, width, width), lambda i: (i, 0, 0)),
        compiler_params=ROOM,
        cost_estimate=costs(10**11),
    )(*scalars, patterns, pick)


def merge_body(on_ends, off_ends, left, right, quarters, mid, on, off, sides, sem):
    rim = left.shape[-1]
    width = 2 * rim
    tile_rows = left.shape[2] - width
    on_rows, off_rows = slice(tile_rows, tile_rows + rim), slice(tile_rows + rim, tile_rows + width)
    wait_all(run_all([
        (on_ends, on.at[:, :, :, :width]),
        (off_ends, off),
        (left.at[:, :, on_rows], sides.at[0, :, :, :, :rim]),
        (right.at[:, :, on_rows], sides.at[0, :, :, :, rim:]),
        (left.at[:, :, off_rows], sides.at[1, :, :, :, :rim]),
        (right.at[:, :, off_rows], sides.at[1, :, :, :, rim:]),
        (quarters, on.at[:, :, :, width : 3 * width]),
        (mid, on.at[:, :, :, 3 * width :]),
    ], sem))
    on[:, :, :, :width] += sides[0]
    off[...] += sides[1]


def merged(on_ends, off_ends, left, right, quarters, mid):
    slices, _, rim, width = on_ends.shape
    cols = width + quarters.shape[3] + mid.shape[3]
    return pl.pallas_call(
        merge_body,
        out_shape=(shape(slices, 2, rim, cols), jax.ShapeDtypeStruct(off_ends.shape, F32)),
        in_specs=[HBM] * 6,
        out_specs=(VMEM, VMEM),
        scratch_shapes=[pltpu.VMEM((2,) + on_ends.shape, F32), pltpu.SemaphoreType.DMA((8,))],
        compiler_params=ROOM,
        cost_estimate=pl.CostEstimate(flops=10**6, bytes_accessed=10**5, transcendentals=0),
    )(on_ends, off_ends, left, right, quarters, mid)


def inner_total_body(tx, quarters, mid, on, off_quarters, off_mid, out, total, on_part, off_part, sem):
    rim = on.shape[2]
    width = 2 * rim
    rows = quarters.shape[2]
    cols = out.shape[3]
    last = cols - 2 * width
    middle = slice(width, last)
    odd = tx[0] % 2
    wait_all(run_all([
        (quarters.at[:, :, :, :width], total.at[:, :, :, :width]),
        (mid, total.at[:, :, :, middle]),
        (quarters.at[:, :, :, width:], total.at[:, :, :, last:]),
        (on.at[:, :, :, width : 2 * width], on_part.at[:, :, :, :width]),
        (on.at[:, :, :, 3 * width :], on_part.at[:, :, :, middle]),
        (on.at[:, :, :, 2 * width : 3 * width], on_part.at[:, :, :, last:]),
        (off_quarters.at[:, :, :, :width], off_part.at[:, :, :, :width]),
        (off_mid, off_part.at[:, :, :, middle]),
        (off_quarters.at[:, :, :, width:], off_part.at[:, :, :, last:]),
    ], sem))
    total[:, :, rows_at((1 - odd) * (rows - rim), rim)] += on_part[...]
    total[:, :, rows_at(odd * (rows - rim), rim)] += off_part[...]
    wait_all(run_all([(total, out.at[:, :, :, rim : cols - rim])], sem))


def inner_total(tx, parts, tile_shape):
    rim, width = parts[2].shape[2], 2 * parts[2].shape[2]
    cols = tile_shape[3] - width
    return pl.pallas_call(
        inner_total_body,
        out_shape=jax.ShapeDtypeStruct(tile_shape, F32),
        in_specs=[SMEM] + [HBM] * len(parts),
        out_specs=HBM,
        scratch_shapes=[pltpu.VMEM(tile_shape[:3] + (cols,), F32)]
        + [pltpu.VMEM(tile_shape[:2] + (rim, cols), F32)] * 2
        + [pltpu.SemaphoreType.DMA((9,))],
        compiler_params=ROOM,
        cost_estimate=costs(10**8),
    )(tx, *parts)


def end_total_body(tx, ends, left, right, on, off, inner, out, total, sides, on_part, off_part, sem):
    del inner
    rim = on.shape[2]
    rows, cols = out.shape[2:]
    odd = tx[0] % 2
    wait_all(run_all([
        (ends, total),
        (left.at[:, :, :rows], sides.at[:, :, :, :rim]),
        (right.at[:, :, :rows], sides.at[:, :, :, rim:]),
        (on.at[:, :, :, : 2 * rim], on_part),
        (off, off_part),
    ], sem))
    total[...] += sides[...]
    total[:, :, rows_at((1 - odd) * (rows - rim), rim)] += on_part[...]
    total[:, :, rows_at(odd * (rows - rim), rim)] += off_part[...]
    wait_all(run_all([
        (total.at[:, :, :, :rim], out.at[:, :, :, :rim]),
        (total.at[:, :, :, rim:], out.at[:, :, :, cols - rim :]),
    ], sem))


def end_total(tx, parts, inner):
    ends, off = parts[0], parts[-1]
    return pl.pallas_call(
        end_total_body,
        out_shape=jax.ShapeDtypeStruct(inner.shape, F32),
        in_specs=[SMEM] + [HBM] * (len(parts) + 1),
        out_specs=HBM,
        scratch_shapes=[pltpu.VMEM(ends.shape, F32)] * 2 + [pltpu.VMEM(off.shape, F32)] * 2 + [pltpu.SemaphoreType.DMA((5,))],
        input_output_aliases={len(parts) + 1: 0},
        compiler_params=ROOM,
        cost_estimate=costs(10**11),
    )(tx, *parts, inner)


def along(x, step):
    count = lax.axis_size("ty")
    return lax.ppermute(x, "ty", [(i, i + step) for i in range(count) if 0 <= i + step < count])


def across(x, first, skip=None):
    pairs = []
    for i in range(first, lax.axis_size("tx") - 1, 2):
        if i != skip:
            pairs += [(i, i + 1), (i + 1, i)]
    return lax.ppermute(x, "tx", pairs)


def relay_out(x):
    count = lax.axis_size("tx")
    return lax.ppermute(x, "tx", [(count // 2 - 1, count - 1), (count // 2, 0)])


def relay_in(x):
    count = lax.axis_size("tx")
    return lax.ppermute(x, "tx", [(count - 1, count // 2), (0, count // 2 - 1)])


def after(x, *others):
    return lax.optimization_barrier((x,) + others)[0]


def halved(flat, apart):
    bit = (lax.axis_index("tx") // apart) % 2
    half = flat.shape[0] // 2
    pairs = [(i, i ^ apart) for i in range(lax.axis_size("tx"))]
    mine = lax.dynamic_slice_in_dim(flat, bit * half, half, 0)
    other = lax.dynamic_slice_in_dim(flat, (1 - bit) * half, half, 0)
    return mine + lax.ppermute(other, "tx", pairs)


def doubled(flat, apart, meanwhile):
    bit = (lax.axis_index("tx") // apart) % 2
    other = lax.ppermute(flat, "tx", [(i, i ^ apart) for i in range(lax.axis_size("tx"))])
    return joined(flat, after(other, meanwhile), bit)


def joined(flat, other, bit):
    return jnp.concatenate([jnp.where(bit == 0, flat, other), jnp.where(bit == 0, other, flat)], axis=0)


def per_device(object_slab, probe, patterns, centers, counts):
    slices, _, tile_rows, tile_cols = object_slab.shape
    width = probe.shape[-1]
    rim = width // 2
    axes = lax.axis_size("tx"), lax.axis_size("ty")
    middle = axes[0] // 2
    tx, ty = (lax.axis_index(axis).astype(jnp.int32).reshape(1) for axis in ("tx", "ty"))
    full = tile_rows + width
    mid_cols = tile_cols - 3 * width
    ends_shape = shape(slices, 2, rim, width)
    quarters_shape = shape(slices, 2, rim, 2 * width)
    mid_shape = shape(slices, 2, rim, mid_cols)
    side_shape = shape(slices, 2, full, rim)
    tile = object_slab

    column_shape = shape(slices, 2, tile_rows, rim)
    to_left, to_right, quarters, mid = copies_call(
        pack_body, (tx,), (tile,), (column_shape, column_shape, quarters_shape, mid_shape), 10**8
    )
    carried = relay_out(quarters)
    left, right = along(to_right, 1), along(to_left, -1)
    off_quarters = across(quarters, 1, middle - 1)
    off_mid = across(mid, 1)
    on_shape = shape(slices, 2, rim, tile_cols + width)
    part = patterns.shape[0] // 2
    early = amplitudes_of(axes, (tx, ty, counts), after(patterns, to_left), 0, part)

    def strips(patterns, tile, left, right):
        on, ends = copies_call(strips_body, (tx,), (tile, left, right), (on_shape, quarters_shape), 10**8)
        late = amplitudes_of(axes, (tx, ty, counts), after(patterns, on), part, part)
        return across(on, 0), ends, late

    def nothing(patterns, tile, left, right):
        return jnp.zeros(on_shape.shape, F32), jnp.zeros(quarters_shape.shape, F32), patterns[part:]

    relayed = relay_in(carried)
    on, ends, late = lax.cond(counts[0] >= 0, strips, nothing, patterns, after(tile, early, carried), left, right)
    amplitudes = (early, late)
    off_ends = across(ends, 1)

    scalars = (tx, ty, centers, counts)
    g_quarters, g_tile_mid, g_on_mid, g_off_mid, g_probe = field_call(
        inner_body, axes, 3, scalars, (tile, on, off_quarters, relayed, off_mid), amplitudes, probe,
        (shape(2, slices, 2, full, width), shape(slices, 2, tile_rows, mid_cols), mid_shape, mid_shape), tile_rows,
    )
    back_mid = across(g_off_mid, 1)
    g_tile_ends, g_tile_quarters, g_on_ends, g_on_quarters, g_off_ends, g_off_quarters, g_left, g_right, g_probe = field_call(
        outer_body, axes, 4, scalars, (tile, on, off_quarters, relayed, off_ends, left, right, g_quarters, g_probe), amplitudes, probe,
        (
            shape(slices, 2, tile_rows, width), shape(slices, 2, tile_rows, 2 * width), ends_shape, quarters_shape,
            ends_shape, quarters_shape, side_shape, side_shape,
        ),
        tile_rows,
    )
    g_off_quarters, g_left, g_right, g_probe, _ = lax.optimization_barrier((g_off_quarters, g_left, g_right, g_probe, back_mid))
    from_left, from_right = along(g_right, 1), along(g_left, -1)
    back_quarters = across(g_off_quarters, 1)
    apart = [1] + [2**k for k in range(axes[0].bit_length() - 2, 1, -1)]
    shard = g_probe.size // width // 2 ** len(apart)
    some = counts[0] >= 0

    def shared(flat):
        for step in apart:
            flat = halved(flat, step)
        for step in (2**k for k in range(axes[1].bit_length() - 1)):
            flat = flat + lax.ppermute(flat, "ty", [(i, i ^ step) for i in range(axes[1])])
        return flat / jnp.sqrt(jnp.maximum(jnp.sum(counts), 1).astype(F32))

    flat = lax.cond(counts[0] >= 0, shared, lambda x: x[:shard], g_probe.reshape(-1, width))
    other = lax.ppermute(flat, "tx", [(i, i ^ 2) for i in range(axes[0])])
    on_all, off_ends = merged(after(g_on_ends, flat, back_quarters), g_off_ends, from_left, from_right, g_on_quarters, g_on_mid)
    back_ends = across(off_ends, 1)
    back_on = across(on_all, 0)
    inner = inner_total(tx, (g_tile_quarters, g_tile_mid, back_on, back_quarters, back_mid), tile.shape)
    flat = after(flat + other, on_all)
    for step in reversed(apart[1:]):
        flat = doubled(flat, step, inner)
    last = lax.ppermute(flat, "tx", [(i, i ^ 1) for i in range(axes[0])])
    inner = end_total(tx, (g_tile_ends, from_left, from_right, back_on, back_ends), inner)
    probe_sum = joined(flat, after(last, inner), lax.axis_index("tx") % 2).reshape(probe.shape)
    return (inner, probe_sum)


def solution(mesh):
    placed = (
        P(None, None, "tx", "ty"),
        P(),
        P(("tx", "ty"), None, None),
        P(("tx", "ty"), None),
        P(),
    )
    return jax.shard_map(
        per_device,
        mesh=mesh,
        in_specs=placed,
        out_specs=(P(None, None, "tx", "ty"), P()),
        check_vma=False,
    )
```

```python
import functools
import math

import jax
import jax.numpy as jnp
import ml_dtypes
import numpy as np
from jax import lax
from jax.experimental import pallas as pl
from jax.experimental.pallas import tpu as pltpu
from jax.sharding import PartitionSpec as P

KAPPA = 40.0
F32 = jnp.float32
FWD, INV, PROP, ADJ = 0, 1, 2, 3
LEFT = {FWD: (0, 2), INV: (1, 3), PROP: (4, 6), ADJ: (5, 7)}
RIGHT = {FWD: (1, 3), INV: (0, 2), PROP: (5, 7), ADJ: (4, 6)}


def tables(width):
    half = width // 2
    n = np.arange(half)
    freq = ((np.arange(width) + half) % width - half) / width
    factor = np.exp(-1j * math.pi * KAPPA * freq * freq)
    turn = 2j * np.pi / width
    scale = 1.0 / math.sqrt(width)
    even = np.exp(-turn * ((2 * n[:, None] * n[None, :]) % width)) * scale
    odd = np.exp(-turn * (((2 * n[:, None] + 1) * n[None, :]) % width)) * scale

    def combined(freqs):
        apart = n[:, None] - n[None, :]
        total = np.zeros((half, half), complex)
        for k in freqs:
            total += factor[k] * np.exp(turn * ((k * apart) % width))
        return total / width

    parts = []
    for c in (even, odd, combined(range(0, width, 2)), combined(range(1, width, 2))):
        real = np.block([[c.real, -c.imag], [c.imag, c.real]])
        for m in (real, real.T):
            hi = m.astype(ml_dtypes.bfloat16)
            lo = (m - hi.astype(np.float64)).astype(ml_dtypes.bfloat16)
            parts.append(np.concatenate([hi, lo], axis=0))
    return jnp.asarray(np.stack(parts))


def split(x):
    hi = x.astype(jnp.bfloat16)
    return hi, (x - hi.astype(F32)).astype(jnp.bfloat16)


def pair(x, y, axis):
    return jnp.concatenate([x, y], axis=axis)


def product(x, both, axis):
    size = both.shape[1]
    hi, lo = split(x)
    if axis == 0:
        first = jnp.dot(both, hi, preferred_element_type=F32)
        return first[:size] + first[size:] + jnp.dot(both[:size], lo, preferred_element_type=F32)
    first = jnp.dot(pair(hi, lo, 0), both[:size], preferred_element_type=F32)
    return first[: x.shape[0]] + first[x.shape[0] :] + jnp.dot(hi, both[size:], preferred_element_type=F32)


def one_side(re, im, kind, axis, table):
    half = re.shape[axis] // 2

    def halves(x):
        return (x[:half], x[half:]) if axis == 0 else (x[:, :half], x[:, half:])

    a, b = halves(re)
    c, d = halves(im)
    if kind != INV:
        a, b, c, d = a + b, a - b, c + d, c - d
    even, odd = (LEFT if axis == 0 else RIGHT)[kind]
    a, c = halves(product(pair(a, c, axis), table[even], axis))
    b, d = halves(product(pair(b, d, axis), table[odd], axis))
    if kind == FWD:
        return pair(a, b, axis), pair(c, d, axis)
    return pair(a + b, a - b, axis), pair(c + d, c - d, axis)


def transform(re, im, kind, table):
    re, im = one_side(re, im, kind, 1, table)
    return one_side(re, im, kind, 0, table)


def times(a, b, c, d):
    return a * c - b * d, a * d + b * c


def conj_times(a, b, c, d):
    return a * c + b * d, a * d - b * c


class Slot:
    def __init__(self, start, block, amplitude, obj, acc):
        width = obj.shape[-1]
        self.width, self.block, self.amplitude, self.obj, self.acc = width, block, amplitude, obj, acc
        self.row, self.shift = start[0], start[1] % width
        self.below = lax.broadcasted_iota(jnp.int32, (width, width), 0) < self.row
        self.beside = lax.broadcasted_iota(jnp.int32, (width, width), 1) < self.shift

    def cut(self, level):
        width, block, obj = self.width, self.block, self.obj

        def part(k):
            upper = jnp.where(self.beside, obj[block + 1, level, k, :width], obj[block, level, k, :width])
            lower = jnp.where(self.beside, obj[block + 1, level, k, width:], obj[block, level, k, width:])
            return jnp.where(self.below, lower, upper)

        return part(0), part(1)

    def deposit(self, level, terms):
        width, block, acc = self.width, self.block, self.acc
        for k, term in enumerate(terms):
            zero = jnp.zeros_like(term)
            upper = jnp.where(self.below, zero, term)
            lower = jnp.where(self.below, term, zero)
            acc[block, level, k, :width] += jnp.where(self.beside, zero, upper)
            acc[block, level, k, width:] += jnp.where(self.beside, zero, lower)
            acc[block + 1, level, k, :width] += jnp.where(self.beside, upper, zero)
            acc[block + 1, level, k, width:] += jnp.where(self.beside, lower, zero)

    def rolled(self, x):
        return pltpu.roll(pltpu.roll(x, self.row, 0), self.shift, 1)

    def rolled_back(self, x):
        width = self.width
        return pltpu.roll(pltpu.roll(x, (width - self.row) % width, 0), (width - self.shift) % width, 1)


def visit(slots, probe, table, g_probe):
    def transformed(fields, kind):
        for axis in (1, 0):
            fields = [one_side(*field, kind, axis, table) for field in fields]
        return fields

    u0 = [(slot.rolled(probe[0]), slot.rolled(probe[1])) for slot in slots]
    o0 = [slot.cut(0) for slot in slots]
    u1 = transformed([times(*u, *o) for u, o in zip(u0, o0)], PROP)
    o1 = [slot.cut(1) for slot in slots]
    far = transformed([times(*u, *o) for u, o in zip(u1, o1)], FWD)
    factors = [1.0 - slot.amplitude() * lax.rsqrt(re * re + im * im + 1.0) for slot, (re, im) in zip(slots, far)]
    chi = transformed([(re * factor, im * factor) for factor, (re, im) in zip(factors, far)], INV)
    back = [conj_times(*o, *x) for o, x in zip(o1, chi)]
    for slot, u, x in zip(slots, u1, chi):
        slot.deposit(1, conj_times(*u, *x))
    chi = transformed(back, ADJ)
    for slot, u, x in zip(slots, u0, chi):
        slot.deposit(0, conj_times(*u, *x))
    for slot, o, x in zip(slots, o0, chi):
        for part, term in enumerate(conj_times(*o, *x)):
            g_probe[part] += slot.rolled_back(term)


class Place:
    def __init__(self, axes, scalars, tile_rows, tile_cols, rim):
        down, along, self.centers, counts = scalars
        tx, ty = down[0], along[0]
        odd = tx % 2
        self.count = counts[tx * axes[1] + ty]
        self.relayed = (tx == axes[0] // 2) | (tx == axes[0] // 2 - 1)
        self.first = tx * tile_rows, ty * tile_cols
        inner = tile_rows - rim
        self.on_tile, self.off_tile = rows_at((1 - odd) * inner, rim), rows_at(odd * inner, rim)
        outer = tile_rows + rim
        self.on, self.off = rows_at((1 - odd) * outer, rim), rows_at(odd * outer, rim)

    def start(self, slot):
        return self.centers[slot, 0] - self.first[0], self.centers[slot, 1] - self.first[1]


def rows_at(first, count):
    return pl.ds(pl.multiple_of(first, count), count)


def start_all(pairs, sem, at):
    copies = [pltpu.make_async_copy(a, b, sem.at[at + i]) for i, (a, b) in enumerate(pairs)]
    for copy in copies:
        copy.start()
    return copies


def run_all(pairs, sem):
    return start_all(pairs, sem, 0)


def wait_all(copies):
    for copy in copies:
        copy.wait()


class Loads:
    def __init__(self, pairs, sem, at):
        self.pairs, self.sem, self.at = pairs, sem, at

    def copies(self):
        return [pltpu.make_async_copy(a, b, self.sem.at[self.at + i]) for i, (a, b) in enumerate(self.pairs)]

    def start(self):
        for copy in self.copies():
            copy.start()

    def wait(self):
        wait_all(self.copies())


class ChosenLoads(Loads):
    def __init__(self, pairs, flag, other, sem, at):
        super().__init__(pairs, sem, at)
        self.flag, self.other = flag, other

    def start(self):
        copies = self.copies()
        for copy in copies[:-1]:
            copy.start()
        place = self.sem.at[self.at + len(copies) - 1]
        pl.when(self.flag)(lambda: pltpu.make_async_copy(self.other, self.pairs[-1][1], place).start())
        pl.when(jnp.logical_not(self.flag))(lambda: copies[-1].start())


def two_groups(here, firsts, step, loads, stores, amplitudes, amps, amp_sem, order, sem, probe, table, obj, acc, g_probe):
    width = probe.shape[-1]

    def listed(g, count):
        def look(slot, n):
            order[n] = slot
            return n + (here.start(slot)[1] // width == firsts[g]).astype(jnp.int32)

        return lax.fori_loop(0, here.count, look, count)

    first = listed(0, jnp.zeros((), jnp.int32))
    count = listed(1, first)

    part = amplitudes[0].shape[0]

    def amplitude_copy(slot, source):
        return pltpu.make_async_copy(source, amps.at[slot], amp_sem.at[slot])

    def fetch(i, _):
        slot = order[i]
        pl.when(slot < part)(lambda: amplitude_copy(slot, amplitudes[0].at[slot]).start())
        pl.when(slot >= part)(lambda: amplitude_copy(slot, amplitudes[1].at[slot - part]).start())
        return 0

    lax.fori_loop(0, count, fetch, 0)

    def store(g):
        start_all(stores[g], sem, g * len(stores[0]))

    def slot_at(i):
        slot = order[i]

        def amplitude():
            amplitude_copy(slot, amplitudes[0].at[0]).wait()
            return amps[slot]

        return Slot(here.start(slot), step * (i >= first).astype(jnp.int32), amplitude, obj, acc)

    def after_first(i):
        pl.when((i < first) & (first <= i + 2))(lambda: store(0))

    def two(p, _):
        i = 2 * p
        pl.when((i + 1 >= first) & (i - 1 < first))(loads[1].wait)
        visit([slot_at(i), slot_at(i + 1)], probe, table, g_probe)
        after_first(i)
        return 0

    def one():
        visit([slot_at(count - 1)], probe, table, g_probe)
        after_first(count - 1)

    loads[0].wait()
    loads[1].start()
    pl.when(first == 0)(lambda: store(0))
    pairs = count // 2
    lax.fori_loop(0, pairs, two, 0)
    pl.when(2 * pairs - 1 < first)(loads[1].wait)
    pl.when(count % 2 == 1)(one)
    store(1)
    for g in (0, 1):
        wait_all([pltpu.make_async_copy(a, b, sem.at[g * len(stores[0]) + i]) for i, (a, b) in enumerate(stores[g])])


def inner_body(
    axes, tx, ty, centers, counts, tile, on, off_quarters, relayed, off_mid, early, late, probe_in, table_in,
    g_quarters, g_tile_mid, g_on_mid, g_off_mid, g_probe, obj, acc, probe, table, amps, order, sem, out_sem, amp_sem,
):
    width = probe.shape[-1]
    rim = width // 2
    tile_rows, tile_cols = tile.shape[2], tile.shape[3]
    here = Place(axes, (tx, ty, centers, counts), tile_rows, tile_cols, rim)
    own = slice(rim, rim + tile_rows)
    loads = ([(probe_in, probe), (table_in, table)], [])
    for k in range(3):
        there = slice(rim + k * width, rim + (k + 1) * width)
        loads[k // 2].append((tile.at[:, :, :, there], obj.at[k, :, :, own]))
        loads[k // 2].append((on.at[:, :, :, (k + 1) * width : (k + 2) * width], obj.at[k, :, :, here.on]))
    loads[0].append((off_mid, obj.at[1, :, :, here.off]))
    waits = []
    for k in (0, 1):
        lanes = slice(k * width, (k + 1) * width)
        loads[k].append((off_quarters.at[:, :, :, lanes], obj.at[2 * k, :, :, here.off]))
        waits.append(ChosenLoads(loads[k], here.relayed, relayed.at[:, :, :, lanes], sem, 16 * k))
    waits[0].start()
    acc[...] = jnp.zeros_like(acc)
    g_probe[...] = jnp.zeros_like(g_probe)
    stores = (
        [(acc.at[0], g_quarters.at[0])],
        [
            (acc.at[2], g_quarters.at[1]),
            (acc.at[1, :, :, own], g_tile_mid),
            (acc.at[1, :, :, here.on], g_on_mid),
            (acc.at[1, :, :, here.off], g_off_mid),
        ],
    )
    two_groups(here, (1, 2), 1, waits, stores, (early, late), amps, amp_sem, order, out_sem, probe, table, obj, acc, g_probe)


def outer_body(
    axes, tx, ty, centers, counts, tile, on, off_quarters, relayed, off_ends, left, right, carried, carried_probe, early, late, probe_in, table_in,
    g_tile_ends, g_tile_quarters, g_on_ends, g_on_quarters, g_off_ends, g_off_quarters,
    g_left, g_right, g_probe,
    obj, acc, probe, table, amps, order, sem, out_sem, amp_sem,
):
    width = probe.shape[-1]
    rim = width // 2
    tile_rows, tile_cols = tile.shape[2], tile.shape[3]
    here = Place(axes, (tx, ty, centers, counts), tile_rows, tile_cols, rim)
    own = slice(rim, rim + tile_rows)
    one, two = slice(0, rim), slice(rim, width)
    waits, stores = [], []
    for k, (end, quarter, near, far, half, side, g_side) in enumerate((
        (0, 1, two, slice(0, rim), one, left, g_left),
        (3, 2, one, slice(tile_cols - rim, tile_cols), two, right, g_right),
    )):
        first = rim if k == 0 else tile_cols - rim - width
        there = slice(first, first + width)
        edge = k * tile_cols
        loads = [(probe_in, probe), (table_in, table), (carried_probe, g_probe)] if k == 0 else []
        loads += [
            (tile.at[:, :, :, far], obj.at[end, :, :, own, near]),
            (side, obj.at[end, :, :, own, half]),
            (on.at[:, :, :, edge : edge + width], obj.at[end, :, :, here.on]),
            (off_ends.at[:, :, :, k * width : (k + 1) * width], obj.at[end, :, :, here.off]),
            (tile.at[:, :, :, there], obj.at[quarter, :, :, own]),
            (on.at[:, :, :, first + rim : first + rim + width], obj.at[quarter, :, :, here.on]),
            (carried.at[k], acc.at[quarter]),
        ]
        lanes = slice(k * width, (k + 1) * width)
        loads.append((off_quarters.at[:, :, :, lanes], obj.at[quarter, :, :, here.off]))
        waits.append(ChosenLoads(loads, here.relayed, relayed.at[:, :, :, lanes], sem, 16 * k))
        stores.append([
            (acc.at[end, :, :, own, near], g_tile_ends.at[:, :, :, half]),
            (acc.at[end, :, :, here.on, near], g_on_ends.at[:, :, :, half]),
            (acc.at[end, :, :, here.off, near], g_off_ends.at[:, :, :, half]),
            (acc.at[end, :, :, own, half], g_side.at[:, :, :tile_rows]),
            (acc.at[end, :, :, here.on, half], g_side.at[:, :, tile_rows : tile_rows + rim]),
            (acc.at[end, :, :, here.off, half], g_side.at[:, :, tile_rows + rim :]),
            (acc.at[quarter, :, :, own], g_tile_quarters.at[:, :, :, lanes]),
            (acc.at[quarter, :, :, here.on], g_on_quarters.at[:, :, :, lanes]),
            (acc.at[quarter, :, :, here.off], g_off_quarters.at[:, :, :, lanes]),
        ])
    waits[0].start()
    for end in (0, 3):
        acc[end] = jnp.zeros_like(acc[end])
    last_block = (tile_cols + 2 * rim) // width - 2
    two_groups(here, (0, last_block), 2, waits, stores, (early, late), amps, amp_sem, order, out_sem, probe, table, obj, acc, g_probe)


SMEM = pl.BlockSpec(memory_space=pltpu.SMEM)
VMEM = pl.BlockSpec(memory_space=pltpu.VMEM)
HBM = pl.BlockSpec(memory_space=pltpu.HBM)
ROOM = pltpu.CompilerParams(vmem_limit_bytes=63 * 2**20)


def shape(*dims):
    return jax.ShapeDtypeStruct(dims, F32)


def costs(flops):
    return pl.CostEstimate(flops=flops, bytes_accessed=10**7, transcendentals=0)


def field_call(body, axes, blocks, scalars, arrays, amplitudes, probe, outs, tile_rows):
    width = probe.shape[-1]
    padded = (blocks, 2, 2, tile_rows + width, width)
    table = tables(width)
    slots = sum(part.shape[0] for part in amplitudes)
    return pl.pallas_call(
        functools.partial(body, axes),
        out_shape=tuple(outs) + (jax.ShapeDtypeStruct(probe.shape, F32),),
        in_specs=[SMEM] * len(scalars) + [HBM] * (len(arrays) + 4),
        out_specs=(HBM,) * len(outs) + (VMEM,),
        scratch_shapes=[
            pltpu.VMEM(padded, F32),
            pltpu.VMEM(padded, F32),
            pltpu.VMEM(probe.shape, F32),
            pltpu.VMEM(table.shape, table.dtype),
            pltpu.VMEM((slots, width, width), F32),
            pltpu.SMEM((slots + 1,), jnp.int32),
            pltpu.SemaphoreType.DMA((32,)),
            pltpu.SemaphoreType.DMA((18,)),
            pltpu.SemaphoreType.DMA((slots,)),
        ],
        compiler_params=ROOM,
        cost_estimate=costs(2 * 10**10),
    )(*scalars, *arrays, *amplitudes, probe, table)


def pack_body(tx, tile, left, right, quarters, mid, sem):
    rim = left.shape[-1]
    width = 2 * rim
    tile_rows, tile_cols = tile.shape[2], tile.shape[3]
    rows = rows_at((tx[0] % 2) * (tile_rows - rim), rim)
    quarter = rim + width
    far = tile_cols - quarter
    wait_all(run_all([
        (tile.at[:, :, :, :rim], left),
        (tile.at[:, :, :, tile_cols - rim :], right),
        (tile.at[:, :, rows, rim:quarter], quarters.at[:, :, :, :width]),
        (tile.at[:, :, rows, far : far + width], quarters.at[:, :, :, width:]),
        (tile.at[:, :, rows, quarter:far], mid),
    ], sem))


def strips_body(tx, tile, left, right, on, ends, sem):
    rim = left.shape[-1]
    tile_rows, tile_cols = tile.shape[2], tile.shape[3]
    odd = tx[0] % 2
    inner = tile_rows - rim
    on_rows, off_rows = rows_at((1 - odd) * inner, rim), rows_at(odd * inner, rim)
    wait_all(run_all([
        (left.at[:, :, on_rows], on.at[:, :, :, :rim]),
        (tile.at[:, :, on_rows], on.at[:, :, :, rim : rim + tile_cols]),
        (right.at[:, :, on_rows], on.at[:, :, :, rim + tile_cols :]),
        (left.at[:, :, off_rows], ends.at[:, :, :, :rim]),
        (tile.at[:, :, off_rows, :rim], ends.at[:, :, :, rim : 2 * rim]),
        (tile.at[:, :, off_rows, tile_cols - rim :], ends.at[:, :, :, 2 * rim : 3 * rim]),
        (right.at[:, :, off_rows], ends.at[:, :, :, 3 * rim :]),
    ], sem))


def copies_call(body, scalars, arrays, outs, flops):
    return pl.pallas_call(
        body,
        out_shape=tuple(outs),
        in_specs=[SMEM] * len(scalars) + [HBM] * len(arrays),
        out_specs=(VMEM,) * len(outs),
        scratch_shapes=[pltpu.SemaphoreType.DMA((8,))],
        compiler_params=ROOM,
        cost_estimate=costs(flops),
    )(*scalars, *arrays)


def amplitude_body(axes, first, tx, ty, counts, patterns, pick, out):
    width = patterns.shape[-1]

    def work():
        hi, lo = split(jnp.sqrt(patterns[0]))
        both = jnp.dot(pick[0], pair(hi, lo, 1), preferred_element_type=F32).astype(jnp.bfloat16)
        out[0] = jnp.dot(both, pick[1:].reshape(-1, width), preferred_element_type=F32)

    pl.when(first + pl.program_id(0) < counts[tx[0] * axes[1] + ty[0]])(work)


def amplitudes_of(axes, scalars, patterns, first, count):
    width = patterns.shape[-1]
    pick = np.zeros((width, width))
    pick[np.arange(width), np.concatenate([np.arange(0, width, 2), np.arange(1, width, 2)])] = 1
    pick = jnp.asarray(np.stack([pick, pick.T, pick.T]).astype(ml_dtypes.bfloat16))
    block = pl.BlockSpec((1, width, width), lambda i: (first + i, 0, 0))
    return pl.pallas_call(
        functools.partial(amplitude_body, axes, first),
        grid=(count,),
        out_shape=shape(count, width, width),
        in_specs=[SMEM, SMEM, SMEM, block, VMEM],
        out_specs=pl.BlockSpec((1, width, width), lambda i: (i, 0, 0)),
        compiler_params=ROOM,
        cost_estimate=costs(10**11),
    )(*scalars, patterns, pick)


def merge_body(on_ends, off_ends, left, right, quarters, mid, on, off, sides, sem):
    rim = left.shape[-1]
    width = 2 * rim
    tile_rows = left.shape[2] - width
    on_rows, off_rows = slice(tile_rows, tile_rows + rim), slice(tile_rows + rim, tile_rows + width)
    wait_all(run_all([
        (on_ends, on.at[:, :, :, :width]),
        (off_ends, off),
        (left.at[:, :, on_rows], sides.at[0, :, :, :, :rim]),
        (right.at[:, :, on_rows], sides.at[0, :, :, :, rim:]),
        (left.at[:, :, off_rows], sides.at[1, :, :, :, :rim]),
        (right.at[:, :, off_rows], sides.at[1, :, :, :, rim:]),
        (quarters, on.at[:, :, :, width : 3 * width]),
        (mid, on.at[:, :, :, 3 * width :]),
    ], sem))
    on[:, :, :, :width] += sides[0]
    off[...] += sides[1]


def merged(on_ends, off_ends, left, right, quarters, mid):
    slices, _, rim, width = on_ends.shape
    cols = width + quarters.shape[3] + mid.shape[3]
    return pl.pallas_call(
        merge_body,
        out_shape=(shape(slices, 2, rim, cols), jax.ShapeDtypeStruct(off_ends.shape, F32)),
        in_specs=[HBM] * 6,
        out_specs=(VMEM, VMEM),
        scratch_shapes=[pltpu.VMEM((2,) + on_ends.shape, F32), pltpu.SemaphoreType.DMA((8,))],
        compiler_params=ROOM,
        cost_estimate=pl.CostEstimate(flops=10**6, bytes_accessed=10**5, transcendentals=0),
    )(on_ends, off_ends, left, right, quarters, mid)


def inner_total_body(axes, tx, quarters, mid, on, off_quarters, far_quarters, off_mid, out, total, on_part, off_part, sem):
    rim = on.shape[2]
    width = 2 * rim
    rows = quarters.shape[2]
    cols = out.shape[3]
    last = cols - 2 * width
    middle = slice(width, last)
    odd = tx[0] % 2
    wait_all(run_all([
        (quarters.at[:, :, :, :width], total.at[:, :, :, :width]),
        (mid, total.at[:, :, :, middle]),
        (quarters.at[:, :, :, width:], total.at[:, :, :, last:]),
        (on.at[:, :, :, width : 2 * width], on_part.at[:, :, :, :width]),
        (on.at[:, :, :, 3 * width :], on_part.at[:, :, :, middle]),
        (on.at[:, :, :, 2 * width : 3 * width], on_part.at[:, :, :, last:]),
        (off_mid, off_part.at[:, :, :, middle]),
    ], sem))
    is_far = (tx[0] == axes[0] // 2) | (tx[0] == axes[0] // 2 - 1)
    for here, source in ((is_far, far_quarters), (jnp.logical_not(is_far), off_quarters)):
        pairs = [(source.at[:, :, :, :width], off_part.at[:, :, :, :width]), (source.at[:, :, :, width:], off_part.at[:, :, :, last:])]
        pl.when(here)(lambda pairs=pairs: wait_all(run_all(pairs, sem)))
    total[:, :, rows_at((1 - odd) * (rows - rim), rim)] += on_part[...]
    total[:, :, rows_at(odd * (rows - rim), rim)] += off_part[...]
    wait_all(run_all([(total, out.at[:, :, :, rim : cols - rim])], sem))


def inner_total(axes, tx, parts, tile_shape):
    rim, width = parts[2].shape[2], 2 * parts[2].shape[2]
    cols = tile_shape[3] - width
    return pl.pallas_call(
        functools.partial(inner_total_body, axes),
        out_shape=jax.ShapeDtypeStruct(tile_shape, F32),
        in_specs=[SMEM] + [HBM] * len(parts),
        out_specs=HBM,
        scratch_shapes=[pltpu.VMEM(tile_shape[:3] + (cols,), F32)]
        + [pltpu.VMEM(tile_shape[:2] + (rim, cols), F32)] * 2
        + [pltpu.SemaphoreType.DMA((9,))],
        compiler_params=ROOM,
        cost_estimate=costs(10**8),
    )(tx, *parts)


def end_total_body(tx, ends, left, right, on, off, inner, out, total, sides, on_part, off_part, sem):
    del inner
    rim = on.shape[2]
    rows, cols = out.shape[2:]
    odd = tx[0] % 2
    wait_all(run_all([
        (ends, total),
        (left.at[:, :, :rows], sides.at[:, :, :, :rim]),
        (right.at[:, :, :rows], sides.at[:, :, :, rim:]),
        (on.at[:, :, :, : 2 * rim], on_part),
        (off, off_part),
    ], sem))
    total[...] += sides[...]
    total[:, :, rows_at((1 - odd) * (rows - rim), rim)] += on_part[...]
    total[:, :, rows_at(odd * (rows - rim), rim)] += off_part[...]
    wait_all(run_all([
        (total.at[:, :, :, :rim], out.at[:, :, :, :rim]),
        (total.at[:, :, :, rim:], out.at[:, :, :, cols - rim :]),
    ], sem))


def end_total(tx, parts, inner):
    ends, off = parts[0], parts[-1]
    return pl.pallas_call(
        end_total_body,
        out_shape=jax.ShapeDtypeStruct(inner.shape, F32),
        in_specs=[SMEM] + [HBM] * (len(parts) + 1),
        out_specs=HBM,
        scratch_shapes=[pltpu.VMEM(ends.shape, F32)] * 2 + [pltpu.VMEM(off.shape, F32)] * 2 + [pltpu.SemaphoreType.DMA((5,))],
        input_output_aliases={len(parts) + 1: 0},
        compiler_params=ROOM,
        cost_estimate=costs(10**11),
    )(tx, *parts, inner)


def along(x, step):
    count = lax.axis_size("ty")
    return lax.ppermute(x, "ty", [(i, i + step) for i in range(count) if 0 <= i + step < count])


def across(x, first, skip=None):
    pairs = []
    for i in range(first, lax.axis_size("tx") - 1, 2):
        if i != skip:
            pairs += [(i, i + 1), (i + 1, i)]
    return lax.ppermute(x, "tx", pairs)


def relay_out(x):
    count = lax.axis_size("tx")
    return lax.ppermute(x, "tx", [(count // 2 - 1, count - 1), (count // 2, 0)])


def relay_in(x):
    count = lax.axis_size("tx")
    return lax.ppermute(x, "tx", [(count - 1, count // 2), (0, count // 2 - 1)])


def after(x, *others):
    return lax.optimization_barrier((x,) + others)[0]


def halved(flat, apart):
    bit = (lax.axis_index("tx") // apart) % 2
    half = flat.shape[0] // 2
    pairs = [(i, i ^ apart) for i in range(lax.axis_size("tx"))]
    mine = lax.dynamic_slice_in_dim(flat, bit * half, half, 0)
    other = lax.dynamic_slice_in_dim(flat, (1 - bit) * half, half, 0)
    return mine + lax.ppermute(other, "tx", pairs)


def doubled(flat, apart, meanwhile):
    bit = (lax.axis_index("tx") // apart) % 2
    other = lax.ppermute(flat, "tx", [(i, i ^ apart) for i in range(lax.axis_size("tx"))])
    return joined(flat, after(other, meanwhile), bit)


def joined(flat, other, bit):
    return jnp.concatenate([jnp.where(bit == 0, flat, other), jnp.where(bit == 0, other, flat)], axis=0)


def per_device(object_slab, probe, patterns, centers, counts):
    slices, _, tile_rows, tile_cols = object_slab.shape
    width = probe.shape[-1]
    rim = width // 2
    axes = lax.axis_size("tx"), lax.axis_size("ty")
    middle = axes[0] // 2
    tx, ty = (lax.axis_index(axis).astype(jnp.int32).reshape(1) for axis in ("tx", "ty"))
    full = tile_rows + width
    mid_cols = tile_cols - 3 * width
    ends_shape = shape(slices, 2, rim, width)
    quarters_shape = shape(slices, 2, rim, 2 * width)
    mid_shape = shape(slices, 2, rim, mid_cols)
    side_shape = shape(slices, 2, full, rim)
    tile = object_slab

    column_shape = shape(slices, 2, tile_rows, rim)
    to_left, to_right, quarters, mid = copies_call(
        pack_body, (tx,), (tile,), (column_shape, column_shape, quarters_shape, mid_shape), 10**8
    )
    carried = relay_out(quarters)
    left, right = along(to_right, 1), along(to_left, -1)
    off_quarters = across(quarters, 1, middle - 1)
    off_mid = across(mid, 1)
    on_shape = shape(slices, 2, rim, tile_cols + width)
    part = patterns.shape[0] // 2
    early = amplitudes_of(axes, (tx, ty, counts), after(patterns, to_left), 0, part)

    def strips(patterns, tile, left, right):
        on, ends = copies_call(strips_body, (tx,), (tile, left, right), (on_shape, quarters_shape), 10**8)
        late = amplitudes_of(axes, (tx, ty, counts), after(patterns, on), part, part)
        return across(on, 0), ends, late

    def nothing(patterns, tile, left, right):
        return jnp.zeros(on_shape.shape, F32), jnp.zeros(quarters_shape.shape, F32), patterns[part:]

    relayed = relay_in(carried)
    on, ends, late = lax.cond(counts[0] >= 0, strips, nothing, patterns, after(tile, early, carried), left, right)
    amplitudes = (early, late)
    off_ends = across(ends, 1)

    scalars = (tx, ty, centers, counts)
    g_quarters, g_tile_mid, g_on_mid, g_off_mid, g_probe = field_call(
        inner_body, axes, 3, scalars, (tile, on, off_quarters, relayed, off_mid), amplitudes, probe,
        (shape(2, slices, 2, full, width), shape(slices, 2, tile_rows, mid_cols), mid_shape, mid_shape), tile_rows,
    )
    back_mid = across(g_off_mid, 1)
    g_tile_ends, g_tile_quarters, g_on_ends, g_on_quarters, g_off_ends, g_off_quarters, g_left, g_right, g_probe = field_call(
        outer_body, axes, 4, scalars, (tile, on, off_quarters, relayed, off_ends, left, right, g_quarters, g_probe), amplitudes, probe,
        (
            shape(slices, 2, tile_rows, width), shape(slices, 2, tile_rows, 2 * width), ends_shape, quarters_shape,
            ends_shape, quarters_shape, side_shape, side_shape,
        ),
        tile_rows,
    )
    g_off_quarters, g_left, g_right, g_probe, _ = lax.optimization_barrier((g_off_quarters, g_left, g_right, g_probe, back_mid))
    from_left, from_right = along(g_right, 1), along(g_left, -1)
    back_quarters = across(g_off_quarters, 1, middle - 1)
    apart = [1] + [2**k for k in range(axes[0].bit_length() - 2, 1, -1)]
    shard = g_probe.size // width // 2 ** len(apart)
    some = counts[0] >= 0

    def shared(flat, quarters):
        for step in apart:
            flat = halved(flat, step)
        far = lax.ppermute(after(quarters, flat), "tx", [(middle - 1, middle), (middle, middle - 1)])
        for step in (2**k for k in range(axes[1].bit_length() - 1)):
            flat = flat + lax.ppermute(flat, "ty", [(i, i ^ step) for i in range(axes[1])])
        return flat / jnp.sqrt(jnp.maximum(jnp.sum(counts), 1).astype(F32)), far

    flat, far_quarters = lax.cond(
        counts[0] >= 0, shared, lambda x, quarters: (x[:shard], quarters), g_probe.reshape(-1, width), g_off_quarters
    )
    other = lax.ppermute(flat, "tx", [(i, i ^ 2) for i in range(axes[0])])
    on_all, off_ends = merged(after(g_on_ends, flat, back_quarters), g_off_ends, from_left, from_right, g_on_quarters, g_on_mid)
    back_ends = across(off_ends, 1)
    back_on = across(on_all, 0)
    inner = inner_total(axes, tx, (g_tile_quarters, g_tile_mid, back_on, back_quarters, far_quarters, back_mid), tile.shape)
    flat = after(flat + other, on_all)
    for step in reversed(apart[1:]):
        flat = doubled(flat, step, inner)
    last = lax.ppermute(flat, "tx", [(i, i ^ 1) for i in range(axes[0])])
    inner = end_total(tx, (g_tile_ends, from_left, from_right, back_on, back_ends), inner)
    probe_sum = joined(flat, after(last, inner), lax.axis_index("tx") % 2).reshape(probe.shape)
    return (inner, probe_sum)


def solution(mesh):
    placed = (
        P(None, None, "tx", "ty"),
        P(),
        P(("tx", "ty"), None, None),
        P(("tx", "ty"), None),
        P(),
    )
    return jax.shard_map(
        per_device,
        mesh=mesh,
        in_specs=placed,
        out_specs=(P(None, None, "tx", "ty"), P()),
        check_vma=False,
    )
```

```python
import functools
import math

import jax
import jax.numpy as jnp
import ml_dtypes
import numpy as np
from jax import lax
from jax.experimental import pallas as pl
from jax.experimental.pallas import tpu as pltpu
from jax.sharding import PartitionSpec as P

KAPPA = 40.0
F32 = jnp.float32
FWD, INV, PROP, ADJ = 0, 1, 2, 3
LEFT = {FWD: (0, 2), INV: (1, 3), PROP: (4, 6), ADJ: (5, 7)}
RIGHT = {FWD: (1, 3), INV: (0, 2), PROP: (5, 7), ADJ: (4, 6)}


def tables(width):
    half = width // 2
    n = np.arange(half)
    freq = ((np.arange(width) + half) % width - half) / width
    factor = np.exp(-1j * math.pi * KAPPA * freq * freq)
    turn = 2j * np.pi / width
    scale = 1.0 / math.sqrt(width)
    even = np.exp(-turn * ((2 * n[:, None] * n[None, :]) % width)) * scale
    odd = np.exp(-turn * (((2 * n[:, None] + 1) * n[None, :]) % width)) * scale

    def combined(freqs):
        apart = n[:, None] - n[None, :]
        total = np.zeros((half, half), complex)
        for k in freqs:
            total += factor[k] * np.exp(turn * ((k * apart) % width))
        return total / width

    parts = []
    for c in (even, odd, combined(range(0, width, 2)), combined(range(1, width, 2))):
        real = np.block([[c.real, -c.imag], [c.imag, c.real]])
        for m in (real, real.T):
            hi = m.astype(ml_dtypes.bfloat16)
            lo = (m - hi.astype(np.float64)).astype(ml_dtypes.bfloat16)
            parts.append(np.concatenate([hi, lo], axis=0))
    return jnp.asarray(np.stack(parts))


def split(x):
    hi = x.astype(jnp.bfloat16)
    return hi, (x - hi.astype(F32)).astype(jnp.bfloat16)


def pair(x, y, axis):
    return jnp.concatenate([x, y], axis=axis)


def product(x, both, axis):
    size = both.shape[1]
    hi, lo = split(x)
    if axis == 0:
        first = jnp.dot(both, hi, preferred_element_type=F32)
        return first[:size] + first[size:] + jnp.dot(both[:size], lo, preferred_element_type=F32)
    first = jnp.dot(pair(hi, lo, 0), both[:size], preferred_element_type=F32)
    return first[: x.shape[0]] + first[x.shape[0] :] + jnp.dot(hi, both[size:], preferred_element_type=F32)


def one_side(re, im, kind, axis, table):
    half = re.shape[axis] // 2

    def halves(x):
        return (x[:half], x[half:]) if axis == 0 else (x[:, :half], x[:, half:])

    a, b = halves(re)
    c, d = halves(im)
    if kind != INV:
        a, b, c, d = a + b, a - b, c + d, c - d
    even, odd = (LEFT if axis == 0 else RIGHT)[kind]
    a, c = halves(product(pair(a, c, axis), table[even], axis))
    b, d = halves(product(pair(b, d, axis), table[odd], axis))
    if kind == FWD:
        return pair(a, b, axis), pair(c, d, axis)
    return pair(a + b, a - b, axis), pair(c + d, c - d, axis)


def transform(re, im, kind, table):
    re, im = one_side(re, im, kind, 1, table)
    return one_side(re, im, kind, 0, table)


def times(a, b, c, d):
    return a * c - b * d, a * d + b * c


def conj_times(a, b, c, d):
    return a * c + b * d, a * d - b * c


class Slot:
    def __init__(self, start, block, amplitude, obj, acc):
        width = obj.shape[-1]
        self.width, self.block, self.amplitude, self.obj, self.acc = width, block, amplitude, obj, acc
        self.row, self.shift = start[0], start[1] % width
        self.below = lax.broadcasted_iota(jnp.int32, (width, width), 0) < self.row
        self.beside = lax.broadcasted_iota(jnp.int32, (width, width), 1) < self.shift

    def cut(self, level):
        width, block, obj = self.width, self.block, self.obj

        def part(k):
            upper = jnp.where(self.beside, obj[block + 1, level, k, :width], obj[block, level, k, :width])
            lower = jnp.where(self.beside, obj[block + 1, level, k, width:], obj[block, level, k, width:])
            return jnp.where(self.below, lower, upper)

        return part(0), part(1)

    def deposit(self, level, terms):
        width, block, acc = self.width, self.block, self.acc
        for k, term in enumerate(terms):
            zero = jnp.zeros_like(term)
            upper = jnp.where(self.below, zero, term)
            lower = jnp.where(self.below, term, zero)
            acc[block, level, k, :width] += jnp.where(self.beside, zero, upper)
            acc[block, level, k, width:] += jnp.where(self.beside, zero, lower)
            acc[block + 1, level, k, :width] += jnp.where(self.beside, upper, zero)
            acc[block + 1, level, k, width:] += jnp.where(self.beside, lower, zero)

    def rolled(self, x):
        return pltpu.roll(pltpu.roll(x, self.row, 0), self.shift, 1)

    def rolled_back(self, x):
        width = self.width
        return pltpu.roll(pltpu.roll(x, (width - self.row) % width, 0), (width - self.shift) % width, 1)


def visit(slots, probe, table, g_probe):
    def transformed(fields, kind):
        for axis in (1, 0):
            fields = [one_side(*field, kind, axis, table) for field in fields]
        return fields

    u0 = [(slot.rolled(probe[0]), slot.rolled(probe[1])) for slot in slots]
    o0 = [slot.cut(0) for slot in slots]
    u1 = transformed([times(*u, *o) for u, o in zip(u0, o0)], PROP)
    o1 = [slot.cut(1) for slot in slots]
    far = transformed([times(*u, *o) for u, o in zip(u1, o1)], FWD)
    factors = [1.0 - slot.amplitude() * lax.rsqrt(re * re + im * im + 1.0) for slot, (re, im) in zip(slots, far)]
    chi = transformed([(re * factor, im * factor) for factor, (re, im) in zip(factors, far)], INV)
    back = [conj_times(*o, *x) for o, x in zip(o1, chi)]
    for slot, u, x in zip(slots, u1, chi):
        slot.deposit(1, conj_times(*u, *x))
    chi = transformed(back, ADJ)
    for slot, u, x in zip(slots, u0, chi):
        slot.deposit(0, conj_times(*u, *x))
    for slot, o, x in zip(slots, o0, chi):
        for part, term in enumerate(conj_times(*o, *x)):
            g_probe[part] += slot.rolled_back(term)


class Place:
    def __init__(self, axes, scalars, tile_rows, tile_cols, rim):
        down, along, self.centers, counts = scalars
        tx, ty = down[0], along[0]
        odd = tx % 2
        self.count = counts[tx * axes[1] + ty]
        self.relayed = (tx == axes[0] // 2) | (tx == axes[0] // 2 - 1)
        self.first = tx * tile_rows, ty * tile_cols
        inner = tile_rows - rim
        self.on_tile, self.off_tile = rows_at((1 - odd) * inner, rim), rows_at(odd * inner, rim)
        outer = tile_rows + rim
        self.on, self.off = rows_at((1 - odd) * outer, rim), rows_at(odd * outer, rim)

    def start(self, slot):
        return self.centers[slot, 0] - self.first[0], self.centers[slot, 1] - self.first[1]


def rows_at(first, count):
    return pl.ds(pl.multiple_of(first, count), count)


def start_all(pairs, sem, at):
    copies = [pltpu.make_async_copy(a, b, sem.at[at + i]) for i, (a, b) in enumerate(pairs)]
    for copy in copies:
        copy.start()
    return copies


def run_all(pairs, sem):
    return start_all(pairs, sem, 0)


def wait_all(copies):
    for copy in copies:
        copy.wait()


class Loads:
    def __init__(self, pairs, sem, at):
        self.pairs, self.sem, self.at = pairs, sem, at

    def copies(self):
        return [pltpu.make_async_copy(a, b, self.sem.at[self.at + i]) for i, (a, b) in enumerate(self.pairs)]

    def start(self):
        for copy in self.copies():
            copy.start()

    def wait(self):
        wait_all(self.copies())


class ChosenLoads(Loads):
    def __init__(self, pairs, flag, other, sem, at):
        super().__init__(pairs, sem, at)
        self.flag, self.other = flag, other

    def start(self):
        copies = self.copies()
        for copy in copies[:-1]:
            copy.start()
        place = self.sem.at[self.at + len(copies) - 1]
        pl.when(self.flag)(lambda: pltpu.make_async_copy(self.other, self.pairs[-1][1], place).start())
        pl.when(jnp.logical_not(self.flag))(lambda: copies[-1].start())


def two_groups(here, firsts, step, loads, stores, amplitudes, amps, amp_sem, order, sem, probe, table, obj, acc, g_probe):
    width = probe.shape[-1]

    def listed(g, count):
        def look(slot, n):
            order[n] = slot
            return n + (here.start(slot)[1] // width == firsts[g]).astype(jnp.int32)

        return lax.fori_loop(0, here.count, look, count)

    first = listed(0, jnp.zeros((), jnp.int32))
    count = listed(1, first)

    part = amplitudes[0].shape[0]

    def amplitude_copy(slot, source):
        return pltpu.make_async_copy(source, amps.at[slot], amp_sem.at[slot])

    def fetch(i, _):
        slot = order[i]
        pl.when(slot < part)(lambda: amplitude_copy(slot, amplitudes[0].at[slot]).start())
        pl.when(slot >= part)(lambda: amplitude_copy(slot, amplitudes[1].at[slot - part]).start())
        return 0

    lax.fori_loop(0, count, fetch, 0)

    def store(g):
        start_all(stores[g], sem, g * len(stores[0]))

    def slot_at(i):
        slot = order[i]

        def amplitude():
            amplitude_copy(slot, amplitudes[0].at[0]).wait()
            return amps[slot]

        return Slot(here.start(slot), step * (i >= first).astype(jnp.int32), amplitude, obj, acc)

    def after_first(i):
        pl.when((i < first) & (first <= i + 2))(lambda: store(0))

    def two(p, _):
        i = 2 * p
        pl.when((i + 1 >= first) & (i - 1 < first))(loads[1].wait)
        pl.when((first == 0) & (p == 0))(lambda: store(0))
        visit([slot_at(i), slot_at(i + 1)], probe, table, g_probe)
        after_first(i)
        return 0

    def one():
        visit([slot_at(count - 1)], probe, table, g_probe)
        after_first(count - 1)

    soon = first < 2
    pl.when(soon)(loads[1].start)
    loads[0].wait()
    pl.when(jnp.logical_not(soon))(loads[1].start)
    pairs = count // 2
    lax.fori_loop(0, pairs, two, 0)
    pl.when(2 * pairs - 1 < first)(loads[1].wait)
    pl.when((first == 0) & (pairs == 0))(lambda: store(0))
    pl.when(count % 2 == 1)(one)
    store(1)
    for g in (0, 1):
        wait_all([pltpu.make_async_copy(a, b, sem.at[g * len(stores[0]) + i]) for i, (a, b) in enumerate(stores[g])])


def inner_body(
    axes, tx, ty, centers, counts, tile, on, off_quarters, relayed, off_mid, early, late, probe_in, table_in,
    g_quarters, g_tile_mid, g_on_mid, g_off_mid, g_probe, obj, acc, probe, table, amps, order, sem, out_sem, amp_sem,
):
    width = probe.shape[-1]
    rim = width // 2
    tile_rows, tile_cols = tile.shape[2], tile.shape[3]
    here = Place(axes, (tx, ty, centers, counts), tile_rows, tile_cols, rim)
    own = slice(rim, rim + tile_rows)
    loads = ([(probe_in, probe), (table_in, table)], [])
    for k in range(3):
        there = slice(rim + k * width, rim + (k + 1) * width)
        loads[k // 2].append((tile.at[:, :, :, there], obj.at[k, :, :, own]))
        loads[k // 2].append((on.at[:, :, :, (k + 1) * width : (k + 2) * width], obj.at[k, :, :, here.on]))
    loads[0].append((off_mid, obj.at[1, :, :, here.off]))
    waits = []
    for k in (0, 1):
        lanes = slice(k * width, (k + 1) * width)
        loads[k].append((off_quarters.at[:, :, :, lanes], obj.at[2 * k, :, :, here.off]))
        waits.append(ChosenLoads(loads[k], here.relayed, relayed.at[:, :, :, lanes], sem, 16 * k))
    waits[0].start()
    acc[...] = jnp.zeros_like(acc)
    g_probe[...] = jnp.zeros_like(g_probe)
    stores = (
        [(acc.at[0], g_quarters.at[0])],
        [
            (acc.at[2], g_quarters.at[1]),
            (acc.at[1, :, :, own], g_tile_mid),
            (acc.at[1, :, :, here.on], g_on_mid),
            (acc.at[1, :, :, here.off], g_off_mid),
        ],
    )
    two_groups(here, (1, 2), 1, waits, stores, (early, late), amps, amp_sem, order, out_sem, probe, table, obj, acc, g_probe)


def outer_body(
    axes, tx, ty, centers, counts, tile, on, off_quarters, relayed, off_ends, left, right, carried, carried_probe, early, late, probe_in, table_in,
    g_tile_ends, g_tile_quarters, g_on_ends, g_on_quarters, g_off_ends, g_off_quarters,
    g_left, g_right, g_probe,
    obj, acc, probe, table, amps, order, sem, out_sem, amp_sem,
):
    width = probe.shape[-1]
    rim = width // 2
    tile_rows, tile_cols = tile.shape[2], tile.shape[3]
    here = Place(axes, (tx, ty, centers, counts), tile_rows, tile_cols, rim)
    own = slice(rim, rim + tile_rows)
    one, two = slice(0, rim), slice(rim, width)
    waits, stores = [], []
    for k, (end, quarter, near, far, half, side, g_side) in enumerate((
        (0, 1, two, slice(0, rim), one, left, g_left),
        (3, 2, one, slice(tile_cols - rim, tile_cols), two, right, g_right),
    )):
        first = rim if k == 0 else tile_cols - rim - width
        there = slice(first, first + width)
        edge = k * tile_cols
        loads = [(probe_in, probe), (table_in, table), (carried_probe, g_probe)] if k == 0 else []
        loads += [
            (tile.at[:, :, :, far], obj.at[end, :, :, own, near]),
            (side, obj.at[end, :, :, own, half]),
            (on.at[:, :, :, edge : edge + width], obj.at[end, :, :, here.on]),
            (off_ends.at[:, :, :, k * width : (k + 1) * width], obj.at[end, :, :, here.off]),
            (tile.at[:, :, :, there], obj.at[quarter, :, :, own]),
            (on.at[:, :, :, first + rim : first + rim + width], obj.at[quarter, :, :, here.on]),
            (carried.at[k], acc.at[quarter]),
        ]
        lanes = slice(k * width, (k + 1) * width)
        loads.append((off_quarters.at[:, :, :, lanes], obj.at[quarter, :, :, here.off]))
        waits.append(ChosenLoads(loads, here.relayed, relayed.at[:, :, :, lanes], sem, 16 * k))
        stores.append([
            (acc.at[end, :, :, own, near], g_tile_ends.at[:, :, :, half]),
            (acc.at[end, :, :, here.on, near], g_on_ends.at[:, :, :, half]),
            (acc.at[end, :, :, here.off, near], g_off_ends.at[:, :, :, half]),
            (acc.at[end, :, :, own, half], g_side.at[:, :, :tile_rows]),
            (acc.at[end, :, :, here.on, half], g_side.at[:, :, tile_rows : tile_rows + rim]),
            (acc.at[end, :, :, here.off, half], g_side.at[:, :, tile_rows + rim :]),
            (acc.at[quarter, :, :, own], g_tile_quarters.at[:, :, :, lanes]),
            (acc.at[quarter, :, :, here.on], g_on_quarters.at[:, :, :, lanes]),
            (acc.at[quarter, :, :, here.off], g_off_quarters.at[:, :, :, lanes]),
        ])
    waits[0].start()
    for end in (0, 3):
        acc[end] = jnp.zeros_like(acc[end])
    last_block = (tile_cols + 2 * rim) // width - 2
    two_groups(here, (0, last_block), 2, waits, stores, (early, late), amps, amp_sem, order, out_sem, probe, table, obj, acc, g_probe)
    positions = lax.fori_loop(0, counts.shape[0], lambda i, n: n + counts[i], jnp.zeros((), jnp.int32))
    g_probe[...] = g_probe[...] / jnp.sqrt(jnp.full(g_probe.shape, jnp.maximum(positions, 1).astype(F32)))


SMEM = pl.BlockSpec(memory_space=pltpu.SMEM)
VMEM = pl.BlockSpec(memory_space=pltpu.VMEM)
HBM = pl.BlockSpec(memory_space=pltpu.HBM)
ROOM = pltpu.CompilerParams(vmem_limit_bytes=63 * 2**20)


def shape(*dims):
    return jax.ShapeDtypeStruct(dims, F32)


def costs(flops):
    return pl.CostEstimate(flops=flops, bytes_accessed=10**7, transcendentals=0)


def field_call(body, axes, blocks, scalars, arrays, amplitudes, probe, outs, tile_rows):
    width = probe.shape[-1]
    padded = (blocks, 2, 2, tile_rows + width, width)
    table = tables(width)
    slots = sum(part.shape[0] for part in amplitudes)
    return pl.pallas_call(
        functools.partial(body, axes),
        out_shape=tuple(outs) + (jax.ShapeDtypeStruct(probe.shape, F32),),
        in_specs=[SMEM] * len(scalars) + [HBM] * (len(arrays) + 4),
        out_specs=(HBM,) * len(outs) + (VMEM,),
        scratch_shapes=[
            pltpu.VMEM(padded, F32),
            pltpu.VMEM(padded, F32),
            pltpu.VMEM(probe.shape, F32),
            pltpu.VMEM(table.shape, table.dtype),
            pltpu.VMEM((slots, width, width), F32),
            pltpu.SMEM((slots + 1,), jnp.int32),
            pltpu.SemaphoreType.DMA((32,)),
            pltpu.SemaphoreType.DMA((18,)),
            pltpu.SemaphoreType.DMA((slots,)),
        ],
        compiler_params=ROOM,
        cost_estimate=costs(2 * 10**10),
    )(*scalars, *arrays, *amplitudes, probe, table)


def pack_body(tx, tile, left, right, quarters, mid, sem):
    rim = left.shape[-1]
    width = 2 * rim
    tile_rows, tile_cols = tile.shape[2], tile.shape[3]
    rows = rows_at((tx[0] % 2) * (tile_rows - rim), rim)
    quarter = rim + width
    far = tile_cols - quarter
    wait_all(run_all([
        (tile.at[:, :, :, :rim], left),
        (tile.at[:, :, :, tile_cols - rim :], right),
        (tile.at[:, :, rows, rim:quarter], quarters.at[:, :, :, :width]),
        (tile.at[:, :, rows, far : far + width], quarters.at[:, :, :, width:]),
        (tile.at[:, :, rows, quarter:far], mid),
    ], sem))


def strips_body(tx, tile, left, right, on, ends, sem):
    rim = left.shape[-1]
    tile_rows, tile_cols = tile.shape[2], tile.shape[3]
    odd = tx[0] % 2
    inner = tile_rows - rim
    on_rows, off_rows = rows_at((1 - odd) * inner, rim), rows_at(odd * inner, rim)
    wait_all(run_all([
        (left.at[:, :, on_rows], on.at[:, :, :, :rim]),
        (tile.at[:, :, on_rows], on.at[:, :, :, rim : rim + tile_cols]),
        (right.at[:, :, on_rows], on.at[:, :, :, rim + tile_cols :]),
        (left.at[:, :, off_rows], ends.at[:, :, :, :rim]),
        (tile.at[:, :, off_rows, :rim], ends.at[:, :, :, rim : 2 * rim]),
        (tile.at[:, :, off_rows, tile_cols - rim :], ends.at[:, :, :, 2 * rim : 3 * rim]),
        (right.at[:, :, off_rows], ends.at[:, :, :, 3 * rim :]),
    ], sem))


def copies_call(body, scalars, arrays, outs, flops):
    return pl.pallas_call(
        body,
        out_shape=tuple(outs),
        in_specs=[SMEM] * len(scalars) + [HBM] * len(arrays),
        out_specs=(VMEM,) * len(outs),
        scratch_shapes=[pltpu.SemaphoreType.DMA((8,))],
        compiler_params=ROOM,
        cost_estimate=costs(flops),
    )(*scalars, *arrays)


def amplitude_body(axes, first, tx, ty, counts, patterns, pick, out):
    width = patterns.shape[-1]

    def work():
        hi, lo = split(jnp.sqrt(patterns[0]))
        both = jnp.dot(pick[0], pair(hi, lo, 1), preferred_element_type=F32).astype(jnp.bfloat16)
        out[0] = jnp.dot(both, pick[1:].reshape(-1, width), preferred_element_type=F32)

    pl.when(first + pl.program_id(0) < counts[tx[0] * axes[1] + ty[0]])(work)


def amplitudes_of(axes, scalars, patterns, first, count):
    width = patterns.shape[-1]
    pick = np.zeros((width, width))
    pick[np.arange(width), np.concatenate([np.arange(0, width, 2), np.arange(1, width, 2)])] = 1
    pick = jnp.asarray(np.stack([pick, pick.T, pick.T]).astype(ml_dtypes.bfloat16))
    block = pl.BlockSpec((1, width, width), lambda i: (first + i, 0, 0))
    return pl.pallas_call(
        functools.partial(amplitude_body, axes, first),
        grid=(count,),
        out_shape=shape(count, width, width),
        in_specs=[SMEM, SMEM, SMEM, block, VMEM],
        out_specs=pl.BlockSpec((1, width, width), lambda i: (i, 0, 0)),
        compiler_params=ROOM,
        cost_estimate=costs(10**11),
    )(*scalars, patterns, pick)


def merge_body(on_ends, off_ends, left, right, quarters, mid, on, off, sides, sem):
    rim = left.shape[-1]
    width = 2 * rim
    tile_rows = left.shape[2] - width
    on_rows, off_rows = slice(tile_rows, tile_rows + rim), slice(tile_rows + rim, tile_rows + width)
    wait_all(run_all([
        (on_ends, on.at[:, :, :, :width]),
        (off_ends, off),
        (left.at[:, :, on_rows], sides.at[0, :, :, :, :rim]),
        (right.at[:, :, on_rows], sides.at[0, :, :, :, rim:]),
        (left.at[:, :, off_rows], sides.at[1, :, :, :, :rim]),
        (right.at[:, :, off_rows], sides.at[1, :, :, :, rim:]),
        (quarters, on.at[:, :, :, width : 3 * width]),
        (mid, on.at[:, :, :, 3 * width :]),
    ], sem))
    on[:, :, :, :width] += sides[0]
    off[...] += sides[1]


def merged(on_ends, off_ends, left, right, quarters, mid):
    slices, _, rim, width = on_ends.shape
    cols = width + quarters.shape[3] + mid.shape[3]
    return pl.pallas_call(
        merge_body,
        out_shape=(shape(slices, 2, rim, cols), jax.ShapeDtypeStruct(off_ends.shape, F32)),
        in_specs=[HBM] * 6,
        out_specs=(VMEM, VMEM),
        scratch_shapes=[pltpu.VMEM((2,) + on_ends.shape, F32), pltpu.SemaphoreType.DMA((8,))],
        compiler_params=ROOM,
        cost_estimate=pl.CostEstimate(flops=10**6, bytes_accessed=10**5, transcendentals=0),
    )(on_ends, off_ends, left, right, quarters, mid)


def inner_total_body(axes, tx, quarters, mid, on, off_quarters, far_quarters, off_mid, out, total, on_part, off_part, sem):
    rim = on.shape[2]
    width = 2 * rim
    rows = quarters.shape[2]
    cols = out.shape[3]
    last = cols - 2 * width
    middle = slice(width, last)
    odd = tx[0] % 2
    wait_all(run_all([
        (quarters.at[:, :, :, :width], total.at[:, :, :, :width]),
        (mid, total.at[:, :, :, middle]),
        (quarters.at[:, :, :, width:], total.at[:, :, :, last:]),
        (on.at[:, :, :, width : 2 * width], on_part.at[:, :, :, :width]),
        (on.at[:, :, :, 3 * width :], on_part.at[:, :, :, middle]),
        (on.at[:, :, :, 2 * width : 3 * width], on_part.at[:, :, :, last:]),
        (off_mid, off_part.at[:, :, :, middle]),
    ], sem))
    is_far = (tx[0] == axes[0] // 2) | (tx[0] == axes[0] // 2 - 1)
    for here, source in ((is_far, far_quarters), (jnp.logical_not(is_far), off_quarters)):
        pairs = [(source.at[:, :, :, :width], off_part.at[:, :, :, :width]), (source.at[:, :, :, width:], off_part.at[:, :, :, last:])]
        pl.when(here)(lambda pairs=pairs: wait_all(run_all(pairs, sem)))
    total[:, :, rows_at((1 - odd) * (rows - rim), rim)] += on_part[...]
    total[:, :, rows_at(odd * (rows - rim), rim)] += off_part[...]
    wait_all(run_all([(total, out.at[:, :, :, rim : cols - rim])], sem))


def inner_total(axes, tx, parts, tile_shape):
    rim, width = parts[2].shape[2], 2 * parts[2].shape[2]
    cols = tile_shape[3] - width
    return pl.pallas_call(
        functools.partial(inner_total_body, axes),
        out_shape=jax.ShapeDtypeStruct(tile_shape, F32),
        in_specs=[SMEM] + [HBM] * len(parts),
        out_specs=HBM,
        scratch_shapes=[pltpu.VMEM(tile_shape[:3] + (cols,), F32)]
        + [pltpu.VMEM(tile_shape[:2] + (rim, cols), F32)] * 2
        + [pltpu.SemaphoreType.DMA((9,))],
        compiler_params=ROOM,
        cost_estimate=costs(10**8),
    )(tx, *parts)


def end_total_body(tx, ends, left, right, on, off, inner, out, total, sides, on_part, off_part, sem):
    del inner
    rim = on.shape[2]
    rows, cols = out.shape[2:]
    odd = tx[0] % 2
    wait_all(run_all([
        (ends, total),
        (left.at[:, :, :rows], sides.at[:, :, :, :rim]),
        (right.at[:, :, :rows], sides.at[:, :, :, rim:]),
        (on.at[:, :, :, : 2 * rim], on_part),
        (off, off_part),
    ], sem))
    total[...] += sides[...]
    total[:, :, rows_at((1 - odd) * (rows - rim), rim)] += on_part[...]
    total[:, :, rows_at(odd * (rows - rim), rim)] += off_part[...]
    wait_all(run_all([
        (total.at[:, :, :, :rim], out.at[:, :, :, :rim]),
        (total.at[:, :, :, rim:], out.at[:, :, :, cols - rim :]),
    ], sem))


def end_total(tx, parts, inner):
    ends, off = parts[0], parts[-1]
    return pl.pallas_call(
        end_total_body,
        out_shape=jax.ShapeDtypeStruct(inner.shape, F32),
        in_specs=[SMEM] + [HBM] * (len(parts) + 1),
        out_specs=HBM,
        scratch_shapes=[pltpu.VMEM(ends.shape, F32)] * 2 + [pltpu.VMEM(off.shape, F32)] * 2 + [pltpu.SemaphoreType.DMA((5,))],
        input_output_aliases={len(parts) + 1: 0},
        compiler_params=ROOM,
        cost_estimate=costs(10**11),
    )(tx, *parts, inner)


def along(x, step):
    count = lax.axis_size("ty")
    return lax.ppermute(x, "ty", [(i, i + step) for i in range(count) if 0 <= i + step < count])


def across(x, first, skip=None):
    pairs = []
    for i in range(first, lax.axis_size("tx") - 1, 2):
        if i != skip:
            pairs += [(i, i + 1), (i + 1, i)]
    return lax.ppermute(x, "tx", pairs)


def relay_out(x):
    count = lax.axis_size("tx")
    return lax.ppermute(x, "tx", [(count // 2 - 1, count - 1), (count // 2, 0)])


def relay_in(x):
    count = lax.axis_size("tx")
    return lax.ppermute(x, "tx", [(count - 1, count // 2), (0, count // 2 - 1)])


def after(x, *others):
    return lax.optimization_barrier((x,) + others)[0]


def halved(flat, apart):
    bit = (lax.axis_index("tx") // apart) % 2
    half = flat.shape[0] // 2
    pairs = [(i, i ^ apart) for i in range(lax.axis_size("tx"))]
    mine = lax.dynamic_slice_in_dim(flat, bit * half, half, 0)
    other = lax.dynamic_slice_in_dim(flat, (1 - bit) * half, half, 0)
    return mine + lax.ppermute(other, "tx", pairs)


def doubled(flat, apart, meanwhile):
    bit = (lax.axis_index("tx") // apart) % 2
    other = lax.ppermute(flat, "tx", [(i, i ^ apart) for i in range(lax.axis_size("tx"))])
    return joined(flat, after(other, meanwhile), bit)


def joined(flat, other, bit):
    return jnp.concatenate([jnp.where(bit == 0, flat, other), jnp.where(bit == 0, other, flat)], axis=0)


def per_device(object_slab, probe, patterns, centers, counts):
    slices, _, tile_rows, tile_cols = object_slab.shape
    width = probe.shape[-1]
    rim = width // 2
    axes = lax.axis_size("tx"), lax.axis_size("ty")
    middle = axes[0] // 2
    tx, ty = (lax.axis_index(axis).astype(jnp.int32).reshape(1) for axis in ("tx", "ty"))
    full = tile_rows + width
    mid_cols = tile_cols - 3 * width
    ends_shape = shape(slices, 2, rim, width)
    quarters_shape = shape(slices, 2, rim, 2 * width)
    mid_shape = shape(slices, 2, rim, mid_cols)
    side_shape = shape(slices, 2, full, rim)
    tile = object_slab

    column_shape = shape(slices, 2, tile_rows, rim)
    to_left, to_right, quarters, mid = copies_call(
        pack_body, (tx,), (tile,), (column_shape, column_shape, quarters_shape, mid_shape), 10**8
    )
    carried = relay_out(quarters)
    left, right = along(to_right, 1), along(to_left, -1)
    off_quarters = across(quarters, 1, middle - 1)
    off_mid = across(mid, 1)
    on_shape = shape(slices, 2, rim, tile_cols + width)
    part = patterns.shape[0] // 2
    early = amplitudes_of(axes, (tx, ty, counts), after(patterns, to_left), 0, part)

    def strips(patterns, tile, left, right):
        on, ends = copies_call(strips_body, (tx,), (tile, left, right), (on_shape, quarters_shape), 10**8)
        late = amplitudes_of(axes, (tx, ty, counts), after(patterns, on), part, part)
        return across(on, 0), ends, late

    def nothing(patterns, tile, left, right):
        return jnp.zeros(on_shape.shape, F32), jnp.zeros(quarters_shape.shape, F32), patterns[part:]

    relayed = relay_in(carried)
    on, ends, late = lax.cond(counts[0] >= 0, strips, nothing, patterns, after(tile, early, carried), left, right)
    amplitudes = (early, late)
    off_ends = across(ends, 1)

    scalars = (tx, ty, centers, counts)
    g_quarters, g_tile_mid, g_on_mid, g_off_mid, g_probe = field_call(
        inner_body, axes, 3, scalars, (tile, on, off_quarters, relayed, off_mid), amplitudes, probe,
        (shape(2, slices, 2, full, width), shape(slices, 2, tile_rows, mid_cols), mid_shape, mid_shape), tile_rows,
    )
    back_mid = across(g_off_mid, 1)
    g_tile_ends, g_tile_quarters, g_on_ends, g_on_quarters, g_off_ends, g_off_quarters, g_left, g_right, g_probe = field_call(
        outer_body, axes, 4, scalars, (tile, on, off_quarters, relayed, off_ends, left, right, g_quarters, g_probe), amplitudes, probe,
        (
            shape(slices, 2, tile_rows, width), shape(slices, 2, tile_rows, 2 * width), ends_shape, quarters_shape,
            ends_shape, quarters_shape, side_shape, side_shape,
        ),
        tile_rows,
    )
    g_off_quarters, g_left, g_right, g_probe, _ = lax.optimization_barrier((g_off_quarters, g_left, g_right, g_probe, back_mid))
    from_left, from_right = along(g_right, 1), along(g_left, -1)
    back_quarters = across(g_off_quarters, 1, middle - 1)
    apart = [1] + [2**k for k in range(axes[0].bit_length() - 2, 1, -1)]
    shard = g_probe.size // width // 2 ** len(apart)
    some = counts[0] >= 0

    def shared(flat, quarters):
        for step in apart:
            flat = halved(flat, step)
        far = lax.ppermute(after(quarters, flat), "tx", [(middle - 1, middle), (middle, middle - 1)])
        for step in (2**k for k in range(axes[1].bit_length() - 1)):
            flat = flat + lax.ppermute(flat, "ty", [(i, i ^ step) for i in range(axes[1])])
        return flat, far

    flat, far_quarters = lax.cond(
        counts[0] >= 0, shared, lambda x, quarters: (x[:shard], quarters), g_probe.reshape(-1, width), g_off_quarters
    )
    other = lax.ppermute(flat, "tx", [(i, i ^ 2) for i in range(axes[0])])
    on_all, off_ends = merged(after(g_on_ends, flat, back_quarters), g_off_ends, from_left, from_right, g_on_quarters, g_on_mid)
    back_ends = across(off_ends, 1)
    back_on = across(on_all, 0)
    inner = inner_total(axes, tx, (g_tile_quarters, g_tile_mid, back_on, back_quarters, far_quarters, back_mid), tile.shape)
    flat = after(flat + other, on_all)
    for step in reversed(apart[1:]):
        flat = doubled(flat, step, inner)
    last = lax.ppermute(flat, "tx", [(i, i ^ 1) for i in range(axes[0])])
    inner = end_total(tx, (g_tile_ends, from_left, from_right, back_on, back_ends), inner)
    probe_sum = joined(flat, after(last, inner), lax.axis_index("tx") % 2).reshape(probe.shape)
    return (inner, probe_sum)


def solution(mesh):
    placed = (
        P(None, None, "tx", "ty"),
        P(),
        P(("tx", "ty"), None, None),
        P(("tx", "ty"), None),
        P(),
    )
    return jax.shard_map(
        per_device,
        mesh=mesh,
        in_specs=placed,
        out_specs=(P(None, None, "tx", "ty"), P()),
        check_vma=False,
    )
```

```python
import functools
import math

import jax
import jax.numpy as jnp
import ml_dtypes
import numpy as np
from jax import lax
from jax.experimental import pallas as pl
from jax.experimental.pallas import tpu as pltpu
from jax.sharding import PartitionSpec as P

KAPPA = 40.0
F32 = jnp.float32
FWD, INV, PROP, ADJ = 0, 1, 2, 3
LEFT = {FWD: (0, 2), INV: (1, 3), PROP: (4, 6), ADJ: (5, 7)}
RIGHT = {FWD: (1, 3), INV: (0, 2), PROP: (5, 7), ADJ: (4, 6)}


def tables(width):
    half = width // 2
    n = np.arange(half)
    freq = ((np.arange(width) + half) % width - half) / width
    factor = np.exp(-1j * math.pi * KAPPA * freq * freq)
    turn = 2j * np.pi / width
    scale = 1.0 / math.sqrt(width)
    even = np.exp(-turn * ((2 * n[:, None] * n[None, :]) % width)) * scale
    odd = np.exp(-turn * (((2 * n[:, None] + 1) * n[None, :]) % width)) * scale

    def combined(freqs):
        apart = n[:, None] - n[None, :]
        total = np.zeros((half, half), complex)
        for k in freqs:
            total += factor[k] * np.exp(turn * ((k * apart) % width))
        return total / width

    parts = []
    for c in (even, odd, combined(range(0, width, 2)), combined(range(1, width, 2))):
        real = np.block([[c.real, -c.imag], [c.imag, c.real]])
        for m in (real, real.T):
            hi = m.astype(ml_dtypes.bfloat16)
            lo = (m - hi.astype(np.float64)).astype(ml_dtypes.bfloat16)
            parts.append(np.concatenate([hi, lo], axis=0))
    return jnp.asarray(np.stack(parts))


def split(x):
    hi = x.astype(jnp.bfloat16)
    return hi, (x - hi.astype(F32)).astype(jnp.bfloat16)


def pair(x, y, axis):
    return jnp.concatenate([x, y], axis=axis)


def product(x, both, axis):
    size = both.shape[1]
    hi, lo = split(x)
    if axis == 0:
        first = jnp.dot(both, hi, preferred_element_type=F32)
        return first[:size] + first[size:] + jnp.dot(both[:size], lo, preferred_element_type=F32)
    first = jnp.dot(pair(hi, lo, 0), both[:size], preferred_element_type=F32)
    return first[: x.shape[0]] + first[x.shape[0] :] + jnp.dot(hi, both[size:], preferred_element_type=F32)


def one_side(re, im, kind, axis, table):
    half = re.shape[axis] // 2

    def halves(x):
        return (x[:half], x[half:]) if axis == 0 else (x[:, :half], x[:, half:])

    a, b = halves(re)
    c, d = halves(im)
    if kind != INV:
        a, b, c, d = a + b, a - b, c + d, c - d
    even, odd = (LEFT if axis == 0 else RIGHT)[kind]
    a, c = halves(product(pair(a, c, axis), table[even], axis))
    b, d = halves(product(pair(b, d, axis), table[odd], axis))
    if kind == FWD:
        return pair(a, b, axis), pair(c, d, axis)
    return pair(a + b, a - b, axis), pair(c + d, c - d, axis)


def transform(re, im, kind, table):
    re, im = one_side(re, im, kind, 1, table)
    return one_side(re, im, kind, 0, table)


def times(a, b, c, d):
    return a * c - b * d, a * d + b * c


def conj_times(a, b, c, d):
    return a * c + b * d, a * d - b * c


class Slot:
    def __init__(self, start, block, amplitude, obj, acc):
        width = obj.shape[-1]
        self.width, self.block, self.amplitude, self.obj, self.acc = width, block, amplitude, obj, acc
        self.row, self.shift = start[0], start[1] % width
        self.below = lax.broadcasted_iota(jnp.int32, (width, width), 0) < self.row
        self.beside = lax.broadcasted_iota(jnp.int32, (width, width), 1) < self.shift

    def cut(self, level):
        width, block, obj = self.width, self.block, self.obj

        def part(k):
            upper = jnp.where(self.beside, obj[block + 1, level, k, :width], obj[block, level, k, :width])
            lower = jnp.where(self.beside, obj[block + 1, level, k, width:], obj[block, level, k, width:])
            return jnp.where(self.below, lower, upper)

        return part(0), part(1)

    def deposit(self, level, terms):
        width, block, acc = self.width, self.block, self.acc
        for k, term in enumerate(terms):
            zero = jnp.zeros_like(term)
            upper = jnp.where(self.below, zero, term)
            lower = jnp.where(self.below, term, zero)
            acc[block, level, k, :width] += jnp.where(self.beside, zero, upper)
            acc[block, level, k, width:] += jnp.where(self.beside, zero, lower)
            acc[block + 1, level, k, :width] += jnp.where(self.beside, upper, zero)
            acc[block + 1, level, k, width:] += jnp.where(self.beside, lower, zero)

    def rolled(self, x):
        return pltpu.roll(pltpu.roll(x, self.row, 0), self.shift, 1)

    def rolled_back(self, x):
        width = self.width
        return pltpu.roll(pltpu.roll(x, (width - self.row) % width, 0), (width - self.shift) % width, 1)


def visit(slots, probe, table, g_probe):
    def transformed(fields, kind):
        for axis in (1, 0):
            fields = [one_side(*field, kind, axis, table) for field in fields]
        return fields

    u0 = [(slot.rolled(probe[0]), slot.rolled(probe[1])) for slot in slots]
    o0 = [slot.cut(0) for slot in slots]
    u1 = transformed([times(*u, *o) for u, o in zip(u0, o0)], PROP)
    o1 = [slot.cut(1) for slot in slots]
    far = transformed([times(*u, *o) for u, o in zip(u1, o1)], FWD)
    factors = [1.0 - slot.amplitude() * lax.rsqrt(re * re + im * im + 1.0) for slot, (re, im) in zip(slots, far)]
    chi = transformed([(re * factor, im * factor) for factor, (re, im) in zip(factors, far)], INV)
    back = [conj_times(*o, *x) for o, x in zip(o1, chi)]
    for slot, u, x in zip(slots, u1, chi):
        slot.deposit(1, conj_times(*u, *x))
    chi = transformed(back, ADJ)
    for slot, u, x in zip(slots, u0, chi):
        slot.deposit(0, conj_times(*u, *x))
    for slot, o, x in zip(slots, o0, chi):
        for part, term in enumerate(conj_times(*o, *x)):
            g_probe[part] += slot.rolled_back(term)


class Place:
    def __init__(self, axes, scalars, tile_rows, tile_cols, rim):
        down, along, self.centers, counts = scalars
        tx, ty = down[0], along[0]
        odd = tx % 2
        self.count = counts[tx * axes[1] + ty]
        self.relayed = (tx == axes[0] // 2) | (tx == axes[0] // 2 - 1)
        self.first = tx * tile_rows, ty * tile_cols
        inner = tile_rows - rim
        self.on_tile, self.off_tile = rows_at((1 - odd) * inner, rim), rows_at(odd * inner, rim)
        outer = tile_rows + rim
        self.on, self.off = rows_at((1 - odd) * outer, rim), rows_at(odd * outer, rim)

    def start(self, slot):
        return self.centers[0, slot] - self.first[0], self.centers[1, slot] - self.first[1]


def rows_at(first, count):
    return pl.ds(pl.multiple_of(first, count), count)


def start_all(pairs, sem, at):
    copies = [pltpu.make_async_copy(a, b, sem.at[at + i]) for i, (a, b) in enumerate(pairs)]
    for copy in copies:
        copy.start()
    return copies


def run_all(pairs, sem):
    return start_all(pairs, sem, 0)


def wait_all(copies):
    for copy in copies:
        copy.wait()


class Loads:
    def __init__(self, pairs, sem, at):
        self.pairs, self.sem, self.at = pairs, sem, at

    def copies(self):
        return [pltpu.make_async_copy(a, b, self.sem.at[self.at + i]) for i, (a, b) in enumerate(self.pairs)]

    def start(self):
        for copy in self.copies():
            copy.start()

    def wait(self):
        wait_all(self.copies())


class ChosenLoads(Loads):
    def __init__(self, pairs, flag, other, sem, at):
        super().__init__(pairs, sem, at)
        self.flag, self.other = flag, other

    def start(self):
        copies = self.copies()
        for copy in copies[:-1]:
            copy.start()
        place = self.sem.at[self.at + len(copies) - 1]
        pl.when(self.flag)(lambda: pltpu.make_async_copy(self.other, self.pairs[-1][1], place).start())
        pl.when(jnp.logical_not(self.flag))(lambda: copies[-1].start())


def two_groups(here, firsts, step, loads, stores, amplitudes, amps, amp_sem, order, sem, probe, table, obj, acc, g_probe):
    width = probe.shape[-1]

    def listed(g, count):
        def look(slot, n):
            order[n] = slot
            return n + (here.start(slot)[1] // width == firsts[g]).astype(jnp.int32)

        return lax.fori_loop(0, here.count, look, count)

    first = listed(0, jnp.zeros((), jnp.int32))
    count = listed(1, first)

    part = amplitudes[0].shape[0]

    def amplitude_copy(slot, source):
        return pltpu.make_async_copy(source, amps.at[slot], amp_sem.at[slot])

    def fetch(i, _):
        slot = order[i]
        pl.when(slot < part)(lambda: amplitude_copy(slot, amplitudes[0].at[slot]).start())
        pl.when(slot >= part)(lambda: amplitude_copy(slot, amplitudes[1].at[slot - part]).start())
        return 0

    lax.fori_loop(0, count, fetch, 0)

    def store(g):
        start_all(stores[g], sem, g * len(stores[0]))

    def slot_at(i):
        slot = order[i]

        def amplitude():
            amplitude_copy(slot, amplitudes[0].at[0]).wait()
            return amps[slot]

        return Slot(here.start(slot), step * (i >= first).astype(jnp.int32), amplitude, obj, acc)

    def after_first(i):
        pl.when((i < first) & (first <= i + 2))(lambda: store(0))

    def two(p, _):
        i = 2 * p
        pl.when((i + 1 >= first) & (i - 1 < first))(loads[1].wait)
        pl.when((first == 0) & (p == 0))(lambda: store(0))
        visit([slot_at(i), slot_at(i + 1)], probe, table, g_probe)
        after_first(i)
        return 0

    def one():
        visit([slot_at(count - 1)], probe, table, g_probe)
        after_first(count - 1)

    soon = first < 2
    pl.when(soon)(loads[1].start)
    loads[0].wait()
    pl.when(jnp.logical_not(soon))(loads[1].start)
    pairs = count // 2
    lax.fori_loop(0, pairs, two, 0)
    pl.when(2 * pairs - 1 < first)(loads[1].wait)
    pl.when((first == 0) & (pairs == 0))(lambda: store(0))
    pl.when(count % 2 == 1)(one)
    store(1)
    for g in (0, 1):
        wait_all([pltpu.make_async_copy(a, b, sem.at[g * len(stores[0]) + i]) for i, (a, b) in enumerate(stores[g])])


def inner_body(
    axes, tx, ty, centers, counts, tile, on, off_quarters, relayed, off_mid, early, late, probe_in, table_in,
    g_quarters, g_tile_mid, g_on_mid, g_off_mid, g_probe, obj, acc, probe, table, amps, order, sem, out_sem, amp_sem,
):
    width = probe.shape[-1]
    rim = width // 2
    tile_rows, tile_cols = tile.shape[2], tile.shape[3]
    here = Place(axes, (tx, ty, centers, counts), tile_rows, tile_cols, rim)
    own = slice(rim, rim + tile_rows)
    loads = ([(probe_in, probe), (table_in, table)], [])
    for k in range(3):
        there = slice(rim + k * width, rim + (k + 1) * width)
        loads[k // 2].append((tile.at[:, :, :, there], obj.at[k, :, :, own]))
        loads[k // 2].append((on.at[:, :, :, (k + 1) * width : (k + 2) * width], obj.at[k, :, :, here.on]))
    loads[0].append((off_mid, obj.at[1, :, :, here.off]))
    waits = []
    for k in (0, 1):
        lanes = slice(k * width, (k + 1) * width)
        loads[k].append((off_quarters.at[:, :, :, lanes], obj.at[2 * k, :, :, here.off]))
        waits.append(ChosenLoads(loads[k], here.relayed, relayed.at[:, :, :, lanes], sem, 16 * k))
    waits[0].start()
    acc[...] = jnp.zeros_like(acc)
    g_probe[...] = jnp.zeros_like(g_probe)
    stores = (
        [(acc.at[0], g_quarters.at[0])],
        [
            (acc.at[2], g_quarters.at[1]),
            (acc.at[1, :, :, own], g_tile_mid),
            (acc.at[1, :, :, here.on], g_on_mid),
            (acc.at[1, :, :, here.off], g_off_mid),
        ],
    )
    two_groups(here, (1, 2), 1, waits, stores, (early, late), amps, amp_sem, order, out_sem, probe, table, obj, acc, g_probe)


def outer_body(
    axes, tx, ty, centers, counts, tile, on, off_quarters, relayed, off_ends, left, right, carried, carried_probe, early, late, probe_in, table_in,
    g_tile_ends, g_tile_quarters, g_on_ends, g_on_quarters, g_off_ends, g_off_quarters,
    g_left, g_right, g_probe,
    obj, acc, probe, table, amps, order, sem, out_sem, amp_sem,
):
    width = probe.shape[-1]
    rim = width // 2
    tile_rows, tile_cols = tile.shape[2], tile.shape[3]
    here = Place(axes, (tx, ty, centers, counts), tile_rows, tile_cols, rim)
    own = slice(rim, rim + tile_rows)
    one, two = slice(0, rim), slice(rim, width)
    waits, stores = [], []
    for k, (end, quarter, near, far, half, side, g_side) in enumerate((
        (0, 1, two, slice(0, rim), one, left, g_left),
        (3, 2, one, slice(tile_cols - rim, tile_cols), two, right, g_right),
    )):
        first = rim if k == 0 else tile_cols - rim - width
        there = slice(first, first + width)
        edge = k * tile_cols
        loads = [(probe_in, probe), (table_in, table), (carried_probe, g_probe)] if k == 0 else []
        loads += [
            (tile.at[:, :, :, far], obj.at[end, :, :, own, near]),
            (side, obj.at[end, :, :, own, half]),
            (on.at[:, :, :, edge : edge + width], obj.at[end, :, :, here.on]),
            (off_ends.at[:, :, :, k * width : (k + 1) * width], obj.at[end, :, :, here.off]),
            (tile.at[:, :, :, there], obj.at[quarter, :, :, own]),
            (on.at[:, :, :, first + rim : first + rim + width], obj.at[quarter, :, :, here.on]),
            (carried.at[k], acc.at[quarter]),
        ]
        lanes = slice(k * width, (k + 1) * width)
        loads.append((off_quarters.at[:, :, :, lanes], obj.at[quarter, :, :, here.off]))
        waits.append(ChosenLoads(loads, here.relayed, relayed.at[:, :, :, lanes], sem, 16 * k))
        stores.append([
            (acc.at[end, :, :, own, near], g_tile_ends.at[:, :, :, half]),
            (acc.at[end, :, :, here.on, near], g_on_ends.at[:, :, :, half]),
            (acc.at[end, :, :, here.off, near], g_off_ends.at[:, :, :, half]),
            (acc.at[end, :, :, own, half], g_side.at[:, :, :tile_rows]),
            (acc.at[end, :, :, here.on, half], g_side.at[:, :, tile_rows : tile_rows + rim]),
            (acc.at[end, :, :, here.off, half], g_side.at[:, :, tile_rows + rim :]),
            (acc.at[quarter, :, :, own], g_tile_quarters.at[:, :, :, lanes]),
            (acc.at[quarter, :, :, here.on], g_on_quarters.at[:, :, :, lanes]),
            (acc.at[quarter, :, :, here.off], g_off_quarters.at[:, :, :, lanes]),
        ])
    waits[0].start()
    for end in (0, 3):
        acc[end] = jnp.zeros_like(acc[end])
    last_block = (tile_cols + 2 * rim) // width - 2
    two_groups(here, (0, last_block), 2, waits, stores, (early, late), amps, amp_sem, order, out_sem, probe, table, obj, acc, g_probe)
    positions = lax.fori_loop(0, counts.shape[0], lambda i, n: n + counts[i], jnp.zeros((), jnp.int32))
    g_probe[...] = g_probe[...] / jnp.sqrt(jnp.full(g_probe.shape, jnp.maximum(positions, 1).astype(F32)))


SMEM = pl.BlockSpec(memory_space=pltpu.SMEM)
VMEM = pl.BlockSpec(memory_space=pltpu.VMEM)
HBM = pl.BlockSpec(memory_space=pltpu.HBM)
ROOM = pltpu.CompilerParams(vmem_limit_bytes=63 * 2**20)


def shape(*dims):
    return jax.ShapeDtypeStruct(dims, F32)


def costs(flops):
    return pl.CostEstimate(flops=flops, bytes_accessed=10**7, transcendentals=0)


def field_call(body, axes, blocks, scalars, arrays, amplitudes, probe, outs, tile_rows):
    width = probe.shape[-1]
    padded = (blocks, 2, 2, tile_rows + width, width)
    table = tables(width)
    slots = sum(part.shape[0] for part in amplitudes)
    return pl.pallas_call(
        functools.partial(body, axes),
        out_shape=tuple(outs) + (jax.ShapeDtypeStruct(probe.shape, F32),),
        in_specs=[SMEM] * len(scalars) + [HBM] * (len(arrays) + 4),
        out_specs=(HBM,) * len(outs) + (VMEM,),
        scratch_shapes=[
            pltpu.VMEM(padded, F32),
            pltpu.VMEM(padded, F32),
            pltpu.VMEM(probe.shape, F32),
            pltpu.VMEM(table.shape, table.dtype),
            pltpu.VMEM((slots, width, width), F32),
            pltpu.SMEM((slots + 1,), jnp.int32),
            pltpu.SemaphoreType.DMA((32,)),
            pltpu.SemaphoreType.DMA((18,)),
            pltpu.SemaphoreType.DMA((slots,)),
        ],
        compiler_params=ROOM,
        cost_estimate=costs(2 * 10**10),
    )(*scalars, *arrays, *amplitudes, probe, table)


def pack_body(tx, tile, left, right, quarters, mid, sem):
    rim = left.shape[-1]
    width = 2 * rim
    tile_rows, tile_cols = tile.shape[2], tile.shape[3]
    rows = rows_at((tx[0] % 2) * (tile_rows - rim), rim)
    quarter = rim + width
    far = tile_cols - quarter
    wait_all(run_all([
        (tile.at[:, :, :, :rim], left),
        (tile.at[:, :, :, tile_cols - rim :], right),
        (tile.at[:, :, rows, rim:quarter], quarters.at[:, :, :, :width]),
        (tile.at[:, :, rows, far : far + width], quarters.at[:, :, :, width:]),
        (tile.at[:, :, rows, quarter:far], mid),
    ], sem))


def strips_body(tx, tile, left, right, on, ends, sem):
    rim = left.shape[-1]
    tile_rows, tile_cols = tile.shape[2], tile.shape[3]
    odd = tx[0] % 2
    inner = tile_rows - rim
    on_rows, off_rows = rows_at((1 - odd) * inner, rim), rows_at(odd * inner, rim)
    wait_all(run_all([
        (left.at[:, :, on_rows], on.at[:, :, :, :rim]),
        (tile.at[:, :, on_rows], on.at[:, :, :, rim : rim + tile_cols]),
        (right.at[:, :, on_rows], on.at[:, :, :, rim + tile_cols :]),
        (left.at[:, :, off_rows], ends.at[:, :, :, :rim]),
        (tile.at[:, :, off_rows, :rim], ends.at[:, :, :, rim : 2 * rim]),
        (tile.at[:, :, off_rows, tile_cols - rim :], ends.at[:, :, :, 2 * rim : 3 * rim]),
        (right.at[:, :, off_rows], ends.at[:, :, :, 3 * rim :]),
    ], sem))


def copies_call(body, scalars, arrays, outs, flops):
    return pl.pallas_call(
        body,
        out_shape=tuple(outs),
        in_specs=[SMEM] * len(scalars) + [HBM] * len(arrays),
        out_specs=(VMEM,) * len(outs),
        scratch_shapes=[pltpu.SemaphoreType.DMA((8,))],
        compiler_params=ROOM,
        cost_estimate=costs(flops),
    )(*scalars, *arrays)


def amplitude_body(axes, first, tx, ty, counts, patterns, pick, out):
    width = patterns.shape[-1]

    def work():
        hi, lo = split(jnp.sqrt(patterns[0]))
        both = jnp.dot(pick[0], pair(hi, lo, 1), preferred_element_type=F32).astype(jnp.bfloat16)
        out[0] = jnp.dot(both, pick[1:].reshape(-1, width), preferred_element_type=F32)

    pl.when(first + pl.program_id(0) < counts[tx[0] * axes[1] + ty[0]])(work)


def amplitudes_of(axes, scalars, patterns, first, count):
    width = patterns.shape[-1]
    pick = np.zeros((width, width))
    pick[np.arange(width), np.concatenate([np.arange(0, width, 2), np.arange(1, width, 2)])] = 1
    pick = jnp.asarray(np.stack([pick, pick.T, pick.T]).astype(ml_dtypes.bfloat16))
    block = pl.BlockSpec((1, width, width), lambda i: (first + i, 0, 0))
    return pl.pallas_call(
        functools.partial(amplitude_body, axes, first),
        grid=(count,),
        out_shape=shape(count, width, width),
        in_specs=[SMEM, SMEM, SMEM, block, VMEM],
        out_specs=pl.BlockSpec((1, width, width), lambda i: (i, 0, 0)),
        compiler_params=ROOM,
        cost_estimate=costs(10**11),
    )(*scalars, patterns, pick)


def merge_body(on_ends, off_ends, left, right, quarters, mid, on, off, sides, sem):
    rim = left.shape[-1]
    width = 2 * rim
    tile_rows = left.shape[2] - width
    on_rows, off_rows = slice(tile_rows, tile_rows + rim), slice(tile_rows + rim, tile_rows + width)
    wait_all(run_all([
        (on_ends, on.at[:, :, :, :width]),
        (off_ends, off),
        (left.at[:, :, on_rows], sides.at[0, :, :, :, :rim]),
        (right.at[:, :, on_rows], sides.at[0, :, :, :, rim:]),
        (left.at[:, :, off_rows], sides.at[1, :, :, :, :rim]),
        (right.at[:, :, off_rows], sides.at[1, :, :, :, rim:]),
        (quarters, on.at[:, :, :, width : 3 * width]),
        (mid, on.at[:, :, :, 3 * width :]),
    ], sem))
    on[:, :, :, :width] += sides[0]
    off[...] += sides[1]


def merged(on_ends, off_ends, left, right, quarters, mid):
    slices, _, rim, width = on_ends.shape
    cols = width + quarters.shape[3] + mid.shape[3]
    return pl.pallas_call(
        merge_body,
        out_shape=(shape(slices, 2, rim, cols), jax.ShapeDtypeStruct(off_ends.shape, F32)),
        in_specs=[HBM] * 6,
        out_specs=(VMEM, VMEM),
        scratch_shapes=[pltpu.VMEM((2,) + on_ends.shape, F32), pltpu.SemaphoreType.DMA((8,))],
        compiler_params=ROOM,
        cost_estimate=pl.CostEstimate(flops=10**6, bytes_accessed=10**5, transcendentals=0),
    )(on_ends, off_ends, left, right, quarters, mid)


def inner_total_body(axes, tx, quarters, mid, on, off_quarters, far_quarters, off_mid, out, total, on_part, off_part, sem):
    rim = on.shape[2]
    width = 2 * rim
    rows = quarters.shape[2]
    cols = out.shape[3]
    last = cols - 2 * width
    middle = slice(width, last)
    odd = tx[0] % 2
    wait_all(run_all([
        (quarters.at[:, :, :, :width], total.at[:, :, :, :width]),
        (mid, total.at[:, :, :, middle]),
        (quarters.at[:, :, :, width:], total.at[:, :, :, last:]),
        (on.at[:, :, :, width : 2 * width], on_part.at[:, :, :, :width]),
        (on.at[:, :, :, 3 * width :], on_part.at[:, :, :, middle]),
        (on.at[:, :, :, 2 * width : 3 * width], on_part.at[:, :, :, last:]),
        (off_mid, off_part.at[:, :, :, middle]),
    ], sem))
    is_far = (tx[0] == axes[0] // 2) | (tx[0] == axes[0] // 2 - 1)
    for here, source in ((is_far, far_quarters), (jnp.logical_not(is_far), off_quarters)):
        pairs = [(source.at[:, :, :, :width], off_part.at[:, :, :, :width]), (source.at[:, :, :, width:], off_part.at[:, :, :, last:])]
        pl.when(here)(lambda pairs=pairs: wait_all(run_all(pairs, sem)))
    total[:, :, rows_at((1 - odd) * (rows - rim), rim)] += on_part[...]
    total[:, :, rows_at(odd * (rows - rim), rim)] += off_part[...]
    wait_all(run_all([(total, out.at[:, :, :, rim : cols - rim])], sem))


def inner_total(axes, tx, parts, tile_shape):
    rim, width = parts[2].shape[2], 2 * parts[2].shape[2]
    cols = tile_shape[3] - width
    return pl.pallas_call(
        functools.partial(inner_total_body, axes),
        out_shape=jax.ShapeDtypeStruct(tile_shape, F32),
        in_specs=[SMEM] + [HBM] * len(parts),
        out_specs=HBM,
        scratch_shapes=[pltpu.VMEM(tile_shape[:3] + (cols,), F32)]
        + [pltpu.VMEM(tile_shape[:2] + (rim, cols), F32)] * 2
        + [pltpu.SemaphoreType.DMA((9,))],
        compiler_params=ROOM,
        cost_estimate=costs(10**8),
    )(tx, *parts)


def end_total_body(tx, ends, left, right, on, off, inner, out, total, sides, on_part, off_part, sem):
    del inner
    rim = on.shape[2]
    rows, cols = out.shape[2:]
    odd = tx[0] % 2
    wait_all(run_all([
        (ends, total),
        (left.at[:, :, :rows], sides.at[:, :, :, :rim]),
        (right.at[:, :, :rows], sides.at[:, :, :, rim:]),
        (on.at[:, :, :, : 2 * rim], on_part),
        (off, off_part),
    ], sem))
    total[...] += sides[...]
    total[:, :, rows_at((1 - odd) * (rows - rim), rim)] += on_part[...]
    total[:, :, rows_at(odd * (rows - rim), rim)] += off_part[...]
    wait_all(run_all([
        (total.at[:, :, :, :rim], out.at[:, :, :, :rim]),
        (total.at[:, :, :, rim:], out.at[:, :, :, cols - rim :]),
    ], sem))


def end_total(tx, parts, inner):
    ends, off = parts[0], parts[-1]
    return pl.pallas_call(
        end_total_body,
        out_shape=jax.ShapeDtypeStruct(inner.shape, F32),
        in_specs=[SMEM] + [HBM] * (len(parts) + 1),
        out_specs=HBM,
        scratch_shapes=[pltpu.VMEM(ends.shape, F32)] * 2 + [pltpu.VMEM(off.shape, F32)] * 2 + [pltpu.SemaphoreType.DMA((5,))],
        input_output_aliases={len(parts) + 1: 0},
        compiler_params=ROOM,
        cost_estimate=costs(10**11),
    )(tx, *parts, inner)


def along(x, step):
    count = lax.axis_size("ty")
    return lax.ppermute(x, "ty", [(i, i + step) for i in range(count) if 0 <= i + step < count])


def across(x, first, skip=None):
    pairs = []
    for i in range(first, lax.axis_size("tx") - 1, 2):
        if i != skip:
            pairs += [(i, i + 1), (i + 1, i)]
    return lax.ppermute(x, "tx", pairs)


def relay_out(x):
    count = lax.axis_size("tx")
    return lax.ppermute(x, "tx", [(count // 2 - 1, count - 1), (count // 2, 0)])


def relay_in(x):
    count = lax.axis_size("tx")
    return lax.ppermute(x, "tx", [(count - 1, count // 2), (0, count // 2 - 1)])


def after(x, *others):
    return lax.optimization_barrier((x,) + others)[0]


def halved(flat, apart):
    bit = (lax.axis_index("tx") // apart) % 2
    half = flat.shape[0] // 2
    pairs = [(i, i ^ apart) for i in range(lax.axis_size("tx"))]
    mine = lax.dynamic_slice_in_dim(flat, bit * half, half, 0)
    other = lax.dynamic_slice_in_dim(flat, (1 - bit) * half, half, 0)
    return mine + lax.ppermute(other, "tx", pairs)


def doubled(flat, apart, meanwhile):
    bit = (lax.axis_index("tx") // apart) % 2
    other = lax.ppermute(flat, "tx", [(i, i ^ apart) for i in range(lax.axis_size("tx"))])
    return joined(flat, after(other, meanwhile), bit)


def joined(flat, other, bit):
    return jnp.concatenate([jnp.where(bit == 0, flat, other), jnp.where(bit == 0, other, flat)], axis=0)


def per_device(object_slab, probe, patterns, centers, counts):
    slices, _, tile_rows, tile_cols = object_slab.shape
    width = probe.shape[-1]
    rim = width // 2
    axes = lax.axis_size("tx"), lax.axis_size("ty")
    middle = axes[0] // 2
    tx, ty = (lax.axis_index(axis).astype(jnp.int32).reshape(1) for axis in ("tx", "ty"))
    full = tile_rows + width
    mid_cols = tile_cols - 3 * width
    ends_shape = shape(slices, 2, rim, width)
    quarters_shape = shape(slices, 2, rim, 2 * width)
    mid_shape = shape(slices, 2, rim, mid_cols)
    side_shape = shape(slices, 2, full, rim)
    tile = object_slab

    column_shape = shape(slices, 2, tile_rows, rim)
    to_left, to_right, quarters, mid = copies_call(
        pack_body, (tx,), (tile,), (column_shape, column_shape, quarters_shape, mid_shape), 10**8
    )
    carried = relay_out(quarters)
    left, right = along(to_right, 1), along(to_left, -1)
    off_quarters = across(quarters, 1, middle - 1)
    off_mid = across(mid, 1)
    on_shape = shape(slices, 2, rim, tile_cols + width)
    part = patterns.shape[0] // 2
    early = amplitudes_of(axes, (tx, ty, counts), after(patterns, to_left), 0, part)

    def strips(patterns, tile, left, right):
        on, ends = copies_call(strips_body, (tx,), (tile, left, right), (on_shape, quarters_shape), 10**8)
        late = amplitudes_of(axes, (tx, ty, counts), after(patterns, on), part, part)
        return across(on, 0), ends, late

    def nothing(patterns, tile, left, right):
        return jnp.zeros(on_shape.shape, F32), jnp.zeros(quarters_shape.shape, F32), patterns[part:]

    relayed = relay_in(carried)
    on, ends, late = lax.cond(counts[0] >= 0, strips, nothing, patterns, after(tile, early, carried), left, right)
    amplitudes = (early, late)
    off_ends = across(ends, 1)

    scalars = (tx, ty, centers.T, counts)
    g_quarters, g_tile_mid, g_on_mid, g_off_mid, g_probe = field_call(
        inner_body, axes, 3, scalars, (tile, on, off_quarters, relayed, off_mid), amplitudes, probe,
        (shape(2, slices, 2, full, width), shape(slices, 2, tile_rows, mid_cols), mid_shape, mid_shape), tile_rows,
    )
    back_mid = across(g_off_mid, 1)
    g_tile_ends, g_tile_quarters, g_on_ends, g_on_quarters, g_off_ends, g_off_quarters, g_left, g_right, g_probe = field_call(
        outer_body, axes, 4, scalars, (tile, on, off_quarters, relayed, off_ends, left, right, g_quarters, g_probe), amplitudes, probe,
        (
            shape(slices, 2, tile_rows, width), shape(slices, 2, tile_rows, 2 * width), ends_shape, quarters_shape,
            ends_shape, quarters_shape, side_shape, side_shape,
        ),
        tile_rows,
    )
    g_off_quarters, g_left, g_right, g_probe, _ = lax.optimization_barrier((g_off_quarters, g_left, g_right, g_probe, back_mid))
    from_left, from_right = along(g_right, 1), along(g_left, -1)
    back_quarters = across(g_off_quarters, 1, middle - 1)
    apart = [1] + [2**k for k in range(axes[0].bit_length() - 2, 1, -1)]
    shard = g_probe.size // width // 2 ** len(apart)
    some = counts[0] >= 0

    def shared(flat, quarters):
        for step in apart:
            flat = halved(flat, step)
        far = lax.ppermute(after(quarters, flat), "tx", [(middle - 1, middle), (middle, middle - 1)])
        for step in (2**k for k in range(axes[1].bit_length() - 1)):
            flat = flat + lax.ppermute(flat, "ty", [(i, i ^ step) for i in range(axes[1])])
        return flat, far

    flat, far_quarters = lax.cond(
        counts[0] >= 0, shared, lambda x, quarters: (x[:shard], quarters), g_probe.reshape(-1, width), g_off_quarters
    )
    other = lax.ppermute(flat, "tx", [(i, i ^ 2) for i in range(axes[0])])
    on_all, off_ends = merged(after(g_on_ends, flat, back_quarters), g_off_ends, from_left, from_right, g_on_quarters, g_on_mid)
    back_ends = across(off_ends, 1)
    back_on = across(on_all, 0)
    inner = inner_total(axes, tx, (g_tile_quarters, g_tile_mid, back_on, back_quarters, far_quarters, back_mid), tile.shape)
    flat = after(flat + other, on_all)
    for step in reversed(apart[1:]):
        flat = doubled(flat, step, inner)
    last = lax.ppermute(flat, "tx", [(i, i ^ 1) for i in range(axes[0])])
    inner = end_total(tx, (g_tile_ends, from_left, from_right, back_on, back_ends), inner)
    probe_sum = joined(flat, after(last, inner), lax.axis_index("tx") % 2).reshape(probe.shape)
    return (inner, probe_sum)


def solution(mesh):
    placed = (
        P(None, None, "tx", "ty"),
        P(),
        P(("tx", "ty"), None, None),
        P(("tx", "ty"), None),
        P(),
    )
    return jax.shard_map(
        per_device,
        mesh=mesh,
        in_specs=placed,
        out_specs=(P(None, None, "tx", "ty"), P()),
        check_vma=False,
    )
```

```python
import functools
import math

import jax
import jax.numpy as jnp
import ml_dtypes
import numpy as np
from jax import lax
from jax.experimental import pallas as pl
from jax.experimental.pallas import tpu as pltpu
from jax.sharding import PartitionSpec as P

KAPPA = 40.0
F32 = jnp.float32
FWD, INV, PROP, ADJ = 0, 1, 2, 3
LEFT = {FWD: (0, 2), INV: (1, 3), PROP: (4, 6), ADJ: (5, 7)}
RIGHT = {FWD: (1, 3), INV: (0, 2), PROP: (5, 7), ADJ: (4, 6)}


def tables(width):
    half = width // 2
    n = np.arange(half)
    freq = ((np.arange(width) + half) % width - half) / width
    factor = np.exp(-1j * math.pi * KAPPA * freq * freq)
    turn = 2j * np.pi / width
    scale = 1.0 / math.sqrt(width)
    even = np.exp(-turn * ((2 * n[:, None] * n[None, :]) % width)) * scale
    odd = np.exp(-turn * (((2 * n[:, None] + 1) * n[None, :]) % width)) * scale

    def combined(freqs):
        apart = n[:, None] - n[None, :]
        total = np.zeros((half, half), complex)
        for k in freqs:
            total += factor[k] * np.exp(turn * ((k * apart) % width))
        return total / width

    parts = []
    for c in (even, odd, combined(range(0, width, 2)), combined(range(1, width, 2))):
        real = np.block([[c.real, -c.imag], [c.imag, c.real]])
        for m in (real, real.T):
            hi = m.astype(ml_dtypes.bfloat16)
            lo = (m - hi.astype(np.float64)).astype(ml_dtypes.bfloat16)
            parts.append(np.concatenate([hi, lo], axis=0))
    return jnp.asarray(np.stack(parts))


def split(x):
    hi = x.astype(jnp.bfloat16)
    return hi, (x - hi.astype(F32)).astype(jnp.bfloat16)


def pair(x, y, axis):
    return jnp.concatenate([x, y], axis=axis)


def product(x, both, axis):
    size = both.shape[1]
    hi, lo = split(x)
    if axis == 0:
        first = jnp.dot(both, hi, preferred_element_type=F32)
        return first[:size] + first[size:] + jnp.dot(both[:size], lo, preferred_element_type=F32)
    first = jnp.dot(pair(hi, lo, 0), both[:size], preferred_element_type=F32)
    return first[: x.shape[0]] + first[x.shape[0] :] + jnp.dot(hi, both[size:], preferred_element_type=F32)


def one_side(re, im, kind, axis, table):
    half = re.shape[axis] // 2

    def halves(x):
        return (x[:half], x[half:]) if axis == 0 else (x[:, :half], x[:, half:])

    a, b = halves(re)
    c, d = halves(im)
    if kind != INV:
        a, b, c, d = a + b, a - b, c + d, c - d
    even, odd = (LEFT if axis == 0 else RIGHT)[kind]
    a, c = halves(product(pair(a, c, axis), table[even], axis))
    b, d = halves(product(pair(b, d, axis), table[odd], axis))
    if kind == FWD:
        return pair(a, b, axis), pair(c, d, axis)
    return pair(a + b, a - b, axis), pair(c + d, c - d, axis)


def transform(re, im, kind, table):
    re, im = one_side(re, im, kind, 1, table)
    return one_side(re, im, kind, 0, table)


def times(a, b, c, d):
    return a * c - b * d, a * d + b * c


def conj_times(a, b, c, d):
    return a * c + b * d, a * d - b * c


class Slot:
    def __init__(self, start, block, amplitude, obj, acc):
        width = obj.shape[-1]
        self.width, self.block, self.amplitude, self.obj, self.acc = width, block, amplitude, obj, acc
        self.row, self.shift = start[0], start[1] % width
        self.below = lax.broadcasted_iota(jnp.int32, (width, width), 0) < self.row
        self.beside = lax.broadcasted_iota(jnp.int32, (width, width), 1) < self.shift

    def cut(self, level):
        width, block, obj = self.width, self.block, self.obj

        def part(k):
            upper = jnp.where(self.beside, obj[block + 1, level, k, :width], obj[block, level, k, :width])
            lower = jnp.where(self.beside, obj[block + 1, level, k, width:], obj[block, level, k, width:])
            return jnp.where(self.below, lower, upper)

        return part(0), part(1)

    def deposit(self, level, terms):
        width, block, acc = self.width, self.block, self.acc
        for k, term in enumerate(terms):
            zero = jnp.zeros_like(term)
            upper = jnp.where(self.below, zero, term)
            lower = jnp.where(self.below, term, zero)
            acc[block, level, k, :width] += jnp.where(self.beside, zero, upper)
            acc[block, level, k, width:] += jnp.where(self.beside, zero, lower)
            acc[block + 1, level, k, :width] += jnp.where(self.beside, upper, zero)
            acc[block + 1, level, k, width:] += jnp.where(self.beside, lower, zero)

    def rolled(self, x):
        return pltpu.roll(pltpu.roll(x, self.row, 0), self.shift, 1)

    def rolled_back(self, x):
        width = self.width
        return pltpu.roll(pltpu.roll(x, (width - self.row) % width, 0), (width - self.shift) % width, 1)


def visit(slots, probe, table, g_probe):
    def transformed(fields, kind):
        for axis in (1, 0):
            fields = [one_side(*field, kind, axis, table) for field in fields]
        return fields

    u0 = [(slot.rolled(probe[0]), slot.rolled(probe[1])) for slot in slots]
    o0 = [slot.cut(0) for slot in slots]
    u1 = transformed([times(*u, *o) for u, o in zip(u0, o0)], PROP)
    o1 = [slot.cut(1) for slot in slots]
    far = transformed([times(*u, *o) for u, o in zip(u1, o1)], FWD)
    factors = [1.0 - slot.amplitude() * lax.rsqrt(re * re + im * im + 1.0) for slot, (re, im) in zip(slots, far)]
    chi = transformed([(re * factor, im * factor) for factor, (re, im) in zip(factors, far)], INV)
    back = [conj_times(*o, *x) for o, x in zip(o1, chi)]
    for slot, u, x in zip(slots, u1, chi):
        slot.deposit(1, conj_times(*u, *x))
    chi = transformed(back, ADJ)
    for slot, u, x in zip(slots, u0, chi):
        slot.deposit(0, conj_times(*u, *x))
    for slot, o, x in zip(slots, o0, chi):
        for part, term in enumerate(conj_times(*o, *x)):
            g_probe[part] += slot.rolled_back(term)


class Place:
    def __init__(self, axes, scalars, tile_rows, tile_cols, rim):
        down, along, self.centers, counts = scalars
        tx, ty = down[0], along[0]
        odd = tx % 2
        self.count = counts[tx * axes[1] + ty]
        self.relayed = (tx == axes[0] // 2) | (tx == axes[0] // 2 - 1)
        self.first = tx * tile_rows, ty * tile_cols
        inner = tile_rows - rim
        self.on_tile, self.off_tile = rows_at((1 - odd) * inner, rim), rows_at(odd * inner, rim)
        outer = tile_rows + rim
        self.on, self.off = rows_at((1 - odd) * outer, rim), rows_at(odd * outer, rim)

    def start(self, slot):
        return self.centers[0, slot] - self.first[0], self.centers[1, slot] - self.first[1]


def rows_at(first, count):
    return pl.ds(pl.multiple_of(first, count), count)


def start_all(pairs, sem, at):
    copies = [pltpu.make_async_copy(a, b, sem.at[at + i]) for i, (a, b) in enumerate(pairs)]
    for copy in copies:
        copy.start()
    return copies


def run_all(pairs, sem):
    return start_all(pairs, sem, 0)


def wait_all(copies):
    for copy in copies:
        copy.wait()


class Loads:
    def __init__(self, pairs, sem, at):
        self.pairs, self.sem, self.at = pairs, sem, at

    def copies(self):
        return [pltpu.make_async_copy(a, b, self.sem.at[self.at + i]) for i, (a, b) in enumerate(self.pairs)]

    def start(self):
        for copy in self.copies():
            copy.start()

    def wait(self):
        wait_all(self.copies())


class ChosenLoads(Loads):
    def __init__(self, pairs, flag, other, sem, at):
        super().__init__(pairs, sem, at)
        self.flag, self.other = flag, other

    def start(self):
        copies = self.copies()
        for copy in copies[:-1]:
            copy.start()
        place = self.sem.at[self.at + len(copies) - 1]
        pl.when(self.flag)(lambda: pltpu.make_async_copy(self.other, self.pairs[-1][1], place).start())
        pl.when(jnp.logical_not(self.flag))(lambda: copies[-1].start())


def two_groups(here, firsts, step, loads, stores, amplitudes, amps, amp_sem, order, sem, probe, table, obj, acc, g_probe, finish=None):
    width = probe.shape[-1]

    def listed(g, count):
        def look(slot, n):
            order[n] = slot
            return n + (here.start(slot)[1] // width == firsts[g]).astype(jnp.int32)

        return lax.fori_loop(0, here.count, look, count)

    first = listed(0, jnp.zeros((), jnp.int32))
    count = listed(1, first)

    part = amplitudes[0].shape[0]

    def amplitude_copy(slot, source):
        return pltpu.make_async_copy(source, amps.at[slot], amp_sem.at[slot])

    def fetch(i, _):
        slot = order[i]
        pl.when(slot < part)(lambda: amplitude_copy(slot, amplitudes[0].at[slot]).start())
        pl.when(slot >= part)(lambda: amplitude_copy(slot, amplitudes[1].at[slot - part]).start())
        return 0

    lax.fori_loop(0, count, fetch, 0)

    def store(g):
        start_all(stores[g], sem, g * len(stores[0]))

    def slot_at(i):
        slot = order[i]

        def amplitude():
            amplitude_copy(slot, amplitudes[0].at[0]).wait()
            return amps[slot]

        return Slot(here.start(slot), step * (i >= first).astype(jnp.int32), amplitude, obj, acc)

    def after_first(i):
        pl.when((i < first) & (first <= i + 2))(lambda: store(0))

    def two(p, _):
        i = 2 * p
        pl.when((i + 1 >= first) & (i - 1 < first))(loads[1].wait)
        pl.when((first == 0) & (p == 0))(lambda: store(0))
        visit([slot_at(i), slot_at(i + 1)], probe, table, g_probe)
        after_first(i)
        return 0

    def one():
        visit([slot_at(count - 1)], probe, table, g_probe)
        after_first(count - 1)

    soon = first < 2
    pl.when(soon)(loads[1].start)
    loads[0].wait()
    pl.when(jnp.logical_not(soon))(loads[1].start)
    pairs = count // 2
    lax.fori_loop(0, pairs, two, 0)
    pl.when(2 * pairs - 1 < first)(loads[1].wait)
    pl.when((first == 0) & (pairs == 0))(lambda: store(0))
    pl.when(count % 2 == 1)(one)
    store(1)
    if finish is not None:
        finish()
    for g in (0, 1):
        wait_all([pltpu.make_async_copy(a, b, sem.at[g * len(stores[0]) + i]) for i, (a, b) in enumerate(stores[g])])


def inner_body(
    axes, tx, ty, centers, counts, tile, on, off_quarters, relayed, off_mid, early, late, probe_in, table_in,
    g_quarters, g_tile_mid, g_on_mid, g_off_mid, g_probe, obj, acc, probe, table, amps, order, sem, out_sem, amp_sem,
):
    width = probe.shape[-1]
    rim = width // 2
    tile_rows, tile_cols = tile.shape[2], tile.shape[3]
    here = Place(axes, (tx, ty, centers, counts), tile_rows, tile_cols, rim)
    own = slice(rim, rim + tile_rows)
    loads = ([(probe_in, probe), (table_in, table)], [])
    for k in range(3):
        there = slice(rim + k * width, rim + (k + 1) * width)
        loads[k // 2].append((tile.at[:, :, :, there], obj.at[k, :, :, own]))
        loads[k // 2].append((on.at[:, :, :, (k + 1) * width : (k + 2) * width], obj.at[k, :, :, here.on]))
    loads[0].append((off_mid, obj.at[1, :, :, here.off]))
    waits = []
    for k in (0, 1):
        lanes = slice(k * width, (k + 1) * width)
        loads[k].append((off_quarters.at[:, :, :, lanes], obj.at[2 * k, :, :, here.off]))
        waits.append(ChosenLoads(loads[k], here.relayed, relayed.at[:, :, :, lanes], sem, 16 * k))
    waits[0].start()
    acc[...] = jnp.zeros_like(acc)
    g_probe[...] = jnp.zeros_like(g_probe)
    stores = (
        [(acc.at[0], g_quarters.at[0])],
        [
            (acc.at[2], g_quarters.at[1]),
            (acc.at[1, :, :, own], g_tile_mid),
            (acc.at[1, :, :, here.on], g_on_mid),
            (acc.at[1, :, :, here.off], g_off_mid),
        ],
    )
    two_groups(here, (1, 2), 1, waits, stores, (early, late), amps, amp_sem, order, out_sem, probe, table, obj, acc, g_probe)


def outer_body(
    axes, tx, ty, centers, counts, tile, on, off_quarters, relayed, off_ends, left, right, carried, carried_probe, early, late, probe_in, table_in,
    g_tile_ends, g_tile_quarters, g_on_ends, g_on_quarters, g_off_ends, g_off_quarters,
    g_left, g_right, g_probe,
    obj, acc, probe, table, amps, order, sem, out_sem, amp_sem,
):
    width = probe.shape[-1]
    rim = width // 2
    tile_rows, tile_cols = tile.shape[2], tile.shape[3]
    here = Place(axes, (tx, ty, centers, counts), tile_rows, tile_cols, rim)
    own = slice(rim, rim + tile_rows)
    one, two = slice(0, rim), slice(rim, width)
    waits, stores = [], []
    for k, (end, quarter, near, far, half, side, g_side) in enumerate((
        (0, 1, two, slice(0, rim), one, left, g_left),
        (3, 2, one, slice(tile_cols - rim, tile_cols), two, right, g_right),
    )):
        first = rim if k == 0 else tile_cols - rim - width
        there = slice(first, first + width)
        edge = k * tile_cols
        loads = [(probe_in, probe), (table_in, table), (carried_probe, g_probe)] if k == 0 else []
        loads += [
            (tile.at[:, :, :, far], obj.at[end, :, :, own, near]),
            (side, obj.at[end, :, :, own, half]),
            (on.at[:, :, :, edge : edge + width], obj.at[end, :, :, here.on]),
            (off_ends.at[:, :, :, k * width : (k + 1) * width], obj.at[end, :, :, here.off]),
            (tile.at[:, :, :, there], obj.at[quarter, :, :, own]),
            (on.at[:, :, :, first + rim : first + rim + width], obj.at[quarter, :, :, here.on]),
            (carried.at[k], acc.at[quarter]),
        ]
        lanes = slice(k * width, (k + 1) * width)
        loads.append((off_quarters.at[:, :, :, lanes], obj.at[quarter, :, :, here.off]))
        waits.append(ChosenLoads(loads, here.relayed, relayed.at[:, :, :, lanes], sem, 16 * k))
        stores.append([
            (acc.at[end, :, :, own, near], g_tile_ends.at[:, :, :, half]),
            (acc.at[end, :, :, here.on, near], g_on_ends.at[:, :, :, half]),
            (acc.at[end, :, :, here.off, near], g_off_ends.at[:, :, :, half]),
            (acc.at[end, :, :, own, half], g_side.at[:, :, :tile_rows]),
            (acc.at[end, :, :, here.on, half], g_side.at[:, :, tile_rows : tile_rows + rim]),
            (acc.at[end, :, :, here.off, half], g_side.at[:, :, tile_rows + rim :]),
            (acc.at[quarter, :, :, own], g_tile_quarters.at[:, :, :, lanes]),
            (acc.at[quarter, :, :, here.on], g_on_quarters.at[:, :, :, lanes]),
            (acc.at[quarter, :, :, here.off], g_off_quarters.at[:, :, :, lanes]),
        ])
    waits[0].start()
    for end in (0, 3):
        acc[end] = jnp.zeros_like(acc[end])
    last_block = (tile_cols + 2 * rim) // width - 2
    def scale_probe():
        positions = lax.fori_loop(0, counts.shape[0], lambda i, n: n + counts[i], jnp.zeros((), jnp.int32))
        g_probe[...] = g_probe[...] / jnp.sqrt(jnp.full(g_probe.shape, jnp.maximum(positions, 1).astype(F32)))

    two_groups(here, (0, last_block), 2, waits, stores, (early, late), amps, amp_sem, order, out_sem, probe, table, obj, acc, g_probe, scale_probe)


SMEM = pl.BlockSpec(memory_space=pltpu.SMEM)
VMEM = pl.BlockSpec(memory_space=pltpu.VMEM)
HBM = pl.BlockSpec(memory_space=pltpu.HBM)
ROOM = pltpu.CompilerParams(vmem_limit_bytes=63 * 2**20)


def shape(*dims):
    return jax.ShapeDtypeStruct(dims, F32)


def costs(flops):
    return pl.CostEstimate(flops=flops, bytes_accessed=10**7, transcendentals=0)


def field_call(body, axes, blocks, scalars, arrays, amplitudes, probe, outs, tile_rows):
    width = probe.shape[-1]
    padded = (blocks, 2, 2, tile_rows + width, width)
    table = tables(width)
    slots = sum(part.shape[0] for part in amplitudes)
    return pl.pallas_call(
        functools.partial(body, axes),
        out_shape=tuple(outs) + (jax.ShapeDtypeStruct(probe.shape, F32),),
        in_specs=[SMEM] * len(scalars) + [HBM] * (len(arrays) + 4),
        out_specs=(HBM,) * len(outs) + (VMEM,),
        scratch_shapes=[
            pltpu.VMEM(padded, F32),
            pltpu.VMEM(padded, F32),
            pltpu.VMEM(probe.shape, F32),
            pltpu.VMEM(table.shape, table.dtype),
            pltpu.VMEM((slots, width, width), F32),
            pltpu.SMEM((slots + 1,), jnp.int32),
            pltpu.SemaphoreType.DMA((32,)),
            pltpu.SemaphoreType.DMA((18,)),
            pltpu.SemaphoreType.DMA((slots,)),
        ],
        compiler_params=ROOM,
        cost_estimate=costs(2 * 10**10),
    )(*scalars, *arrays, *amplitudes, probe, table)


def pack_body(tx, tile, left, right, quarters, mid, sem):
    rim = left.shape[-1]
    width = 2 * rim
    tile_rows, tile_cols = tile.shape[2], tile.shape[3]
    rows = rows_at((tx[0] % 2) * (tile_rows - rim), rim)
    quarter = rim + width
    far = tile_cols - quarter
    wait_all(run_all([
        (tile.at[:, :, :, :rim], left),
        (tile.at[:, :, :, tile_cols - rim :], right),
        (tile.at[:, :, rows, rim:quarter], quarters.at[:, :, :, :width]),
        (tile.at[:, :, rows, far : far + width], quarters.at[:, :, :, width:]),
        (tile.at[:, :, rows, quarter:far], mid),
    ], sem))


def strips_body(tx, tile, left, right, on, ends, sem):
    rim = left.shape[-1]
    tile_rows, tile_cols = tile.shape[2], tile.shape[3]
    odd = tx[0] % 2
    inner = tile_rows - rim
    on_rows, off_rows = rows_at((1 - odd) * inner, rim), rows_at(odd * inner, rim)
    wait_all(run_all([
        (left.at[:, :, on_rows], on.at[:, :, :, :rim]),
        (tile.at[:, :, on_rows], on.at[:, :, :, rim : rim + tile_cols]),
        (right.at[:, :, on_rows], on.at[:, :, :, rim + tile_cols :]),
        (left.at[:, :, off_rows], ends.at[:, :, :, :rim]),
        (tile.at[:, :, off_rows, :rim], ends.at[:, :, :, rim : 2 * rim]),
        (tile.at[:, :, off_rows, tile_cols - rim :], ends.at[:, :, :, 2 * rim : 3 * rim]),
        (right.at[:, :, off_rows], ends.at[:, :, :, 3 * rim :]),
    ], sem))


def copies_call(body, scalars, arrays, outs, flops):
    return pl.pallas_call(
        body,
        out_shape=tuple(outs),
        in_specs=[SMEM] * len(scalars) + [HBM] * len(arrays),
        out_specs=(VMEM,) * len(outs),
        scratch_shapes=[pltpu.SemaphoreType.DMA((8,))],
        compiler_params=ROOM,
        cost_estimate=costs(flops),
    )(*scalars, *arrays)


def amplitude_body(axes, first, tx, ty, counts, patterns, pick, out):
    width = patterns.shape[-1]

    def work():
        hi, lo = split(jnp.sqrt(patterns[0]))
        both = jnp.dot(pick[0], pair(hi, lo, 1), preferred_element_type=F32).astype(jnp.bfloat16)
        out[0] = jnp.dot(both, pick[1:].reshape(-1, width), preferred_element_type=F32)

    pl.when(first + pl.program_id(0) < counts[tx[0] * axes[1] + ty[0]])(work)


def amplitudes_of(axes, scalars, patterns, first, count):
    width = patterns.shape[-1]
    pick = np.zeros((width, width))
    pick[np.arange(width), np.concatenate([np.arange(0, width, 2), np.arange(1, width, 2)])] = 1
    pick = jnp.asarray(np.stack([pick, pick.T, pick.T]).astype(ml_dtypes.bfloat16))
    block = pl.BlockSpec((1, width, width), lambda i: (first + i, 0, 0))
    return pl.pallas_call(
        functools.partial(amplitude_body, axes, first),
        grid=(count,),
        out_shape=shape(count, width, width),
        in_specs=[SMEM, SMEM, SMEM, block, VMEM],
        out_specs=pl.BlockSpec((1, width, width), lambda i: (i, 0, 0)),
        compiler_params=ROOM,
        cost_estimate=costs(10**11),
    )(*scalars, patterns, pick)


def merge_body(on_ends, off_ends, left, right, quarters, mid, on, off, sides, sem):
    rim = left.shape[-1]
    width = 2 * rim
    tile_rows = left.shape[2] - width
    on_rows, off_rows = slice(tile_rows, tile_rows + rim), slice(tile_rows + rim, tile_rows + width)
    wait_all(run_all([
        (on_ends, on.at[:, :, :, :width]),
        (off_ends, off),
        (left.at[:, :, on_rows], sides.at[0, :, :, :, :rim]),
        (right.at[:, :, on_rows], sides.at[0, :, :, :, rim:]),
        (left.at[:, :, off_rows], sides.at[1, :, :, :, :rim]),
        (right.at[:, :, off_rows], sides.at[1, :, :, :, rim:]),
        (quarters, on.at[:, :, :, width : 3 * width]),
        (mid, on.at[:, :, :, 3 * width :]),
    ], sem))
    on[:, :, :, :width] += sides[0]
    off[...] += sides[1]


def merged(on_ends, off_ends, left, right, quarters, mid):
    slices, _, rim, width = on_ends.shape
    cols = width + quarters.shape[3] + mid.shape[3]
    return pl.pallas_call(
        merge_body,
        out_shape=(shape(slices, 2, rim, cols), jax.ShapeDtypeStruct(off_ends.shape, F32)),
        in_specs=[HBM] * 6,
        out_specs=(VMEM, VMEM),
        scratch_shapes=[pltpu.VMEM((2,) + on_ends.shape, F32), pltpu.SemaphoreType.DMA((8,))],
        compiler_params=ROOM,
        cost_estimate=pl.CostEstimate(flops=10**6, bytes_accessed=10**5, transcendentals=0),
    )(on_ends, off_ends, left, right, quarters, mid)


def inner_total_body(axes, tx, quarters, mid, on, off_quarters, far_quarters, off_mid, out, total, on_part, off_part, sem):
    rim = on.shape[2]
    width = 2 * rim
    rows = quarters.shape[2]
    cols = out.shape[3]
    last = cols - 2 * width
    middle = slice(width, last)
    odd = tx[0] % 2
    wait_all(run_all([
        (quarters.at[:, :, :, :width], total.at[:, :, :, :width]),
        (mid, total.at[:, :, :, middle]),
        (quarters.at[:, :, :, width:], total.at[:, :, :, last:]),
        (on.at[:, :, :, width : 2 * width], on_part.at[:, :, :, :width]),
        (on.at[:, :, :, 3 * width :], on_part.at[:, :, :, middle]),
        (on.at[:, :, :, 2 * width : 3 * width], on_part.at[:, :, :, last:]),
        (off_mid, off_part.at[:, :, :, middle]),
    ], sem))
    is_far = (tx[0] == axes[0] // 2) | (tx[0] == axes[0] // 2 - 1)
    for here, source in ((is_far, far_quarters), (jnp.logical_not(is_far), off_quarters)):
        pairs = [(source.at[:, :, :, :width], off_part.at[:, :, :, :width]), (source.at[:, :, :, width:], off_part.at[:, :, :, last:])]
        pl.when(here)(lambda pairs=pairs: wait_all(run_all(pairs, sem)))
    total[:, :, rows_at((1 - odd) * (rows - rim), rim)] += on_part[...]
    total[:, :, rows_at(odd * (rows - rim), rim)] += off_part[...]
    wait_all(run_all([(total, out.at[:, :, :, rim : cols - rim])], sem))


def inner_total(axes, tx, parts, tile_shape):
    rim, width = parts[2].shape[2], 2 * parts[2].shape[2]
    cols = tile_shape[3] - width
    return pl.pallas_call(
        functools.partial(inner_total_body, axes),
        out_shape=jax.ShapeDtypeStruct(tile_shape, F32),
        in_specs=[SMEM] + [HBM] * len(parts),
        out_specs=HBM,
        scratch_shapes=[pltpu.VMEM(tile_shape[:3] + (cols,), F32)]
        + [pltpu.VMEM(tile_shape[:2] + (rim, cols), F32)] * 2
        + [pltpu.SemaphoreType.DMA((9,))],
        compiler_params=ROOM,
        cost_estimate=costs(10**8),
    )(tx, *parts)


def end_total_body(tx, ends, left, right, on, off, inner, out, total, sides, on_part, off_part, sem):
    del inner
    rim = on.shape[2]
    rows, cols = out.shape[2:]
    odd = tx[0] % 2
    wait_all(run_all([
        (ends, total),
        (left.at[:, :, :rows], sides.at[:, :, :, :rim]),
        (right.at[:, :, :rows], sides.at[:, :, :, rim:]),
        (on.at[:, :, :, : 2 * rim], on_part),
        (off, off_part),
    ], sem))
    total[...] += sides[...]
    total[:, :, rows_at((1 - odd) * (rows - rim), rim)] += on_part[...]
    total[:, :, rows_at(odd * (rows - rim), rim)] += off_part[...]
    wait_all(run_all([
        (total.at[:, :, :, :rim], out.at[:, :, :, :rim]),
        (total.at[:, :, :, rim:], out.at[:, :, :, cols - rim :]),
    ], sem))


def end_total(tx, parts, inner):
    ends, off = parts[0], parts[-1]
    return pl.pallas_call(
        end_total_body,
        out_shape=jax.ShapeDtypeStruct(inner.shape, F32),
        in_specs=[SMEM] + [HBM] * (len(parts) + 1),
        out_specs=HBM,
        scratch_shapes=[pltpu.VMEM(ends.shape, F32)] * 2 + [pltpu.VMEM(off.shape, F32)] * 2 + [pltpu.SemaphoreType.DMA((5,))],
        input_output_aliases={len(parts) + 1: 0},
        compiler_params=ROOM,
        cost_estimate=costs(10**11),
    )(tx, *parts, inner)


def along(x, step):
    count = lax.axis_size("ty")
    return lax.ppermute(x, "ty", [(i, i + step) for i in range(count) if 0 <= i + step < count])


def across(x, first, skip=None):
    pairs = []
    for i in range(first, lax.axis_size("tx") - 1, 2):
        if i != skip:
            pairs += [(i, i + 1), (i + 1, i)]
    return lax.ppermute(x, "tx", pairs)


def relay_out(x):
    count = lax.axis_size("tx")
    return lax.ppermute(x, "tx", [(count // 2 - 1, count - 1), (count // 2, 0)])


def relay_in(x):
    count = lax.axis_size("tx")
    return lax.ppermute(x, "tx", [(count - 1, count // 2), (0, count // 2 - 1)])


def after(x, *others):
    return lax.optimization_barrier((x,) + others)[0]


def halved(flat, apart):
    bit = (lax.axis_index("tx") // apart) % 2
    half = flat.shape[0] // 2
    pairs = [(i, i ^ apart) for i in range(lax.axis_size("tx"))]
    mine = lax.dynamic_slice_in_dim(flat, bit * half, half, 0)
    other = lax.dynamic_slice_in_dim(flat, (1 - bit) * half, half, 0)
    return mine + lax.ppermute(other, "tx", pairs)


def doubled(flat, apart, meanwhile):
    bit = (lax.axis_index("tx") // apart) % 2
    other = lax.ppermute(flat, "tx", [(i, i ^ apart) for i in range(lax.axis_size("tx"))])
    return joined(flat, after(other, meanwhile), bit)


def joined(flat, other, bit):
    return jnp.concatenate([jnp.where(bit == 0, flat, other), jnp.where(bit == 0, other, flat)], axis=0)


def per_device(object_slab, probe, patterns, centers, counts):
    slices, _, tile_rows, tile_cols = object_slab.shape
    width = probe.shape[-1]
    rim = width // 2
    axes = lax.axis_size("tx"), lax.axis_size("ty")
    middle = axes[0] // 2
    tx, ty = (lax.axis_index(axis).astype(jnp.int32).reshape(1) for axis in ("tx", "ty"))
    full = tile_rows + width
    mid_cols = tile_cols - 3 * width
    ends_shape = shape(slices, 2, rim, width)
    quarters_shape = shape(slices, 2, rim, 2 * width)
    mid_shape = shape(slices, 2, rim, mid_cols)
    side_shape = shape(slices, 2, full, rim)
    tile = object_slab

    column_shape = shape(slices, 2, tile_rows, rim)
    to_left, to_right, quarters, mid = copies_call(
        pack_body, (tx,), (tile,), (column_shape, column_shape, quarters_shape, mid_shape), 10**8
    )
    carried = relay_out(quarters)
    left, right = along(to_right, 1), along(to_left, -1)
    off_quarters = across(quarters, 1, middle - 1)
    off_mid = across(mid, 1)
    on_shape = shape(slices, 2, rim, tile_cols + width)
    part = patterns.shape[0] // 2
    early = amplitudes_of(axes, (tx, ty, counts), after(patterns, to_left), 0, part)

    def strips(patterns, tile, left, right):
        on, ends = copies_call(strips_body, (tx,), (tile, left, right), (on_shape, quarters_shape), 10**8)
        late = amplitudes_of(axes, (tx, ty, counts), after(patterns, on), part, part)
        return across(on, 0), ends, late

    def nothing(patterns, tile, left, right):
        return jnp.zeros(on_shape.shape, F32), jnp.zeros(quarters_shape.shape, F32), patterns[part:]

    relayed = relay_in(carried)
    on, ends, late = lax.cond(counts[0] >= 0, strips, nothing, patterns, after(tile, early, carried), left, right)
    amplitudes = (early, late)
    off_ends = across(ends, 1)

    scalars = (tx, ty, centers.T, counts)
    g_quarters, g_tile_mid, g_on_mid, g_off_mid, g_probe = field_call(
        inner_body, axes, 3, scalars, (tile, on, off_quarters, relayed, off_mid), amplitudes, probe,
        (shape(2, slices, 2, full, width), shape(slices, 2, tile_rows, mid_cols), mid_shape, mid_shape), tile_rows,
    )
    back_mid = across(g_off_mid, 1)
    g_tile_ends, g_tile_quarters, g_on_ends, g_on_quarters, g_off_ends, g_off_quarters, g_left, g_right, g_probe = field_call(
        outer_body, axes, 4, scalars, (tile, on, off_quarters, relayed, off_ends, left, right, g_quarters, g_probe), amplitudes, probe,
        (
            shape(slices, 2, tile_rows, width), shape(slices, 2, tile_rows, 2 * width), ends_shape, quarters_shape,
            ends_shape, quarters_shape, side_shape, side_shape,
        ),
        tile_rows,
    )
    g_off_quarters, g_left, g_right, g_probe, _ = lax.optimization_barrier((g_off_quarters, g_left, g_right, g_probe, back_mid))
    from_left, from_right = along(g_right, 1), along(g_left, -1)
    back_quarters = across(g_off_quarters, 1, middle - 1)
    apart = [1] + [2**k for k in range(axes[0].bit_length() - 2, 1, -1)]
    shard = g_probe.size // width // 2 ** len(apart)
    some = counts[0] >= 0

    def shared(flat, quarters):
        for step in apart:
            flat = halved(flat, step)
        far = lax.ppermute(after(quarters, flat), "tx", [(middle - 1, middle), (middle, middle - 1)])
        for step in (2**k for k in range(axes[1].bit_length() - 1)):
            flat = flat + lax.ppermute(flat, "ty", [(i, i ^ step) for i in range(axes[1])])
        return flat, far

    flat, far_quarters = lax.cond(
        counts[0] >= 0, shared, lambda x, quarters: (x[:shard], quarters), g_probe.reshape(-1, width), g_off_quarters
    )
    other = lax.ppermute(flat, "tx", [(i, i ^ 2) for i in range(axes[0])])
    on_all, off_ends = merged(after(g_on_ends, flat, back_quarters), g_off_ends, from_left, from_right, g_on_quarters, g_on_mid)
    back_ends = across(off_ends, 1)
    back_on = across(on_all, 0)
    inner = inner_total(axes, tx, (g_tile_quarters, g_tile_mid, back_on, back_quarters, far_quarters, back_mid), tile.shape)
    flat = after(flat + other, on_all)
    for step in reversed(apart[1:]):
        flat = doubled(flat, step, inner)
    last = lax.ppermute(flat, "tx", [(i, i ^ 1) for i in range(axes[0])])
    inner = end_total(tx, (g_tile_ends, from_left, from_right, back_on, back_ends), inner)
    probe_sum = joined(flat, after(last, inner), lax.axis_index("tx") % 2).reshape(probe.shape)
    return (inner, probe_sum)


def solution(mesh):
    placed = (
        P(None, None, "tx", "ty"),
        P(),
        P(("tx", "ty"), None, None),
        P(("tx", "ty"), None),
        P(),
    )
    return jax.shard_map(
        per_device,
        mesh=mesh,
        in_specs=placed,
        out_specs=(P(None, None, "tx", "ty"), P()),
        check_vma=False,
    )
```
